128 devices in a mesh: dp: 32 (over x_hi, z, y), tensor: 4 (over x_lo, core).
Axes of the slice: x: 4 (x_hi: 2, x_lo: 2; x = x_hi * 2 + x_lo), y: 4, z: 4, core: 2. Of those that a mesh axis runs over, the one named last changes fastest.
Arguments:
- tokens: bfloat16 [32768, 640], P(('dp', 'tensor')), may hold values from -6 to 6
- segments: int32 [32, 1024], P('dp'), may hold values from 0 to 2, as said below
- cotangent: bfloat16 [32768, 640], P(('dp', 'tensor')), may hold values from -24 to 24
- w_query: bfloat16 [640, 1024], P('dp', 'tensor'), may hold values from -0.25 to 0.25
- w_keyval: bfloat16 [640, 512], P('dp'), may hold values from -0.25 to 0.25
- w_out: bfloat16 [1024, 640], P('tensor', 'dp'), may hold values from -0.1875 to 0.1875
- w_gate: bfloat16 [640, 2048], P('dp', 'tensor'), may hold values from -0.25 to 0.25
- w_up: bfloat16 [640, 2048], P('dp', 'tensor'), may hold values from -0.25 to 0.25
- w_down: bfloat16 [2048, 640], P('tensor', 'dp'), may hold values from -0.125 to 0.125
- gain_in: float32 [640], replicated, may hold values from 0.25 to 1.75
- gain_post_attn: float32 [640], replicated, may hold values from 0.25 to 1.75
- gain_pre_ff: float32 [640], replicated, may hold values from 0.25 to 1.75
- gain_post_ff: float32 [640], replicated, may hold values from 0.25 to 1.75
- gain_query: float32 [256], replicated, may hold values from 0.25 to 1.75
- gain_key: float32 [256], replicated, may hold values from 0.25 to 1.75
Outputs:
- output: bfloat16 [32768, 640], P(('dp', 'tensor'))
- grad_x: float32 [32768, 640], P(('dp', 'tensor'))
- grad_query: float32 [640, 1024], P('dp', 'tensor')
- grad_keyval: float32 [640, 512], P('dp')
- grad_out: float32 [1024, 640], P('tensor', 'dp')
- grad_gate: float32 [640, 2048], P('dp', 'tensor')
- grad_up: float32 [640, 2048], P('dp', 'tensor')
- grad_down: float32 [2048, 640], P('tensor', 'dp')
- grad_gain_in: float32 [640], replicated
- grad_gain_post_attn: float32 [640], replicated
- grad_gain_pre_ff: float32 [640], replicated
- grad_gain_post_ff: float32 [640], replicated
- grad_gain_query: float32 [256], replicated
- grad_gain_key: float32 [256], replicated
The draws below stay inside these ranges and needn't reach their ends.
Inputs may be any that keep to these rules, and one draw needn't show every extreme that they name: `segments`: along each row the numbers never fall; each row holds three documents numbered 0, 1, 2, each of one token or more, where document 1 starts within the first 256 tokens and ends within the last 256.
All inputs are finite; a program needn't handle non-finite values.
Results may differ from the reference program's by a relative error of at most 0.024.
Values may be sent and summed in bfloat16 or wider, within the bound.
A program may use at most 128 MiB of HBM per device.

```python
import jax
import jax.numpy as jnp
from jax import lax

D = 640
HEADS = 4
HD = 256
FF = 2048
WINDOW = 512
TOK_DEV = 256
SEQ = 1024
TOKENS = 32768
N_DP = 32


def draw_segments(key, part):
    key_head, key_tail = jax.random.split(jax.random.fold_in(key, 17))
    head_cut = jax.random.randint(key_head, (N_DP, 1), 1, TOK_DEV)
    tail_cut = jax.random.randint(key_tail, (N_DP, 1), SEQ - TOK_DEV + 1, SEQ)
    row_index = jnp.arange(SEQ, dtype=jnp.int32)[None, :]
    return (row_index >= head_cut).astype(jnp.int32) + (row_index >= tail_cut).astype(jnp.int32)


def spiked(array, stream_key, source, target, shards_of, factor):
    owner, partner = [(jnp.arange(array.shape[position]) // (array.shape[position] // shards_of)).reshape([-1 if axis == position else 1 for axis in range(array.ndim)]) for position in (source, target)]
    chosen = jax.random.permutation(stream_key, shards_of)[partner]
    strong = (owner == chosen) | (owner == (partner + shards_of // 2) % shards_of)
    return jnp.where(strong, factor * array, array)


def block_levels(stream_key, shape, shards, least, largest):
    def one(dim, shards_of):
        steps = jax.random.uniform(jax.random.fold_in(jax.random.fold_in(stream_key, 6), dim), (shards_of,), jnp.float32, least / len(shards), largest / len(shards))
        return jnp.repeat(jnp.exp(steps), shape[dim] // shards_of).reshape((-1,) + (1,) * (len(shape) - dim - 1))

    level = one(*shards[0])
    for cut in shards[1:]:
        level = level * one(*cut)
    return level


def scatter_about(rng, dims, scale, most, cuts=(), kind=jnp.bfloat16):
    factor_of = block_levels(rng, dims, cuts, -0.22, 0.18) if cuts else 1.0
    result = jax.random.normal(rng, dims, jnp.float32) * scale * factor_of
    return jnp.minimum(jnp.maximum(result, -most), most).astype(kind)


def noise_with(stream_key, extent, width, most, cuts, heavy, kind=jnp.bfloat16):
    drawn = width * jax.random.normal(stream_key, extent, jnp.float32)
    if cuts:
        drawn = drawn * block_levels(stream_key, extent, cuts, -0.22, 0.18)
    return jnp.clip(spiked(drawn, jax.random.fold_in(stream_key, 3), *heavy), -most, most).astype(kind)


def setup_inputs(seed: int = 0) -> dict:
    keys = jax.random.split(jax.random.key(seed), 16)
    return {
        "tokens": scatter_about(keys[0], (TOKENS, D), 1.0, 6.0, ((0, 128),)),
        "segments": draw_segments(jax.random.fold_in(keys[15], 71), 0),
        "cotangent": noise_with(keys[2], (TOKENS, D), 1.0, 24.0, ((0, 128),), (0, 1, 128, 5.5)),
        "w_query": scatter_about(keys[3], (D, HEADS * HD), D ** -0.5, 0.25, ((0, 32), (1, 4))),
        "w_keyval": scatter_about(keys[4], (D, 2 * HD), D ** -0.5, 0.25, ((0, 32),)),
        "w_out": scatter_about(keys[5], (HEADS * HD, D), (HEADS * HD) ** -0.5, 0.1875, ((0, 4), (1, 32))),
        "w_gate": scatter_about(keys[6], (D, FF), D ** -0.5, 0.25, ((0, 32), (1, 4))),
        "w_up": scatter_about(keys[7], (D, FF), D ** -0.5, 0.25, ((0, 32), (1, 4))),
        "w_down": scatter_about(keys[8], (FF, D), FF ** -0.5, 0.125, ((0, 4), (1, 32))),
        "gain_in": jnp.clip(1.0 + 0.15 * jax.random.normal(keys[9], (D,), jnp.float32), 0.25, 1.75),
        "gain_post_attn": jnp.clip(1.0 + 0.15 * jax.random.normal(keys[10], (D,), jnp.float32), 0.25, 1.75),
        "gain_pre_ff": jnp.clip(1.0 + 0.15 * jax.random.normal(keys[11], (D,), jnp.float32), 0.25, 1.75),
        "gain_post_ff": jnp.clip(1.0 + 0.15 * jax.random.normal(keys[12], (D,), jnp.float32), 0.25, 1.75),
        "gain_query": jnp.clip(1.0 + 0.15 * jax.random.normal(keys[13], (HD,), jnp.float32), 0.25, 1.75),
        "gain_key": jnp.clip(1.0 + 0.15 * jax.random.normal(keys[14], (HD,), jnp.float32), 0.25, 1.75),
    }


norm_eps = 1e-06
rope_base = 10000.0

@jax.custom_vjp
def low(v):
    return lax.optimization_barrier(v.astype(jnp.bfloat16)).astype(jnp.float32)

@jax.custom_vjp
def low_back(v):
    return v

def low_keep(v):
    return (low(v), None)

def low_pass(kept, grad):
    return (grad,)

def back_keep(v):
    return (v, None)

def back_low(kept, grad):
    return (low(grad),)
low.defvjp(low_keep, low_pass)
low_back.defvjp(back_keep, back_low)

def matmul(left_rows, right_rows):
    return jnp.dot(left_rows, right_rows, precision=lax.Precision.HIGHEST, preferred_element_type=jnp.float32)

def rms_scale(array_in, gain_row):
    return array_in * lax.rsqrt(lax.optimization_barrier(jnp.mean(array_in * array_in, axis=-1, keepdims=True)) + norm_eps) * gain_row

def rotate_half(array_in):
    half_width = array_in.shape[-1] // 2
    return jnp.concatenate([-array_in[..., half_width:], array_in[..., :half_width]], axis=-1)

def rope_tables(position_ids, head_width):
    inv_freq = rope_base ** (-jnp.arange(0, head_width, 2).astype(jnp.float32) / head_width)
    angles = position_ids.astype(jnp.float32)[:, None] * inv_freq[None, :]
    angles = jnp.concatenate([angles, angles], axis=-1)
    return (jnp.cos(angles), jnp.sin(angles))

def segment_positions(seg_ids):
    row_index = jnp.arange(seg_ids.shape[0], dtype=jnp.int32)
    prev_ids = jnp.concatenate([seg_ids[:1] - 1, seg_ids[:-1]])
    doc_start = lax.cummax(jnp.where(seg_ids != prev_ids, row_index, 0), axis=0)
    return row_index - doc_start

def prepare(raw_rows, gain_row, cos_rows, sin_rows):
    normed = rms_scale(raw_rows, gain_row)
    return normed * cos_rows + rotate_half(normed) * sin_rows

def forward(x_rows, params, seg_ids):
    w_query, w_keyval, w_out, w_gate, w_up, w_down, gain_in, gain_post_attn, gain_pre_ff, gain_post_ff, gain_query, gain_key = params
    seq_len = x_rows.shape[0]
    positions = segment_positions(seg_ids)
    cos_rows, sin_rows = rope_tables(positions, HD)
    attn_input = low(rms_scale(x_rows, gain_in))
    query_raw = low_back(matmul(attn_input, w_query)).reshape(seq_len, HEADS, HD)
    keyval_raw = low_back(matmul(attn_input, w_keyval))
    queries = low(prepare(query_raw, gain_query, cos_rows[:, None, :], sin_rows[:, None, :]))
    key_rows = low(prepare(keyval_raw[:, :HD], gain_key, cos_rows, sin_rows))
    values = low(keyval_raw[:, HD:])
    scores = jnp.einsum('qhd,kd->hqk', queries, key_rows, precision=lax.Precision.HIGHEST)
    scores = low_back(scores * HD ** (-0.5))
    row_index = jnp.arange(seq_len, dtype=jnp.int32)
    offset = row_index[:, None] - row_index[None, :]
    allowed = (seg_ids[:, None] == seg_ids[None, :]) & (offset >= 0) & (offset < WINDOW)
    scores = jnp.where(allowed[None], scores, -1e+30)
    row_max = lax.optimization_barrier(jnp.max(scores, axis=-1, keepdims=True))
    exp_scores = jnp.exp(scores - row_max)
    attn_probs = low(exp_scores / lax.optimization_barrier(jnp.sum(exp_scores, axis=-1, keepdims=True)))
    context = jnp.einsum('hqk,kd->qhd', attn_probs, values, precision=lax.Precision.HIGHEST)
    context = low(low_back(context)).reshape(seq_len, HEADS * HD)
    attn_proj = low_back(matmul(context, w_out))
    mid_rows = x_rows + rms_scale(attn_proj, gain_post_attn)
    mlp_input = low(rms_scale(mid_rows, gain_pre_ff))
    gate_rows = low_back(matmul(mlp_input, w_gate))
    up_rows = low_back(matmul(mlp_input, w_up))
    hidden = low(jax.nn.gelu(gate_rows, approximate=True) * up_rows)
    mlp_proj = low_back(matmul(hidden, w_down))
    return mid_rows + rms_scale(mlp_proj, gain_post_ff)

def reference(tokens, segments, cotangent, w_query, w_keyval, w_out, w_gate, w_up, w_down, gain_in, gain_post_attn, gain_pre_ff, gain_post_ff, gain_query, gain_key):
    params = tuple((item.astype(jnp.float32) for item in (w_query, w_keyval, w_out, w_gate, w_up, w_down, gain_in, gain_post_attn, gain_pre_ff, gain_post_ff, gain_query, gain_key)))
    group_x = tokens.astype(jnp.float32).reshape(N_DP, SEQ, D)
    group_cot = cotangent.astype(jnp.float32).reshape(N_DP, SEQ, D)

    def one_group(totals, inputs):
        x_rows, cot_rows, seg_ids = inputs

        def run_group(x_in, param_set):
            return forward(x_in, param_set, seg_ids)
        out_rows, back_fn = jax.vjp(run_group, x_rows, params)
        dx_rows, dparams = back_fn(cot_rows)
        totals = jax.tree.map(lambda left, right: left + right, totals, dparams)
        return (totals, (out_rows, dx_rows))
    zero_grads = jax.tree.map(jnp.zeros_like, params)
    totals, (group_outs, group_dx) = lax.scan(one_group, zero_grads, (group_x, group_cot, segments))
    output = group_outs.reshape(TOKENS, D).astype(jnp.bfloat16)
    grad_x = group_dx.reshape(TOKENS, D)
    return (output, grad_x, totals[0], totals[1], totals[2], totals[3], totals[4], totals[5], totals[6], totals[7], totals[8], totals[9], totals[10], totals[11])
```

```python
import jax
import jax.numpy as jnp
from jax import lax
from jax.experimental import pallas as pl
from jax.experimental.pallas import tpu as pltpu
from jax.sharding import PartitionSpec as P

HD = 256
WINDOW = 512
D = 640
PART = 256
KEYS = 768
BLOCK = 352
CB = 16
GROUPS = 8
KV0, G0, U0, D0 = 80, 112, 192, 272
LANES = ((0, 112, "xyz"), (112, 128, "yzx"), (240, 112, "zxy"))
norm_eps = 1e-06
rope_base = 10000.0
MESH = pl.DeviceIdType.MESH
f32 = jnp.float32
bf16 = jnp.bfloat16


def place():
    dp = lax.axis_index("dp")
    t = lax.axis_index("tensor")
    return {
        "x": (dp // 16) * 2 + t // 2,
        "y": dp % 4,
        "z": (dp // 4) % 4,
        "c": t % 2,
    }


def device_of(p):
    return {
        "dp": (p["x"] // 2) * 16 + p["z"] * 4 + p["y"],
        "tensor": (p["x"] % 2) * 2 + p["c"],
    }


def moved(p, axis, by):
    size = 2 if axis == "c" else 4
    q = dict(p)
    q[axis] = (p[axis] + by) % size
    return q


def diagonal(p):
    q = moved(p, "c", 1)
    q["x"] = (p["x"] // 2) * 2 + (1 - p["x"] % 2)
    return q


def peers_of(p):
    found = [
        moved(p, axis, by)
        for axis, by in (("x", 1), ("x", 3), ("y", 1), ("y", 2), ("y", 3), ("z", 1), ("z", 3), ("c", 1))
    ]
    return found + [diagonal(p)]


def greet(p):
    barrier = pltpu.get_barrier_semaphore()
    peers = peers_of(p)
    for q in peers:
        pl.semaphore_signal(barrier, inc=1, device_id=device_of(q), device_id_type=MESH)
    pl.semaphore_wait(barrier, len(peers))


def send(src, dst, send_sem, recv_sem, q):
    copy = pltpu.make_async_remote_copy(
        src_ref=src,
        dst_ref=dst,
        send_sem=send_sem,
        recv_sem=recv_sem,
        device_id=device_of(q),
        device_id_type=MESH,
    )
    copy.start()
    return copy


def slab(ref, p, axis, value, gathered, first, rows, core=None):
    at = {a: (value if a == axis else p[a]) for a in "xyz"}
    every = slice(None)
    x_lo = every if "x" in gathered else at["x"] % 2
    x_hi = every if "x" in gathered else at["x"] // 2
    y = every if "y" in gathered else at["y"]
    z = every if "z" in gathered else at["z"]
    where = (x_lo,) + (() if core is None else (core,)) + (y, x_hi, z, pl.ds(first, rows), every)
    return ref.at[where]


def halves(first, rows):
    top = 64
    return ((first, top), (first + top, rows - top))


def gather_kernel(
    s_ref, x_ref, w_ref, xg_ref, got, stage, block,
    one_send, one_recv, ring_send, ring_recv, sib_send, sib_recv, x_send, x_recv, local,
):
    p = place()
    t = lax.axis_index("tensor")
    y = p["y"]
    core = p["c"]
    sibling = moved(p, "c", 1)
    dp = lax.axis_index("dp")
    greet(p)

    first = []
    for k in (1, 3, 2):
        q = moved(p, "y", k)
        first.append(send(s_ref.at[q["y"]], got.at[y], one_send.at[k - 1], one_recv.at[k - 1], q))

    def token_copy(k):
        return pltpu.make_async_remote_copy(
            src_ref=x_ref,
            dst_ref=xg_ref.at[2 - k],
            send_sem=x_send.at[k - 1],
            recv_sem=x_recv.at[k - 1],
            device_id={"dp": dp, "tensor": jnp.minimum(t + k, 3)},
            device_id_type=MESH,
        )

    for k in (1, 2):
        @pl.when(t + k <= 3)
        def _(k=k):
            token_copy(k).start()

    own_tokens = pltpu.make_async_copy(x_ref, xg_ref.at[2], local.at[0])
    own_tokens.start()

    got[pl.ds(y, 1)] = s_ref[pl.ds(y, 1)]
    for copy in first:
        copy.wait_recv()
    for j in range(4):
        stage[20 * j : 20 * j + 20, :] = got[j].astype(f32)[:20, :512]
    for i, at in enumerate((0, G0, U0, D0)):
        block[at : at + 80, :] = stage[:, 128 * i : 128 * i + 128].astype(bf16)
    block[KV0 : KV0 + 32, :] = got[pl.ds(t, 1)][0, :, 512:640]
    own_block = pltpu.make_async_copy(
        block, w_ref.at[p["x"] % 2, core, y, p["x"] // 2, p["z"]], local.at[1]
    )
    own_block.start()

    pending = list(first)
    for phase in range(3):
        started = []
        for lane, (at, rows, order) in enumerate(LANES):
            axis, gathered = order[phase], order[:phase]
            m = p[axis]
            mine = slab(w_ref, p, axis, m, gathered, at, rows, core)
            src = block.at[pl.ds(at, rows), :] if phase == 0 else mine
            up, down = moved(p, axis, 1), moved(p, axis, 3)
            sems = ring_send.at[lane, phase], ring_recv.at[lane, phase]
            to_up = send(src, mine, sems[0].at[0], sems[1].at[0], up)
            to_down = send(src, mine, sems[0].at[1], sems[1].at[1], down)
            if phase == 2:
                pending.append(send(mine, mine, sib_send.at[lane, 0], sib_recv.at[lane, 0], sibling))
            started.append((to_up, to_down, up, down, gathered, sems))
        passed = []
        for lane, (at, rows, order) in enumerate(LANES):
            axis = order[phase]
            to_up, to_down, up, down, gathered, sems = started[lane]
            low, high = halves(at, rows)
            to_up.wait_recv()
            from_down = slab(w_ref, p, axis, down[axis], gathered, *low, core)
            passed.append(send(from_down, from_down, sems[0].at[2], sems[1].at[2], up))
            to_down.wait_recv()
            from_up = slab(w_ref, p, axis, up[axis], gathered, *high, core)
            passed.append(send(from_up, from_up, sems[0].at[3], sems[1].at[3], down))
            if phase == 2:
                for i, q in ((1, down), (2, up)):
                    whole = slab(w_ref, p, axis, q[axis], gathered, at, rows, core)
                    pending.append(send(whole, whole, sib_send.at[lane, i], sib_recv.at[lane, i], sibling))
            pending += [to_up, to_down]
        for lane, (at, rows, order) in enumerate(LANES):
            axis = order[phase]
            gathered = order[:phase]
            far = (p[axis] + 2) % 4
            for i in range(2):
                passed[2 * lane + i].wait_recv()
                if phase == 2:
                    part = slab(w_ref, p, axis, far, gathered, *halves(at, rows)[i], core)
                    pending.append(send(part, part, sib_send.at[lane, 3 + i], sib_recv.at[lane, 3 + i], sibling))
        pending += passed
        if phase == 0:
            own_block.wait()
    for copy in pending:
        copy.wait_send()
    for lane in range(3):
        for i in range(5):
            at, rows, order = LANES[lane]
            axis, gathered = order[2], order[:2]
            if i < 3:
                value = (p[axis] + (0, 3, 1)[i]) % 4
                part = slab(w_ref, p, axis, value, gathered, at, rows, sibling["c"])
            else:
                value = (p[axis] + 2) % 4
                part = slab(w_ref, p, axis, value, gathered, *halves(at, rows)[i - 3], sibling["c"])
            pltpu.make_async_remote_copy(
                src_ref=part, dst_ref=part, send_sem=sib_send.at[lane, i], recv_sem=sib_recv.at[lane, i],
                device_id=device_of(sibling), device_id_type=MESH,
            ).wait_recv()
    own_tokens.wait()
    for k in (1, 2):
        @pl.when(t + k <= 3)
        def _(k=k):
            token_copy(k).wait_send()

        @pl.when(t - k >= 0)
        def _(k=k):
            token_copy(k).wait_recv()


def gather(s_rows, tokens):
    dma = pltpu.SemaphoreType.DMA
    return pl.pallas_call(
        gather_kernel,
        out_shape=(
            jax.ShapeDtypeStruct((2, 2, 4, 2, 4, BLOCK, 128), bf16),
            jax.ShapeDtypeStruct((3, PART, D), bf16),
        ),
        in_specs=[pl.BlockSpec(memory_space=pltpu.VMEM)] * 2,
        out_specs=(pl.BlockSpec(memory_space=pl.ANY), pl.BlockSpec(memory_space=pl.ANY)),
        scratch_shapes=[
            pltpu.VMEM((4, 32, D), bf16),
            pltpu.VMEM((80, 512), f32),
            pltpu.VMEM((BLOCK, 128), bf16),
            dma((3,)), dma((3,)), dma((3, 3, 4)), dma((3, 3, 4)), dma((3, 5)), dma((3, 5)),
            dma((2,)), dma((2,)), dma((2,)),
        ],
        compiler_params=pltpu.CompilerParams(
            collective_id=0, has_side_effects=True, vmem_limit_bytes=32 << 20
        ),
        name="gather_weights",
    )(s_rows, tokens)


def dot(a, b):
    return jnp.dot(a, b, preferred_element_type=f32)


def dot_nt(a, b):
    return lax.dot_general(a, b, (((1,), (1,)), ((), ())), preferred_element_type=f32)


def inv_rms(v):
    return lax.rsqrt(jnp.mean(v * v, axis=-1, keepdims=True) + norm_eps)


def norm_back(v, r, c, e):
    ec = e * c
    vr = v * r
    dv = r * (ec - vr * jnp.mean(vr * ec, axis=-1, keepdims=True))
    return dv, jnp.sum(e * vr, axis=0, keepdims=True)


def turn(u, cos, sin):
    a, b = u[:, :128], u[:, 128:]
    return jnp.concatenate([a * cos - b * sin, b * cos + a * sin], axis=1)


def turn_back(e, cos, sin):
    a, b = e[:, :128], e[:, 128:]
    return jnp.concatenate([a * cos + b * sin, b * cos - a * sin], axis=1)


def columns(w_ref, cb, first):
    return jnp.concatenate(
        [w_ref[cb + i, :, first : first + 80, :].reshape(D, 128) for i in range(2)], axis=1
    )


def put_columns(g_ref, cb, first, value):
    value = value.astype(bf16)
    for i in range(2):
        g_ref[cb + i, :, first : first + 80, :] = value[:, 128 * i : 128 * i + 128].reshape(GROUPS, 80, 128)


def layer_kernel(
    t_ref, x_ref, cot_ref, low_ref, cos_ref, sin_ref, gains_ref, head_gains_ref, w_ref,
    out_ref, gx_ref, dx_ref, g_ref, gn_ref,
    kv32, wkv, attn_in, attn_in_t, kt, vt, kb, vb, qraw, qb, probs, ctx, mlp_in, mlp_in_t, act_s, dact_s, hid_s,
    acc, acc2, dkt, dvt, dkv, mid_s, proj_s,
):
    scale = HD ** -0.5
    t = t_ref[0]
    gin, gpa, gpf, gpo = (gains_ref[i : i + 1, :] for i in range(4))
    gq, gk = head_gains_ref[0:1, :], head_gains_ref[1:2, :]
    row = lax.broadcasted_iota(jnp.int32, (KEYS, 1), 0)

    for tt in range(4):
        for yy in range(4):
            for g in range(GROUPS):
                at = 20 * (4 * g + tt)
                kv32[at : at + 20, 128 * yy : 128 * yy + 128] = (
                    w_ref[4 * tt + yy, g, KV0 : KV0 + 32, :].astype(f32)[:20]
                )
    wkv[...] = kv32[:D, :].astype(bf16)

    def tokens():
        x = x_ref[...].reshape(KEYS, D).astype(f32)
        return jnp.where(row >= (2 - t) * PART, x, 0.0)

    x = tokens()
    a = x * inv_rms(x) * gin
    attn_in[...] = a.astype(bf16)
    attn_in_t[...] = a.T.astype(bf16)

    kv_raw = dot(attn_in[...], wkv[...])
    kraw = kv_raw[:, :HD]
    dkv[...] = kraw
    k = turn(kraw * inv_rms(kraw) * gk, cos_ref[...], sin_ref[...])
    kb[...] = k.astype(bf16)
    kt[...] = k.T.astype(bf16)
    v = kv_raw[:, HD:]
    vb[...] = v.astype(bf16)
    vt[...] = v.T.astype(bf16)

    cos_q, sin_q = cos_ref[2 * PART :, :], sin_ref[2 * PART :, :]
    column = lax.broadcasted_iota(jnp.int32, (PART, KEYS), 1)
    own = lax.broadcasted_iota(jnp.int32, (PART, KEYS), 0)
    acc[...] = jnp.zeros_like(acc)

    def head(h, _):
        raw = dot(attn_in[2 * PART :, :], columns(w_ref, 4 * h, 0))
        qraw[h] = raw
        q = turn(raw * inv_rms(raw) * gq, cos_q, sin_q).astype(bf16)
        qb[h] = q
        s = dot(q, kt[...]) * scale
        s = jnp.where((column >= low_ref[...]) & (column <= own + 2 * PART), s, -1e30)
        e = jnp.exp(s - jnp.max(s, axis=-1, keepdims=True))
        pr = e / jnp.sum(e, axis=-1, keepdims=True)
        probs[h] = pr
        c = dot(pr.astype(bf16), vb[...]).astype(bf16)
        ctx[h] = c
        acc[...] += dot_nt(c, columns(w_ref, 4 * h + 2, 0))
        return 0

    lax.fori_loop(0, 4, head, 0)
    proj = acc[...]
    proj_s[...] = proj
    xf = x_ref[2].astype(f32)
    mid = xf + proj * inv_rms(proj) * gpa
    mid_s[...] = mid
    m = mid * inv_rms(mid) * gpf
    mlp_in[...] = m.astype(bf16)
    mlp_in_t[...] = m.T.astype(bf16)
    acc[...] = jnp.zeros_like(acc)

    def feed(c, _):
        gate = dot(mlp_in[...], columns(w_ref, 2 * c, G0))
        up = dot(mlp_in[...], columns(w_ref, 2 * c, U0))
        k0, k1 = 0.7978845608028654, 0.044715
        sq = gate * gate
        th = jnp.tanh(k0 * (gate + k1 * gate * sq))
        half = 0.5 * (1.0 + th)
        act = gate * half
        hid = (act * up).astype(bf16)
        act_s[c] = act
        dact_s[c] = up * (half + 0.5 * gate * (1.0 - th * th) * (k0 + (3.0 * k0 * k1) * sq))
        hid_s[c] = hid
        acc[...] += dot_nt(hid, columns(w_ref, 2 * c, D0))
        return 0

    lax.fori_loop(0, 8, feed, 0)
    mlp = acc[...]
    r = inv_rms(mlp)
    out_ref[...] = (mid_s[...] + mlp * r * gpo).astype(bf16)
    top = cot_ref[...].astype(f32)
    d_mlp, g_po = norm_back(mlp, r, gpo, top)
    gn_ref[3:4, :] = g_po
    d_mlp_b = d_mlp.astype(bf16)
    d_mlp_t = d_mlp.T.astype(bf16)
    ctx_in = d_mlp_b
    acc[...] = jnp.zeros_like(acc)

    def feed_back(c, _):
        put_columns(g_ref, 2 * c, D0, dot(d_mlp_t, hid_s[c]))
        d_hid = dot(ctx_in, columns(w_ref, 2 * c, D0))
        d_gate = (d_hid * dact_s[c]).astype(bf16)
        d_up = (d_hid * act_s[c]).astype(bf16)
        put_columns(g_ref, 2 * c, G0, dot(mlp_in_t[...], d_gate))
        put_columns(g_ref, 2 * c, U0, dot(mlp_in_t[...], d_up))
        acc[...] += dot_nt(d_gate, columns(w_ref, 2 * c, G0)) + dot_nt(d_up, columns(w_ref, 2 * c, U0))
        return 0

    lax.fori_loop(0, 8, feed_back, 0)
    mid = mid_s[...]
    d_pre, g_pf = norm_back(mid, inv_rms(mid), gpf, acc[...])
    gn_ref[2:3, :] = g_pf
    d_mid = cot_ref[...].astype(f32) + d_pre
    proj = proj_s[...]
    d_proj, g_pa = norm_back(proj, inv_rms(proj), gpa, d_mid)
    gn_ref[1:2, :] = g_pa
    gx_ref[...] = d_mid
    d_proj_b = d_proj.astype(bf16)
    d_proj_t = d_proj.T.astype(bf16)
    dkt[...] = jnp.zeros_like(dkt)
    dvt[...] = jnp.zeros_like(dvt)
    acc[...] = jnp.zeros_like(acc)
    acc2[...] = jnp.zeros_like(acc2)

    def head_back(h, _):
        put_columns(g_ref, 4 * h + 2, 0, dot(d_proj_t, ctx[h]))
        d_ctx = dot(d_proj_b, columns(w_ref, 4 * h + 2, 0))
        d_ctx_b = d_ctx.astype(bf16)
        pr = probs[h]
        d_pr = dot(d_ctx_b, vt[...])
        dvt[...] += dot(d_ctx.T.astype(bf16), pr.astype(bf16))
        inner = jnp.sum(pr * d_pr, axis=-1, keepdims=True)
        ds = (pr * (d_pr - inner)).astype(bf16)
        dq = dot(ds, kb[...]) * scale
        dkt[...] += dot(qb[h].astype(f32).T.astype(bf16), ds)
        raw = qraw[h]
        d_raw, g_q = norm_back(raw, inv_rms(raw), gq, turn_back(dq, cos_q, sin_q))
        acc2[...] += g_q
        d_raw = d_raw.astype(bf16)
        put_columns(g_ref, 4 * h, 0, dot(attn_in_t[:, 2 * PART :], d_raw))
        acc[...] += dot_nt(d_raw, columns(w_ref, 4 * h, 0))
        return 0

    lax.fori_loop(0, 4, head_back, 0)
    gn_ref[4:8, :] = jnp.zeros((4, D), f32)
    gn_ref[4:5, :HD] = acc2[...]
    raw = dkv[...]
    dk, g_k = norm_back(raw, inv_rms(raw), gk, turn_back(dkt[...].T * scale, cos_ref[...], sin_ref[...]))
    gn_ref[5:6, :HD] = g_k
    d_kv = jnp.concatenate([dk, dvt[...].T], axis=1).astype(bf16)
    kv32[:D, :] = dot(attn_in_t[...], d_kv)
    kv32[D:, :] = jnp.zeros((16, 512), f32)
    for tt in range(4):
        for yy in range(4):
            for g in range(GROUPS):
                at = 20 * (4 * g + tt)
                g_ref[4 * tt + yy, g, KV0 : KV0 + 32, :] = (
                    kv32[at : at + 32, 128 * yy : 128 * yy + 128].astype(bf16)
                )
    d_in = dot_nt(d_kv, wkv[...])
    d_in = jnp.concatenate([d_in[: 2 * PART], d_in[2 * PART :] + acc[...]], axis=0)
    x = tokens()
    dx, g_in = norm_back(x, inv_rms(x), gin, d_in)
    gn_ref[0:1, :] = g_in
    gx_ref[...] += dx[2 * PART :]
    dx_ref[...] = dx[: 2 * PART].reshape(2, PART, D).astype(bf16)


def layer(t, x_parts, cotangent, low, cos, sin, gains, head_gains, weights):
    vmem = pl.BlockSpec(memory_space=pltpu.VMEM)
    return pl.pallas_call(
        layer_kernel,
        out_shape=(
            jax.ShapeDtypeStruct((PART, D), bf16),
            jax.ShapeDtypeStruct((PART, D), f32),
            jax.ShapeDtypeStruct((2, PART, D), bf16),
            jax.ShapeDtypeStruct((CB, GROUPS, BLOCK, 128), bf16),
            jax.ShapeDtypeStruct((8, D), f32),
        ),
        in_specs=[pl.BlockSpec(memory_space=pltpu.SMEM)] + [vmem] * 8,
        out_specs=(vmem,) * 5,
        scratch_shapes=[
            pltpu.VMEM((D + 16, 512), f32),
            pltpu.VMEM((D, 512), bf16),
            pltpu.VMEM((KEYS, D), bf16),
            pltpu.VMEM((D, KEYS), bf16),
            pltpu.VMEM((HD, KEYS), bf16),
            pltpu.VMEM((HD, KEYS), bf16),
            pltpu.VMEM((KEYS, HD), bf16),
            pltpu.VMEM((KEYS, HD), bf16),
            pltpu.VMEM((4, PART, HD), f32),
            pltpu.VMEM((4, PART, HD), bf16),
            pltpu.VMEM((4, PART, KEYS), f32),
            pltpu.VMEM((4, PART, HD), bf16),
            pltpu.VMEM((PART, D), bf16),
            pltpu.VMEM((D, PART), bf16),
            pltpu.VMEM((8, PART, 256), f32),
            pltpu.VMEM((8, PART, 256), f32),
            pltpu.VMEM((8, PART, 256), bf16),
            pltpu.VMEM((PART, D), f32),
            pltpu.VMEM((1, HD), f32),
            pltpu.VMEM((HD, KEYS), f32),
            pltpu.VMEM((HD, KEYS), f32),
            pltpu.VMEM((KEYS, HD), f32),
            pltpu.VMEM((PART, D), f32),
            pltpu.VMEM((PART, D), f32),
        ],
        compiler_params=pltpu.CompilerParams(vmem_limit_bytes=60 << 20),
        name="layer",
    )(t, x_parts, cotangent, low, cos, sin, gains, head_gains, weights)


def slab_shape(gathered, rows):
    x = (2,) if "x" in gathered else ()
    y = (4,) if "y" in gathered else ()
    z = (4,) if "z" in gathered else ()
    return x + y + x + z + (rows, 128)


def add_blocks(acc, p, axis, value, gathered, first, rows, terms):
    sizes = slab_shape(gathered, rows)[:-2]
    count = 1
    for n in sizes:
        count *= n

    def step(i, _):
        index = []
        rest = i
        for n in reversed(sizes):
            index.append(rest % n)
            rest = rest // n
        index = index[::-1]
        at = iter(index)
        x_lo = next(at) if "x" in gathered else (value if axis == "x" else p["x"]) % 2
        y = next(at) if "y" in gathered else (value if axis == "y" else p["y"])
        x_hi = next(at) if "x" in gathered else (value if axis == "x" else p["x"]) // 2
        z = next(at) if "z" in gathered else (value if axis == "z" else p["z"])
        target = (x_lo, y, x_hi, z, pl.ds(first, rows), slice(None))
        total = acc[target].astype(f32)
        for term in terms:
            total = total + term[tuple(index)].astype(f32)
        acc[target] = total.astype(bf16)
        return 0

    if count == 1:
        step(0, 0)
    else:
        lax.fori_loop(0, count, step, 0)


def reduce_kernel(
    g_ref, dx_ref, gx_ref, gn_ref, shard_ref, kv_ref, gx_out, gn_out,
    acc, other, *rest,
):
    bufs, rest = rest[:27], rest[27:]
    (
        dx_got, gn_now, gn_got, parts, final,
        load, sib_send, sib_recv, ring_send, ring_recv, one_send, one_recv, kv_send, kv_recv,
        dx_send, dx_recv, gn_send, gn_recv,
    ) = rest
    p = place()
    t = lax.axis_index("tensor")
    dp = lax.axis_index("dp")
    y, core = p["y"], p["c"]
    sibling = moved(p, "c", 1)
    every = slice(None)
    loads = []
    for lane, (at, rows, _) in enumerate(LANES):
        src = g_ref.at[:, core, :, :, :, pl.ds(at, rows), :]
        loads.append(pltpu.make_async_copy(src, acc.at[:, :, :, :, pl.ds(at, rows), :], load.at[lane]))
        loads[-1].start()
    gn_now[0] = gn_ref[...]
    greet(p)

    pending = []
    first = []
    for lane, (at, rows, _) in enumerate(LANES):
        src = g_ref.at[:, sibling["c"], :, :, :, pl.ds(at, rows), :]
        dst = other.at[:, :, :, :, pl.ds(at, rows), :]
        first.append(send(src, dst, sib_send.at[lane], sib_recv.at[lane], sibling))

    def dx_copy(k):
        return pltpu.make_async_remote_copy(
            src_ref=dx_ref.at[2 - k],
            dst_ref=dx_got.at[k - 1],
            send_sem=dx_send.at[k - 1],
            recv_sem=dx_recv.at[k - 1],
            device_id={"dp": dp, "tensor": jnp.maximum(t - k, 0)},
            device_id_type=MESH,
        )

    for k in (1, 2):
        @pl.when(t - k >= 0)
        def _(k=k):
            dx_copy(k).start()

    def pair(i):
        if i == 6:
            return sibling
        axis = "xyz"[i // 2]
        m = p[axis]
        q = dict(p)
        q[axis] = (m // 2) * 2 + (1 - m % 2) if i % 2 == 0 else 3 - m
        return q

    gn_copies = []

    def gn_start(i):
        gn_copies.append(send(gn_now.at[i], gn_got.at[i], gn_send.at[i], gn_recv.at[i], pair(i)))

    def gn_add(i):
        gn_copies[i].wait_recv()
        gn_now[i + 1] = gn_now[i] + gn_got[i]

    gn_start(0)
    for phase in (2, 1, 0):
        stage = 2 - phase
        step_one = []
        for lane, (at, rows, order) in enumerate(LANES):
            axis, gathered = order[phase], order[:phase]
            up, down = moved(p, axis, 1), moved(p, axis, 3)
            far = (p[axis] + 2) % 4
            b = bufs[lane * 9 + stage * 3 : lane * 9 + stage * 3 + 3]
            low, high = halves(at, rows)
            if stage == 0:
                loads[lane].wait()
                first[lane].wait_recv()
                for value in range(4):
                    add_blocks(
                        acc, p, axis, value, gathered, at, rows,
                        [slab(other, p, axis, value, gathered, at, rows)],
                    )
            sems = ring_send.at[lane, stage], ring_recv.at[lane, stage]
            low_buf = b[0].at[(slice(None),) * (len(b[0].shape) - 2) + (pl.ds(0, low[1]),)]
            high_buf = b[0].at[(slice(None),) * (len(b[0].shape) - 2) + (pl.ds(low[1], high[1]),)]
            one = send(slab(acc, p, axis, far, gathered, *low), low_buf, sems[0].at[0], sems[1].at[0], up)
            two = send(slab(acc, p, axis, far, gathered, *high), high_buf, sems[0].at[1], sems[1].at[1], down)
            step_one.append((one, two, low_buf, high_buf))
        gn_add(2 * stage)
        gn_start(2 * stage + 1)
        step_two = []
        for lane, (at, rows, order) in enumerate(LANES):
            axis, gathered = order[phase], order[:phase]
            up, down = moved(p, axis, 1), moved(p, axis, 3)
            b = bufs[lane * 9 + stage * 3 : lane * 9 + stage * 3 + 3]
            low, high = halves(at, rows)
            one, two, low_buf, high_buf = step_one[lane]
            sems = ring_send.at[lane, stage], ring_recv.at[lane, stage]
            one.wait_recv()
            add_blocks(acc, p, axis, up[axis], gathered, *low, [low_buf])
            three = send(slab(acc, p, axis, up[axis], gathered, at, rows), b[1], sems[0].at[2], sems[1].at[2], up)
            two.wait_recv()
            add_blocks(acc, p, axis, down[axis], gathered, *high, [high_buf])
            four = send(slab(acc, p, axis, down[axis], gathered, at, rows), b[2], sems[0].at[3], sems[1].at[3], down)
            step_two.append((three, four))
            pending += [one, two, three, four]
        gn_add(2 * stage + 1)
        gn_start(2 * stage + 2)
        for lane, (at, rows, order) in enumerate(LANES):
            axis, gathered = order[phase], order[:phase]
            b = bufs[lane * 9 + stage * 3 : lane * 9 + stage * 3 + 3]
            three, four = step_two[lane]
            three.wait_recv()
            four.wait_recv()
            add_blocks(acc, p, axis, p[axis], gathered, at, rows, [b[1], b[2]])

    mine = acc[p["x"] % 2, y, p["x"] // 2, p["z"]].astype(f32)
    for i, at in enumerate((0, G0, U0, D0)):
        for j in range(4):
            parts[j, 0:20, 128 * i : 128 * i + 128] = mine[at + 20 * j : at + 20 * j + 20]
    for j in range(4):
        parts[j, :, 512:640] = mine[KV0 : KV0 + 24]
    last = []
    for k in (1, 3, 2):
        q = moved(p, "y", k)
        last.append(send(parts.at[q["y"]], final.at[y], one_send.at[k - 1], one_recv.at[k - 1], q))
    final[pl.ds(y, 1)] = parts[pl.ds(y, 1)]
    gn_add(6)
    gn_out[...] = gn_now[7]
    for copy in last:
        copy.wait_recv()
    shard_ref[...] = final[:, :, :512]

    def kv_copy(k):
        return pltpu.make_async_remote_copy(
            src_ref=final.at[:, :, pl.ds(512, 128)],
            dst_ref=kv_ref,
            send_sem=kv_send.at[k - 1],
            recv_sem=kv_recv,
            device_id={"dp": dp, "tensor": (t + k) % 4},
            device_id_type=MESH,
        )

    @pl.when(t == y)
    def _():
        for k in (1, 2, 3):
            kv_copy(k).start()
        kv_ref[...] = final[:, :, 512:640]

    total = gx_ref[...]
    gx_out[...] = total
    for k in (1, 2):
        @pl.when(t + k <= 3)
        def _(k=k):
            dx_copy(k).wait_recv()
            gx_out[...] += dx_got[k - 1].astype(f32)

        @pl.when(t - k >= 0)
        def _(k=k):
            dx_copy(k).wait_send()

    for copy in first + pending + gn_copies + last:
        copy.wait_send()

    @pl.when(t == y)
    def _():
        for k in (1, 2, 3):
            kv_copy(k).wait_send()

    @pl.when(t != y)
    def _():
        kv_copy(1).wait_recv()


def reduce(grads, dx, gx, gn):
    dma = pltpu.SemaphoreType.DMA
    vmem = pl.BlockSpec(memory_space=pltpu.VMEM)
    hbm = pl.BlockSpec(memory_space=pl.ANY)
    bufs = []
    for _, rows, order in LANES:
        for phase in (2, 1, 0):
            shape = slab_shape(order[:phase], rows)
            bufs += [pltpu.VMEM(shape, bf16)] * 3
    return pl.pallas_call(
        reduce_kernel,
        out_shape=(
            jax.ShapeDtypeStruct((4, 24, 512), f32),
            jax.ShapeDtypeStruct((4, 24, 128), f32),
            jax.ShapeDtypeStruct((PART, D), f32),
            jax.ShapeDtypeStruct((8, D), f32),
        ),
        in_specs=[hbm, hbm, vmem, vmem],
        out_specs=(vmem,) * 4,
        scratch_shapes=[
            pltpu.VMEM((2, 4, 2, 4, BLOCK, 128), bf16),
            pltpu.VMEM((2, 4, 2, 4, BLOCK, 128), bf16),
            *bufs,
            pltpu.VMEM((2, PART, D), bf16),
            pltpu.VMEM((8, 8, D), f32),
            pltpu.VMEM((7, 8, D), f32),
            pltpu.VMEM((4, 24, D), f32),
            pltpu.VMEM((4, 24, D), f32),
            dma((3,)), dma((3,)), dma((3,)), dma((3, 3, 4)), dma((3, 3, 4)), dma((3,)), dma((3,)), dma((3,)), dma,
            dma((2,)), dma((2,)), dma((7,)), dma((7,)),
        ],
        compiler_params=pltpu.CompilerParams(
            collective_id=1, has_side_effects=True, vmem_limit_bytes=48 << 20
        ),
        name="reduce_gradients",
    )(grads, dx, gx, gn)


def window_rows(seg_ids, t):
    index = jnp.arange(seg_ids.shape[0], dtype=jnp.int32)
    n0 = jnp.sum((seg_ids == 0).astype(jnp.int32))
    n1 = jnp.sum((seg_ids <= 1).astype(jnp.int32))
    start = jnp.where(seg_ids == 0, 0, jnp.where(seg_ids == 1, n0, n1))
    positions = jnp.pad(index - start, (2 * PART, 0))
    positions = lax.dynamic_slice_in_dim(positions, t * PART, KEYS)
    low = jnp.maximum(index - (WINDOW - 1), start)
    low = lax.dynamic_slice_in_dim(low, t * PART, PART) - (t - 2) * PART
    return positions, low[:, None]


def shard_blocks(w_query, w_keyval, w_out, w_gate, w_up, w_down):
    out_t = w_out.T
    first = jnp.concatenate([w_query, out_t], axis=1)
    parts = [first, w_gate, w_up, w_down.T, w_keyval]
    rows = jnp.stack([item.reshape(20, 4, 128) for item in parts], axis=2)
    rows = jnp.moveaxis(rows.reshape(20, 4, 640), 1, 0)
    return jnp.pad(rows, ((0, 0), (0, 12), (0, 0)))


def per_device(
    tokens, segments, cotangent, w_query, w_keyval, w_out, w_gate, w_up, w_down,
    gain_in, gain_post_attn, gain_pre_ff, gain_post_ff, gain_query, gain_key,
):
    t = lax.axis_index("tensor")
    weights, x_parts = gather(shard_blocks(w_query, w_keyval, w_out, w_gate, w_up, w_down), tokens)
    positions, low = window_rows(segments[0], t)
    inv_freq = rope_base ** (-jnp.arange(0, HD, 2).astype(f32) / HD)
    angles = positions.astype(f32)[:, None] * inv_freq[None, :]
    gains = jnp.stack([gain_in, gain_post_attn, gain_pre_ff, gain_post_ff])
    head_gains = jnp.stack([gain_query, gain_key])
    output, gx, dx, grads, gn = layer(
        t.reshape(1), x_parts, cotangent, low, jnp.cos(angles), jnp.sin(angles), gains, head_gains,
        weights.reshape(CB, GROUPS, BLOCK, 128),
    )
    shard, kv, grad_x, gn = reduce(grads.reshape(2, 2, 4, 2, 4, BLOCK, 128), dx, gx, gn)
    rows = shard[:, :20].reshape(4, 20, 4, 128)
    first, gate, up, down = (jnp.moveaxis(rows[:, :, i], 0, 1).reshape(20, 512) for i in range(4))
    grad_kv = jnp.moveaxis(kv[:, :20], 0, 1).reshape(20, 512)
    return (
        output, grad_x, first[:, :256], grad_kv, first[:, 256:].T, gate, up, down.T,
        gn[0], gn[1], gn[2], gn[3], gn[4, :HD], gn[5, :HD],
    )


def solution(mesh):
    tok = P(("dp", "tensor"), None)
    weights = (
        P("dp", "tensor"), P("dp", None), P("tensor", "dp"), P("dp", "tensor"), P("dp", "tensor"), P("tensor", "dp"),
    )
    return jax.shard_map(
        per_device,
        mesh=mesh,
        in_specs=(tok, P("dp", None), tok) + weights + (P(),) * 6,
        out_specs=(tok, tok) + weights + (P(),) * 6,
        check_vma=False,
    )
```

```python
import jax
import jax.numpy as jnp
import numpy as np
from jax import lax
from jax.experimental import pallas as pl
from jax.experimental.pallas import tpu as pltpu
from jax.sharding import PartitionSpec as P

HD = 256
WINDOW = 512
D = 640
PART = 256
KEYS = 768
BLOCK = 352
CB = 16
GROUPS = 8
KV0, G0, U0, D0 = 80, 112, 192, 272
ATTN = ((0, 0, 48, "xyz"), (1, 48, 32, "yzx"), (2, 80, 32, "zxy"))
FEED = ((3, 112, 80, "xyz"), (4, 192, 80, "yzx"), (5, 272, 80, "zxy"))
LANES = ATTN + FEED
norm_eps = 1e-06
rope_base = 10000.0
MESH = pl.DeviceIdType.MESH
f32 = jnp.float32
bf16 = jnp.bfloat16


def place():
    dp = lax.axis_index("dp")
    t = lax.axis_index("tensor")
    return {
        "x": (dp // 16) * 2 + t // 2,
        "y": dp % 4,
        "z": (dp // 4) % 4,
        "c": t % 2,
    }


def device_of(p):
    return {
        "dp": (p["x"] // 2) * 16 + p["z"] * 4 + p["y"],
        "tensor": (p["x"] % 2) * 2 + p["c"],
    }


def moved(p, axis, by):
    size = 2 if axis == "c" else 4
    q = dict(p)
    q[axis] = (p[axis] + by) % size
    return q


def diagonal(p):
    q = moved(p, "c", 1)
    q["x"] = (p["x"] // 2) * 2 + (1 - p["x"] % 2)
    return q


def peers_of(p):
    found = [
        moved(p, axis, by)
        for axis, by in (("x", 1), ("x", 3), ("y", 1), ("y", 2), ("y", 3), ("z", 1), ("z", 3), ("c", 1))
    ]
    return found + [diagonal(p)]


def greet(p):
    barrier = pltpu.get_barrier_semaphore()
    peers = peers_of(p)
    for q in peers:
        pl.semaphore_signal(barrier, inc=1, device_id=device_of(q), device_id_type=MESH)
    pl.semaphore_wait(barrier, len(peers))


def send(src, dst, send_sem, recv_sem, q):
    copy = pltpu.make_async_remote_copy(
        src_ref=src,
        dst_ref=dst,
        send_sem=send_sem,
        recv_sem=recv_sem,
        device_id=device_of(q),
        device_id_type=MESH,
    )
    copy.start()
    return copy


def slab(ref, p, axis, value, gathered, first, rows, core=None):
    at = {a: (value if a == axis else p[a]) for a in "xyz"}
    every = slice(None)
    x_lo = every if "x" in gathered else at["x"] % 2
    x_hi = every if "x" in gathered else at["x"] // 2
    y = every if "y" in gathered else at["y"]
    z = every if "z" in gathered else at["z"]
    where = (x_lo,) + (() if core is None else (core,)) + (y, x_hi, z, pl.ds(first, rows), every)
    return ref.at[where]


def halves(first, rows):
    top = rows // 32 * 16 + (16 if rows % 32 else 0)
    return ((first, top), (first + top, rows - top))


def gather_steps(lanes, w_ref, p, sems):
    ring_send, ring_recv, sib_send, sib_recv = sems
    core = p["c"]
    sibling = moved(p, "c", 1)
    pending, to_sibling, passed = [], [], []

    def share(part, lane, i):
        to_sibling.append(send(part, part, sib_send.at[lane, i], sib_recv.at[lane, i], sibling))

    def arrived(phase):
        for i, (lane, at, rows, order) in enumerate(lanes):
            axis, gathered = order[phase], order[:phase]
            for j in range(2):
                passed[2 * i + j].wait_recv()
                if phase == 2:
                    far = (p[axis] + 2) % 4
                    share(slab(w_ref, p, axis, far, gathered, *halves(at, rows)[j], core), lane, 3 + j)
        pending.extend(passed)
        passed.clear()

    for phase in range(3):
        if phase:
            arrived(phase - 1)
        started = []
        for lane, at, rows, order in lanes:
            axis, gathered = order[phase], order[:phase]
            mine = slab(w_ref, p, axis, p[axis], gathered, at, rows, core)
            up, down = moved(p, axis, 1), moved(p, axis, 3)
            ss, rs = ring_send.at[lane, phase], ring_recv.at[lane, phase]
            started.append((send(mine, mine, ss.at[0], rs.at[0], up), send(mine, mine, ss.at[1], rs.at[1], down)))
            if phase == 2:
                share(mine, lane, 0)
        yield
        for (lane, at, rows, order), (to_up, to_down) in zip(lanes, started):
            axis, gathered = order[phase], order[:phase]
            up, down = moved(p, axis, 1), moved(p, axis, 3)
            ss, rs = ring_send.at[lane, phase], ring_recv.at[lane, phase]
            low, high = halves(at, rows)
            to_up.wait_recv()
            part = slab(w_ref, p, axis, down[axis], gathered, *low, core)
            passed.append(send(part, part, ss.at[2], rs.at[2], up))
            to_down.wait_recv()
            part = slab(w_ref, p, axis, up[axis], gathered, *high, core)
            passed.append(send(part, part, ss.at[3], rs.at[3], down))
            if phase == 2:
                for i, q in ((1, down), (2, up)):
                    share(slab(w_ref, p, axis, q[axis], gathered, at, rows, core), lane, i)
            pending.extend([to_up, to_down])
        yield
    arrived(2)
    for copy in to_sibling:
        copy.wait_recv()
    for copy in pending + to_sibling:
        copy.wait_send()
    yield


def slab_shape(gathered, rows):
    x = (2,) if "x" in gathered else ()
    y = (4,) if "y" in gathered else ()
    z = (4,) if "z" in gathered else ()
    return x + y + x + z + (rows, 128)


def add_blocks(acc, p, axis, value, gathered, first, rows, terms):
    sizes = slab_shape(gathered, rows)[:-2]
    count = 1
    for n in sizes:
        count *= n

    def step(i, _):
        index = []
        rest = i
        for n in reversed(sizes):
            index.append(rest % n)
            rest = rest // n
        index = index[::-1]
        at = iter(index)
        x_lo = next(at) if "x" in gathered else (value if axis == "x" else p["x"]) % 2
        y = next(at) if "y" in gathered else (value if axis == "y" else p["y"])
        x_hi = next(at) if "x" in gathered else (value if axis == "x" else p["x"]) // 2
        z = next(at) if "z" in gathered else (value if axis == "z" else p["z"])
        target = (x_lo, p["c"], y, x_hi, z, pl.ds(first, rows), slice(None))
        total = acc[target].astype(f32)
        for term in terms:
            total = total + term[tuple(index)].astype(f32)
        acc[target] = total.astype(bf16)
        return 0

    if count == 1:
        step(0, 0)
    else:
        lax.fori_loop(0, count, step, 0)


def reduce_steps(lanes, g_ref, other, bufs, p, sems):
    ring_send, ring_recv, sib_send, sib_recv = sems
    core = p["c"]
    sibling = moved(p, "c", 1)
    pending, from_sibling = [], {}
    for by in (2, 1, 3, 0):
        for lane, at, rows, order in lanes:
            axis, gathered = order[2], order[:2]
            value = (p[axis] + by) % 4
            src = slab(g_ref, p, axis, value, gathered, at, rows, sibling["c"])
            dst = slab(other, p, axis, value, gathered, at, rows)
            from_sibling[lane, by] = send(src, dst, sib_send.at[lane, by], sib_recv.at[lane, by], sibling)
    yield

    def sibling_part(lane, by, axis, gathered, at, rows):
        from_sibling[lane, by].wait_recv()
        return slab(other, p, axis, (p[axis] + by) % 4, gathered, at, rows)

    for stage in range(3):
        phase = 2 - stage
        one_step = []
        for lane, at, rows, order in lanes:
            axis, gathered = order[phase], order[:phase]
            up, down = moved(p, axis, 1), moved(p, axis, 3)
            far = (p[axis] + 2) % 4
            b = bufs[lane * 9 + stage * 3]
            low, high = halves(at, rows)
            if stage == 0:
                term = sibling_part(lane, 2, axis, gathered, at, rows)
                add_blocks(g_ref, p, axis, far, gathered, at, rows, [term])
            ss, rs = ring_send.at[lane, stage], ring_recv.at[lane, stage]
            lead = (slice(None),) * (len(b.shape) - 2)
            low_buf = b.at[lead + (pl.ds(0, low[1]), slice(None))]
            high_buf = b.at[lead + (pl.ds(low[1], high[1]), slice(None))]
            one = send(slab(g_ref, p, axis, far, gathered, *low, core), low_buf, ss.at[0], rs.at[0], up)
            two = send(slab(g_ref, p, axis, far, gathered, *high, core), high_buf, ss.at[1], rs.at[1], down)
            one_step.append((one, two, low_buf, high_buf))
        yield
        two_step = []
        for (lane, at, rows, order), (one, two, low_buf, high_buf) in zip(lanes, one_step):
            axis, gathered = order[phase], order[:phase]
            up, down = moved(p, axis, 1), moved(p, axis, 3)
            b = bufs[lane * 9 + stage * 3 : lane * 9 + stage * 3 + 3]
            low, high = halves(at, rows)
            ss, rs = ring_send.at[lane, stage], ring_recv.at[lane, stage]
            if stage == 0:
                for by, q in ((1, up), (3, down)):
                    term = sibling_part(lane, by, axis, gathered, at, rows)
                    add_blocks(g_ref, p, axis, q[axis], gathered, at, rows, [term])
            one.wait_recv()
            add_blocks(g_ref, p, axis, up[axis], gathered, *low, [low_buf])
            three = send(slab(g_ref, p, axis, up[axis], gathered, at, rows, core), b[1], ss.at[2], rs.at[2], up)
            two.wait_recv()
            add_blocks(g_ref, p, axis, down[axis], gathered, *high, [high_buf])
            four = send(slab(g_ref, p, axis, down[axis], gathered, at, rows, core), b[2], ss.at[3], rs.at[3], down)
            two_step.append((three, four))
            pending.extend([one, two, three, four])
        yield
        for (lane, at, rows, order), (three, four) in zip(lanes, two_step):
            axis, gathered = order[phase], order[:phase]
            b = bufs[lane * 9 + stage * 3 : lane * 9 + stage * 3 + 3]
            terms = [b[1], b[2]]
            if stage == 0:
                terms.append(sibling_part(lane, 0, axis, gathered, at, rows))
            three.wait_recv()
            four.wait_recv()
            add_blocks(g_ref, p, axis, p[axis], gathered, at, rows, terms)
        if stage == 2:
            for copy in pending + list(from_sibling.values()):
                copy.wait_send()
        yield


def dot(a, b):
    return jnp.dot(a, b, preferred_element_type=f32)


def dot_nt(a, b):
    return lax.dot_general(a, b, (((1,), (1,)), ((), ())), preferred_element_type=f32)


def inv_rms(v):
    return lax.rsqrt(jnp.mean(v * v, axis=-1, keepdims=True) + norm_eps)


def norm_back(v, r, c, e):
    ec = e * c
    vr = v * r
    dv = r * (ec - vr * jnp.mean(vr * ec, axis=-1, keepdims=True))
    return dv, jnp.sum(e * vr, axis=0, keepdims=True)


def turn(u, cos, sin):
    a, b = u[:, :128], u[:, 128:]
    return jnp.concatenate([a * cos - b * sin, b * cos + a * sin], axis=1)


def turn_back(e, cos, sin):
    a, b = e[:, :128], e[:, 128:]
    return jnp.concatenate([a * cos + b * sin, b * cos - a * sin], axis=1)


def columns(w_ref, t, y, first):
    return jnp.concatenate(
        [w_ref[t // 2, t % 2, y + i, :, :, first : first + 80, :].reshape(D, 128) for i in range(2)], axis=1
    )


def put_columns(g_ref, t, y, first, value):
    value = value.astype(bf16)
    for i in range(2):
        g_ref[t // 2, t % 2, y + i, :, :, first : first + 80, :] = (
            value[:, 128 * i : 128 * i + 128].reshape(2, 4, 80, 128)
        )


NB = 9 * len(LANES)


def kernel(
    seg_ref, wq_ref, wkv_ref, wo_ref, wg_ref, wu_ref, wd_ref, x_ref, cot_ref,
    gin_ref, gpa_ref, gpf_ref, gpo_ref, gq_ref, gk_ref, cos_tab, sin_tab, freq_ref,
    out_ref, gx_ref, shard_ref, kv_ref, gn_out,
    *scratch,
):
    bufs, scratch = scratch[:NB], scratch[NB:]
    (
        w_ref, g_ref, other, xg, rows_s, s_ref, got, stage,
        cos_ref, sin_ref, wkv, attn_in, attn_in_t, kt, vt, kb, vb, qraw, qb, probs, ctx,
        mlp_in, mlp_in_t, d_b, d_t, act_s, dact_s, hid_s, acc, acc2, dkt, dvt, proj_s,
        dx_got, gn_now, gn_got, final,
        one_send, one_recv, ring_send, ring_recv, sib_send, sib_recv, x_send, x_recv,
        back_send, back_recv, bsib_send, bsib_recv, last_send, last_recv, kv_send, kv_recv,
        dx_send, dx_recv, gn_send, gn_recv,
    ) = scratch
    p = place()
    t = lax.axis_index("tensor")
    dp = lax.axis_index("dp")
    y = p["y"]
    core = p["c"]
    own = (p["x"] % 2, core, y, p["x"] // 2, p["z"])
    greet(p)

    rows_s[...] = jnp.zeros_like(rows_s)
    out_t = wo_ref[...].astype(f32).T
    down_t = wd_ref[...].astype(f32).T
    for j in range(4):
        if j < 2:
            rows_s[j, :20, :128] = wq_ref[:, 128 * j : 128 * j + 128].astype(f32)
        else:
            rows_s[j, :20, :128] = out_t[:, 128 * j - 256 : 128 * j - 128]
        rows_s[j, :20, 128:256] = wg_ref[:, 128 * j : 128 * j + 128].astype(f32)
        rows_s[j, :20, 256:384] = wu_ref[:, 128 * j : 128 * j + 128].astype(f32)
        rows_s[j, :20, 384:512] = down_t[:, 128 * j : 128 * j + 128]
        rows_s[j, :20, 512:] = wkv_ref[:, 128 * j : 128 * j + 128].astype(f32)
    s_ref[...] = rows_s[...].astype(bf16)
    first = []
    for k in (1, 3, 2):
        q = moved(p, "y", k)
        first.append(send(s_ref.at[q["y"]], got.at[y], one_send.at[k - 1], one_recv.at[k - 1], q))

    def token_copy(src, slot, to):
        return pltpu.make_async_remote_copy(
            src_ref=src, dst_ref=xg.at[slot], send_sem=x_send.at[1 - slot], recv_sem=x_recv.at[1 - slot],
            device_id={"dp": dp, "tensor": to}, device_id_type=MESH,
        )

    @pl.when(t < 3)
    def _():
        token_copy(x_ref, 1, jnp.minimum(t + 1, 3)).start()

    @pl.when(t == 0)
    def _():
        token_copy(x_ref, 0, t + 2).start()

    xg[2] = x_ref[...]
    got[pl.ds(y, 1)] = s_ref[pl.ds(y, 1)]
    for copy in first:
        copy.wait_recv()
    for j in range(4):
        stage[20 * j : 20 * j + 20, :] = got[j].astype(f32)[:20, :512]
    for i, at in enumerate((0, G0, U0, D0)):
        w_ref[own + (slice(at, at + 80),)] = stage[:80, 128 * i : 128 * i + 128].astype(bf16)
    w_ref[own + (slice(KV0, KV0 + 32),)] = got[pl.ds(t, 1)][0, :, 512:640]
    for copy in first:
        copy.wait_send()

    sems = (ring_send, ring_recv, sib_send, sib_recv)
    attn = gather_steps(ATTN, w_ref, p, sems)
    feed = gather_steps(FEED, w_ref, p, sems)
    for _ in range(2):
        next(attn), next(feed)
    for _ in range(2):
        next(attn), next(feed)
    next(attn)

    gin, gpa, gpf, gpo, gq, gk = (
        ref[...].reshape(1, ref.shape[0]) for ref in (gin_ref, gpa_ref, gpf_ref, gpo_ref, gq_ref, gk_ref)
    )
    scale = HD ** -0.5
    seg = seg_ref[...]
    n0 = jnp.sum(jnp.where(seg == 0, 1.0, 0.0), axis=1, keepdims=True)
    n1 = jnp.sum(jnp.where(seg <= 1, 1.0, 0.0), axis=1, keepdims=True)
    base = ((t - 2) * PART).astype(f32)
    which = lax.broadcasted_iota(jnp.int32, (8, 128), 0)
    turn_by = (jnp.where(which == 0, 0.0, jnp.where(which == 1, n0, n1)) - base) * freq_ref[...]
    cb, sb = jnp.cos(turn_by), jnp.sin(turn_by)
    token = lax.broadcasted_iota(jnp.int32, (KEYS, 1), 0).astype(f32) + base
    in0, in1 = token < n0, token < n1
    cd = jnp.where(in0, cb[0:1], jnp.where(in1, cb[1:2], cb[2:3]))
    sd = jnp.where(in0, sb[0:1], jnp.where(in1, sb[1:2], sb[2:3]))
    ca, sa = cos_tab[...], sin_tab[...]
    cos_ref[...] = ca * cd + sa * sd
    sin_ref[...] = sa * cd - ca * sd

    @pl.when(t > 0)
    def _():
        token_copy(x_ref, 1, jnp.minimum(t + 1, 3)).wait_recv()

    @pl.when(t == 2)
    def _():
        token_copy(xg.at[1], 0, jnp.minimum(t + 1, 3)).start()

    @pl.when(t >= 2)
    def _():
        token_copy(x_ref, 0, jnp.minimum(t + 1, 3)).wait_recv()

    @pl.when(t < 3)
    def _():
        token_copy(x_ref, 1, jnp.minimum(t + 1, 3)).wait_send()

    @pl.when(lax.rem(t, 2) == 0)
    def _():
        token_copy(x_ref, 0, jnp.minimum(t + 1, 3)).wait_send()

    def tokens(i):
        return jnp.where(i >= 2 - t, xg[i].astype(f32), 0.0)

    def input_norm(i, _):
        x = tokens(i)
        a = x * inv_rms(x) * gin
        attn_in[i] = a.astype(bf16)
        attn_in_t[i] = a.T.astype(bf16)
        return 0

    lax.fori_loop(0, 3, input_norm, 0)
    acc[...] = jnp.zeros_like(acc)
    next(attn)
    next(feed)
    next(attn)

    def keyval_in(g, _):
        for tt in range(4):
            for yy in range(4):
                stage[20 * tt : 20 * tt + 20, 128 * yy : 128 * yy + 128] = (
                    w_ref[tt // 2, tt % 2, yy, g // 4, g % 4, KV0 : KV0 + 32, :].astype(f32)[:20]
                )
        wkv[g] = stage[:80, :].astype(bf16)
        return 0

    lax.fori_loop(0, GROUPS, keyval_in, 0)

    def rows_of(i):
        return pl.ds(pl.multiple_of(i * PART, PART), PART)

    def keys_values(i, _):
        rows = rows_of(i)
        kv_raw = dot(attn_in[i], wkv[...].reshape(D, 512))
        kraw = kv_raw[:, :HD]
        k = turn(kraw * inv_rms(kraw) * gk, cos_ref[rows, :], sin_ref[rows, :])
        kb[rows, :] = k.astype(bf16)
        kt[:, rows] = k.T.astype(bf16)
        v = kv_raw[:, HD:]
        vb[rows, :] = v.astype(bf16)
        vt[:, rows] = v.T.astype(bf16)
        return 0

    lax.fori_loop(0, 3, keys_values, 0)

    def head(h, _):
        cos_q, sin_q = cos_ref[2 * PART :, :], sin_ref[2 * PART :, :]
        column = lax.broadcasted_iota(jnp.int32, (PART, KEYS), 1)
        last = lax.broadcasted_iota(jnp.int32, (PART, 1), 0) + 2 * PART
        own_token = last.astype(f32) + base
        start = jnp.where(own_token < n0, 0.0, jnp.where(own_token < n1, n0, n1))
        low = jnp.maximum(own_token - (WINDOW - 1), start) - base
        raw = dot(attn_in[2], columns(w_ref, h, 0, 0))
        qraw[h] = raw
        q = turn(raw * inv_rms(raw) * gq, cos_q, sin_q).astype(bf16)
        qb[h] = q
        s = dot(q, kt[...]) * scale
        s = jnp.where((column.astype(f32) >= low) & (column <= last), s, -1e30)
        e = jnp.exp(s - jnp.max(s, axis=-1, keepdims=True))
        pr = e / jnp.sum(e, axis=-1, keepdims=True)
        probs[h] = pr
        c = dot(pr.astype(bf16), vb[...]).astype(bf16)
        ctx[h] = c
        acc[...] += dot_nt(c, columns(w_ref, h, 2, 0))
        return 0

    lax.fori_loop(0, 3, head, 0)
    next(feed)
    lax.fori_loop(3, 4, head, 0)
    proj = acc[...]
    proj_s[...] = proj
    mid = x_ref[...].astype(f32) + proj * inv_rms(proj) * gpa
    gx_ref[...] = mid
    m = mid * inv_rms(mid) * gpf
    mlp_in[...] = m.astype(bf16)
    mlp_in_t[...] = m.T.astype(bf16)
    acc[...] = jnp.zeros_like(acc)
    next(feed)

    def feed_forward(c, _):
        tt, yy = c // 2, 2 * (c % 2)
        gate = dot(mlp_in[...], columns(w_ref, tt, yy, G0))
        up = dot(mlp_in[...], columns(w_ref, tt, yy, U0))
        k0, k1 = 0.7978845608028654, 0.044715
        sq = gate * gate
        th = jnp.tanh(k0 * (gate + k1 * gate * sq))
        half = 0.5 * (1.0 + th)
        act = gate * half
        hid = (act * up).astype(bf16)
        act_s[c] = act
        dact_s[c] = up * (half + 0.5 * gate * (1.0 - th * th) * (k0 + (3.0 * k0 * k1) * sq))
        hid_s[c] = hid
        acc[...] += dot_nt(hid, columns(w_ref, tt, yy, D0))
        return 0

    lax.fori_loop(0, 8, feed_forward, 0)
    mlp = acc[...]
    r = inv_rms(mlp)
    out_ref[...] = (gx_ref[...] + mlp * r * gpo).astype(bf16)
    d_mlp, g_po = norm_back(mlp, r, gpo, cot_ref[...].astype(f32))
    gn_now[0, 3:4, :] = g_po
    d_b[...] = d_mlp.astype(bf16)
    d_t[...] = d_mlp.T.astype(bf16)
    acc[...] = jnp.zeros_like(acc)

    def feed_back(c, _):
        tt, yy = c // 2, 2 * (c % 2)
        put_columns(g_ref, tt, yy, D0, dot(d_t[...], hid_s[c]))
        d_hid = dot(d_b[...], columns(w_ref, tt, yy, D0))
        d_gate = (d_hid * dact_s[c]).astype(bf16)
        d_up = (d_hid * act_s[c]).astype(bf16)
        put_columns(g_ref, tt, yy, G0, dot(mlp_in_t[...], d_gate))
        put_columns(g_ref, tt, yy, U0, dot(mlp_in_t[...], d_up))
        acc[...] += dot_nt(d_gate, columns(w_ref, tt, yy, G0)) + dot_nt(d_up, columns(w_ref, tt, yy, U0))
        return 0

    lax.fori_loop(0, 8, feed_back, 0)
    sems = (back_send, back_recv, bsib_send, bsib_recv)
    feed = reduce_steps(FEED, g_ref, other, bufs, p, sems)
    next(feed)

    mid = gx_ref[...]
    d_pre, g_pf = norm_back(mid, inv_rms(mid), gpf, acc[...])
    gn_now[0, 2:3, :] = g_pf
    d_mid = cot_ref[...].astype(f32) + d_pre
    proj = proj_s[...]
    d_proj, g_pa = norm_back(proj, inv_rms(proj), gpa, d_mid)
    gn_now[0, 1:2, :] = g_pa
    gx_ref[...] = d_mid
    d_b[...] = d_proj.astype(bf16)
    d_t[...] = d_proj.T.astype(bf16)
    dkt[...] = jnp.zeros_like(dkt)
    dvt[...] = jnp.zeros_like(dvt)
    acc[...] = jnp.zeros_like(acc)
    acc2[...] = jnp.zeros_like(acc2)
    next(feed)

    def head_back(h, _):
        cos_q, sin_q = cos_ref[2 * PART :, :], sin_ref[2 * PART :, :]
        put_columns(g_ref, h, 2, 0, dot(d_t[...], ctx[h]))
        d_ctx = dot(d_b[...], columns(w_ref, h, 2, 0))
        d_ctx_b = d_ctx.astype(bf16)
        pr = probs[h]
        d_pr = dot(d_ctx_b, vt[...])
        dvt[...] += dot(d_ctx.T.astype(bf16), pr.astype(bf16))
        inner = jnp.sum(pr * d_pr, axis=-1, keepdims=True)
        ds = (pr * (d_pr - inner)).astype(bf16)
        dq = dot(ds, kb[...]) * scale
        dkt[...] += dot(qb[h].astype(f32).T.astype(bf16), ds)
        raw = qraw[h]
        d_raw, g_q = norm_back(raw, inv_rms(raw), gq, turn_back(dq, cos_q, sin_q))
        acc2[...] += g_q
        d_raw = d_raw.astype(bf16)
        put_columns(g_ref, h, 0, 0, dot(attn_in_t[2], d_raw))
        acc[...] += dot_nt(d_raw, columns(w_ref, h, 0, 0))
        return 0

    lax.fori_loop(0, 2, head_back, 0)
    next(feed)
    lax.fori_loop(2, 4, head_back, 0)
    gn_now[0, 4:8, :] = jnp.zeros((4, D), f32)
    gn_now[0, 4:5, :HD] = acc2[...]
    acc2[...] = jnp.zeros_like(acc2)

    def keys_values_back(i, _):
        rows = rows_of(i)
        raw = dot(attn_in[i], wkv[:, :, :HD].reshape(D, HD))
        e = turn_back(dkt[:, rows].T * scale, cos_ref[rows, :], sin_ref[rows, :])
        dk, g_k = norm_back(raw, inv_rms(raw), gk, e)
        acc2[...] += g_k
        kb[rows, :] = dk.astype(bf16)
        vb[rows, :] = dvt[:, rows].T.astype(bf16)
        return 0

    lax.fori_loop(0, 3, keys_values_back, 0)
    gn_now[0, 5:6, :HD] = acc2[...]
    for half, src in enumerate((kb, vb)):
        grad = sum(dot(attn_in_t[i], src[PART * i : PART * i + PART, :]) for i in range(3))
        stage[80:, :] = jnp.zeros((16, 512), f32)
        for g in range(GROUPS):
            stage[:80, :HD] = grad[80 * g : 80 * g + 80]
            for tt in range(4):
                for yy in range(2):
                    g_ref[tt // 2, tt % 2, 2 * half + yy, g // 4, g % 4, KV0 : KV0 + 32, :] = (
                        stage[20 * tt : 20 * tt + 32, 128 * yy : 128 * yy + 128].astype(bf16)
                    )
    attn = reduce_steps(ATTN, g_ref, other, bufs, p, sems)
    next(attn)

    def input_back(i, extra):
        rows = rows_of(i)
        d_in = dot_nt(kb[rows, :], wkv[:, :, :HD].reshape(D, HD)) + dot_nt(vb[rows, :], wkv[:, :, HD:].reshape(D, HD))
        x = tokens(i)
        dx, g_in = norm_back(x, inv_rms(x), gin, d_in if extra is None else d_in + extra)
        gn_now[0, 0:1, :] += g_in
        return dx

    def input_back_before(i, _):
        attn_in[i] = input_back(i, None).astype(bf16)
        return 0

    gn_now[0, 0:1, :] = jnp.zeros((1, D), f32)
    lax.fori_loop(0, 2, input_back_before, 0)
    gx_ref[...] += input_back(2, acc[...])

    def dx_copy(k):
        return pltpu.make_async_remote_copy(
            src_ref=attn_in.at[2 - k], dst_ref=dx_got.at[k - 1], send_sem=dx_send.at[k - 1], recv_sem=dx_recv.at[k - 1],
            device_id={"dp": dp, "tensor": jnp.maximum(t - k, 0)}, device_id_type=MESH,
        )

    for k in (1, 2):
        @pl.when(t - k >= 0)
        def _(k=k):
            dx_copy(k).start()

    def pair(i):
        if i == 6:
            return moved(p, "c", 1)
        axis = "xyz"[i // 2]
        m = p[axis]
        q = dict(p)
        q[axis] = (m // 2) * 2 + (1 - m % 2) if i % 2 == 0 else 3 - m
        return q

    gn_copies = []

    def gn_start(i):
        gn_copies.append(send(gn_now.at[i], gn_got.at[i], gn_send.at[i], gn_recv.at[i], pair(i)))

    def gn_add(i):
        gn_copies[i].wait_recv()
        gn_now[i + 1] = gn_now[i] + gn_got[i]

    gn_start(0)
    next(attn)
    next(feed)
    next(feed)
    gn_add(0)
    gn_start(1)
    next(attn)
    next(feed)
    gn_add(1)
    gn_start(2)
    next(attn)
    next(attn)
    next(feed)
    next(feed)
    gn_add(2)
    gn_start(3)
    next(attn)
    next(feed)
    gn_add(3)
    gn_start(4)
    next(attn)
    next(attn)
    next(feed)
    gn_add(4)
    gn_start(5)
    next(attn)
    gn_add(5)
    gn_start(6)
    next(attn)

    mine = g_ref[own].astype(f32)
    for i, at in enumerate((0, G0, U0, D0)):
        for j in range(4):
            rows_s[j, 0:20, 128 * i : 128 * i + 128] = mine[at + 20 * j : at + 20 * j + 20]
    for j in range(4):
        rows_s[j, :24, 512:] = mine[KV0 : KV0 + 24]
    last = []
    for k in (1, 3, 2):
        q = moved(p, "y", k)
        last.append(send(rows_s.at[q["y"], pl.ds(0, 24), :], final.at[y], last_send.at[k - 1], last_recv.at[k - 1], q))
    final[pl.ds(y, 1)] = rows_s[pl.ds(y, 1), :24]
    gn_add(6)
    gn_out[...] = gn_now[7]
    for k in (1, 2):
        @pl.when(t + k <= 3)
        def _(k=k):
            dx_copy(k).wait_recv()
            gx_ref[...] += dx_got[k - 1].astype(f32)

        @pl.when(t - k >= 0)
        def _(k=k):
            dx_copy(k).wait_send()

    for copy in last:
        copy.wait_recv()

    def kv_copy(k):
        return pltpu.make_async_remote_copy(
            src_ref=final.at[:, :, pl.ds(512, 128)], dst_ref=kv_ref, send_sem=kv_send.at[k - 1], recv_sem=kv_recv,
            device_id={"dp": dp, "tensor": (t + k) % 4}, device_id_type=MESH,
        )

    @pl.when(t == y)
    def _():
        for k in (1, 2, 3):
            kv_copy(k).start()
        kv_ref[...] = final[:, :, 512:640]

    shard_ref[...] = final[:, :, :512]
    for copy in gn_copies + last:
        copy.wait_send()

    @pl.when(t == y)
    def _():
        for k in (1, 2, 3):
            kv_copy(k).wait_send()

    @pl.when(t != y)
    def _():
        kv_copy(1).wait_recv()


def layer(*args):
    dma = pltpu.SemaphoreType.DMA
    vmem = pl.BlockSpec(memory_space=pltpu.VMEM)
    bufs = []
    for _, _, rows, order in LANES:
        for phase in (2, 1, 0):
            bufs += [pltpu.VMEM(slab_shape(order[:phase], rows), bf16)] * 3
    n = len(LANES)
    return pl.pallas_call(
        kernel,
        out_shape=(
            jax.ShapeDtypeStruct((PART, D), bf16),
            jax.ShapeDtypeStruct((PART, D), f32),
            jax.ShapeDtypeStruct((4, 24, 512), f32),
            jax.ShapeDtypeStruct((4, 24, 128), f32),
            jax.ShapeDtypeStruct((8, D), f32),
        ),
        in_specs=[vmem] * len(args),
        out_specs=(vmem,) * 5,
        scratch_shapes=[
            *bufs,
            pltpu.VMEM((2, 2, 4, 2, 4, BLOCK, 128), bf16),
            pltpu.VMEM((2, 2, 4, 2, 4, BLOCK, 128), bf16),
            pltpu.VMEM((2, 4, 2, 4, BLOCK, 128), bf16),
            pltpu.VMEM((3, PART, D), bf16),
            pltpu.VMEM((4, 32, D), f32),
            pltpu.VMEM((4, 32, D), bf16),
            pltpu.VMEM((4, 32, D), bf16),
            pltpu.VMEM((96, 512), f32),
            pltpu.VMEM((KEYS, 128), f32),
            pltpu.VMEM((KEYS, 128), f32),
            pltpu.VMEM((GROUPS, 80, 512), bf16),
            pltpu.VMEM((3, PART, D), bf16),
            pltpu.VMEM((3, D, PART), bf16),
            pltpu.VMEM((HD, KEYS), bf16),
            pltpu.VMEM((HD, KEYS), bf16),
            pltpu.VMEM((KEYS, HD), bf16),
            pltpu.VMEM((KEYS, HD), bf16),
            pltpu.VMEM((4, PART, HD), f32),
            pltpu.VMEM((4, PART, HD), bf16),
            pltpu.VMEM((4, PART, KEYS), f32),
            pltpu.VMEM((4, PART, HD), bf16),
            pltpu.VMEM((PART, D), bf16),
            pltpu.VMEM((D, PART), bf16),
            pltpu.VMEM((PART, D), bf16),
            pltpu.VMEM((D, PART), bf16),
            pltpu.VMEM((8, PART, 256), f32),
            pltpu.VMEM((8, PART, 256), f32),
            pltpu.VMEM((8, PART, 256), bf16),
            pltpu.VMEM((PART, D), f32),
            pltpu.VMEM((1, HD), f32),
            pltpu.VMEM((HD, KEYS), f32),
            pltpu.VMEM((HD, KEYS), f32),
            pltpu.VMEM((PART, D), f32),
            pltpu.VMEM((2, PART, D), bf16),
            pltpu.VMEM((8, 8, D), f32),
            pltpu.VMEM((7, 8, D), f32),
            pltpu.VMEM((4, 24, D), f32),
            dma((3,)), dma((3,)), dma((n, 3, 4)), dma((n, 3, 4)), dma((n, 5)), dma((n, 5)), dma((2,)), dma((2,)),
            dma((n, 3, 4)), dma((n, 3, 4)), dma((n, 4)), dma((n, 4)), dma((3,)), dma((3,)), dma((3,)), dma,
            dma((2,)), dma((2,)), dma((7,)), dma((7,)),
        ],
        compiler_params=pltpu.CompilerParams(
            collective_id=0, has_side_effects=True, vmem_limit_bytes=62 << 20
        ),
        name="layer",
    )(*args)


def rope_parts():
    freq = (rope_base ** (-np.arange(0, HD, 2, dtype=np.float64) / HD))[None, :]
    angles = np.arange(KEYS, dtype=np.float64)[:, None] * freq
    return tuple(jnp.asarray(item.astype(np.float32)) for item in (np.cos(angles), np.sin(angles), freq))


def per_device(
    tokens, segments, cotangent, w_query, w_keyval, w_out, w_gate, w_up, w_down,
    gain_in, gain_post_attn, gain_pre_ff, gain_post_ff, gain_query, gain_key,
):
    output, grad_x, shard, kv, gn = layer(
        segments, w_query, w_keyval, w_out, w_gate, w_up, w_down, tokens, cotangent,
        gain_in, gain_post_attn, gain_pre_ff, gain_post_ff, gain_query, gain_key, *rope_parts(),
    )
    rows = shard[:, :20].reshape(4, 20, 4, 128)
    first, gate, up, down = (jnp.moveaxis(rows[:, :, i], 0, 1).reshape(20, 512) for i in range(4))
    grad_kv = jnp.moveaxis(kv[:, :20], 0, 1).reshape(20, 512)
    return (
        output, grad_x, first[:, :256], grad_kv, first[:, 256:].T, gate, up, down.T,
        gn[0], gn[1], gn[2], gn[3], gn[4, :HD], gn[5, :HD],
    )


def solution(mesh):
    tok = P(("dp", "tensor"), None)
    weights = (
        P("dp", "tensor"), P("dp", None), P("tensor", "dp"), P("dp", "tensor"), P("dp", "tensor"), P("tensor", "dp"),
    )
    return jax.shard_map(
        per_device,
        mesh=mesh,
        in_specs=(tok, P("dp", None), tok) + weights + (P(),) * 6,
        out_specs=(tok, tok) + weights + (P(),) * 6,
        check_vma=False,
    )
```

```python
import jax
import jax.numpy as jnp
import numpy as np
from jax import lax
from jax.experimental import pallas as pl
from jax.experimental.pallas import tpu as pltpu
from jax.sharding import PartitionSpec as P

HD = 256
WINDOW = 512
D = 640
PART = 256
KEYS = 768
BLOCK = 352
CB = 16
GROUPS = 8
KV0, G0, U0, D0 = 80, 112, 192, 272
ATTN = ((0, 0, 48, "xyz"), (1, 48, 32, "yzx"), (2, 80, 32, "zxy"))
FEED = ((3, 112, 80, "xyz"), (4, 192, 80, "yzx"), (5, 272, 80, "zxy"))
LANES = ATTN + FEED
norm_eps = 1e-06
rope_base = 10000.0
MESH = pl.DeviceIdType.MESH
f32 = jnp.float32
bf16 = jnp.bfloat16


def place():
    dp = lax.axis_index("dp")
    t = lax.axis_index("tensor")
    return {
        "x": (dp // 16) * 2 + t // 2,
        "y": dp % 4,
        "z": (dp // 4) % 4,
        "c": t % 2,
    }


def device_of(p):
    return {
        "dp": (p["x"] // 2) * 16 + p["z"] * 4 + p["y"],
        "tensor": (p["x"] % 2) * 2 + p["c"],
    }


def moved(p, axis, by):
    size = 2 if axis == "c" else 4
    q = dict(p)
    q[axis] = (p[axis] + by) % size
    return q


def diagonal(p):
    q = moved(p, "c", 1)
    q["x"] = (p["x"] // 2) * 2 + (1 - p["x"] % 2)
    return q


def peers_of(p):
    found = [
        moved(p, axis, by)
        for axis, by in (
            ("x", 1), ("x", 2), ("x", 3), ("y", 1), ("y", 2), ("y", 3), ("z", 1), ("z", 2), ("z", 3), ("c", 1)
        )
    ]
    return found + [diagonal(p)]


def greet(p):
    barrier = pltpu.get_barrier_semaphore()
    peers = peers_of(p)
    for q in peers:
        pl.semaphore_signal(barrier, inc=1, device_id=device_of(q), device_id_type=MESH)
    pl.semaphore_wait(barrier, len(peers))


def send(src, dst, send_sem, recv_sem, q):
    copy = pltpu.make_async_remote_copy(
        src_ref=src,
        dst_ref=dst,
        send_sem=send_sem,
        recv_sem=recv_sem,
        device_id=device_of(q),
        device_id_type=MESH,
    )
    copy.start()
    return copy


def block_of(ref, at, first, rows, core=None):
    every = slice(None)
    where = (at["x"] % 2,) + (() if core is None else (core,)) + (at["y"], at["x"] // 2, at["z"], pl.ds(first, rows), every)
    return ref.at[where]


def unit_of(ref, at, axis, first, rows, core=None):
    every = slice(None)
    x_lo, x_hi = (every, every) if axis == "x" else (at["x"] % 2, at["x"] // 2)
    y = every if axis == "y" else at["y"]
    z = every if axis == "z" else at["z"]
    where = (x_lo,) + (() if core is None else (core,)) + (y, x_hi, z, pl.ds(first, rows), every)
    return ref.at[where]


def unit_shape(axis, rows):
    return ((2, 2) if axis == "x" else (4,)) + (rows, 128)


AWAY = (0, 1, 2, 1)
OFFSETS = [(j, k) for j in range(4) for k in range(4)]


def depth(offset):
    return AWAY[offset[0]] + AWAY[offset[1]]


def way_two(lane):
    return 1 if lane % 2 == 0 else 3


def way_three(j):
    return 1 if j % 2 == 0 else 3


def onward(lane, offset):
    j, k = offset
    to = []
    if k == 0:
        to += [(2, 1), (2, 3)]
        if j == 0:
            to += [(1, 1), (1, 3)]
        elif j == way_two(lane):
            to += [(1, j)]
    elif k == way_three(j):
        to += [(2, k)]
    return to


def after(offset, axis_number, by):
    j, k = offset
    return ((j + by) % 4, k) if axis_number == 1 else (j, (k + by) % 4)


def source(p, order, offset):
    return moved(moved(p, order[1], 4 - offset[0]), order[2], 4 - offset[1])


def wait_bytes(ref, sem):
    pltpu.make_async_copy(ref, ref, sem).wait()


def gather_steps(lanes, w_ref, p, sems, shares):
    line_send, line_recv, unit_send, unit_recv, sib_send, sib_recv = sems
    core = p["c"]
    sibling = moved(p, "c", 1)
    sent = []
    lines = []
    for lane, at, rows, order in lanes:
        mine = block_of(w_ref, p, at, rows, core)
        for by in (1, 3, 2):
            q = moved(p, order[0], by)
            lines.append(send(mine, mine, line_send.at[lane, by - 1], line_recv.at[lane, by - 1], q))
    yield

    def pass_on(lane, at, rows, order, offset):
        unit = unit_of(w_ref, source(p, order, offset), order[0], at, rows, core)
        for number, by in onward(lane, offset):
            j, k = after(offset, number, by)
            sem = lane, j * 4 + k
            sent.append(send(unit, unit, unit_send.at[sem], unit_recv.at[sem], moved(p, order[number], by)))
        j, k = offset
        sem = lane, j * 4 + k
        shares.append(send(unit, unit, sib_send.at[sem], sib_recv.at[sem], sibling))

    for i, (lane, at, rows, order) in enumerate(lanes):
        for copy in lines[3 * i : 3 * i + 3]:
            copy.wait_recv()
        pass_on(lane, at, rows, order, (0, 0))
    yield
    for far in (1, 2, 3, 4):
        for lane, at, rows, order in lanes:
            for offset in OFFSETS:
                if depth(offset) == far:
                    j, k = offset
                    unit = unit_of(w_ref, source(p, order, offset), order[0], at, rows, core)
                    pltpu.make_async_remote_copy(
                        src_ref=unit, dst_ref=unit,
                        send_sem=unit_send.at[lane, j * 4 + k], recv_sem=unit_recv.at[lane, j * 4 + k],
                        device_id=device_of(sibling), device_id_type=MESH,
                    ).wait_recv()
                    pass_on(lane, at, rows, order, offset)
        yield
    for copy in shares:
        copy.wait_recv()
    for copy in lines + sent + shares:
        copy.wait_send()
    yield


def add_unit(acc, p, at, axis, first, rows, terms):
    def step(i, _):
        q = dict(at)
        q[axis] = i
        target = (q["x"] % 2, p["c"], q["y"], q["x"] // 2, q["z"], pl.ds(first, rows), slice(None))
        where = (i % 2, i // 2) if axis == "x" else (i,)
        total = acc[target]
        for term in terms:
            total = total + term[where]
        acc[target] = total
        return 0

    lax.fori_loop(0, 4, step, 0)


def reduce_steps(lanes, g_ref, other, bufs, line_bufs, p, sems):
    line_send, line_recv, unit_send, unit_recv, sib_send, sib_recv = sems
    core = p["c"]
    sibling = moved(p, "c", 1)
    halves, sent = {}, {}
    for far in (4, 3, 2, 1, 0):
        for lane, at, rows, order in lanes:
            for offset in OFFSETS:
                if depth(offset) == far:
                    where = source(p, order, offset)
                    src = unit_of(g_ref, where, order[0], at, rows, sibling["c"])
                    dst = unit_of(other, where, order[0], at, rows)
                    sem = lane, offset[0] * 4 + offset[1]
                    halves[lane, offset] = send(src, dst, sib_send.at[sem], sib_recv.at[sem], sibling)
    yield

    def add(lane, at, rows, order, offset):
        halves[lane, offset].wait_recv()
        where = source(p, order, offset)
        terms = [unit_of(other, where, order[0], at, rows)]
        for number, by in onward(lane, offset):
            child = after(offset, number, by)
            sent[lane, child].wait_recv()
            terms.append(bufs[lane].at[child[0] * 4 + child[1] - 1])
        add_unit(g_ref, p, where, order[0], at, rows, terms)

    def back(lane, at, rows, order, offset):
        for parent in OFFSETS:
            for number, by in onward(lane, parent):
                if after(parent, number, by) == offset:
                    j, k = offset
                    sem = lane, j * 4 + k
                    unit = unit_of(g_ref, source(p, order, offset), order[0], at, rows, core)
                    sent[lane, offset] = send(
                        unit, bufs[lane].at[j * 4 + k - 1], unit_send.at[sem], unit_recv.at[sem],
                        moved(p, order[number], 4 - by),
                    )

    for far in (4, 3, 2, 1):
        for lane, at, rows, order in lanes:
            for offset in OFFSETS:
                if depth(offset) == far:
                    add(lane, at, rows, order, offset)
                    back(lane, at, rows, order, offset)
        yield
    lines = []
    for lane, at, rows, order in lanes:
        add(lane, at, rows, order, (0, 0))
        for by in (1, 3, 2):
            q = moved(p, order[0], by)
            src = block_of(g_ref, q, at, rows, core)
            lines.append(
                send(src, line_bufs[lane].at[by - 1], line_send.at[lane, by - 1], line_recv.at[lane, by - 1], q)
            )
    yield
    for i, (lane, at, rows, order) in enumerate(lanes):
        for copy in lines[3 * i : 3 * i + 3]:
            copy.wait_recv()
        target = (p["x"] % 2, core, p["y"], p["x"] // 2, p["z"], pl.ds(at, rows), slice(None))
        total = g_ref[target].astype(f32)
        for by in range(3):
            total = total + line_bufs[lane][by].astype(f32)
        g_ref[target] = total.astype(bf16)
    for copy in lines + list(sent.values()) + list(halves.values()):
        copy.wait_send()
    yield


def dot(a, b):
    return jnp.dot(a, b, preferred_element_type=f32)


def dot_nt(a, b):
    return lax.dot_general(a, b, (((1,), (1,)), ((), ())), preferred_element_type=f32)


def inv_rms(v):
    return lax.rsqrt(jnp.mean(v * v, axis=-1, keepdims=True) + norm_eps)


def norm_back(v, r, c, e):
    ec = e * c
    vr = v * r
    dv = r * (ec - vr * jnp.mean(vr * ec, axis=-1, keepdims=True))
    return dv, jnp.sum(e * vr, axis=0, keepdims=True)


def turn(u, cos, sin):
    a, b = u[:, :128], u[:, 128:]
    return jnp.concatenate([a * cos - b * sin, b * cos + a * sin], axis=1)


def turn_back(e, cos, sin):
    a, b = e[:, :128], e[:, 128:]
    return jnp.concatenate([a * cos + b * sin, b * cos - a * sin], axis=1)


def columns(w_ref, t, y, first):
    return jnp.concatenate(
        [w_ref[t // 2, t % 2, y + i, :, :, first : first + 80, :].reshape(D, 128) for i in range(2)], axis=1
    )


def put_columns(g_ref, t, y, first, value):
    value = value.astype(bf16)
    for i in range(2):
        g_ref[t // 2, t % 2, y + i, :, :, first : first + 80, :] = (
            value[:, 128 * i : 128 * i + 128].reshape(2, 4, 80, 128)
        )


NB = len(LANES)


def kernel(
    seg_ref, wq_ref, wkv_ref, wo_ref, wg_ref, wu_ref, wd_ref, x_ref, cot_ref,
    gin_ref, gpa_ref, gpf_ref, gpo_ref, gq_ref, gk_ref, cos_tab, sin_tab, freq_ref,
    out_ref, gx_ref, shard_ref, kv_ref, gn_out,
    *scratch,
):
    bufs, line_bufs, scratch = scratch[:NB], scratch[NB : 2 * NB], scratch[2 * NB :]
    (
        w_ref, g_ref, other, xg, rows_s, s_ref, got, stage,
        cos_ref, sin_ref, wkv, attn_in, attn_in_t, kt, vt, kb, vb, qraw, qb, probs, ctx,
        mlp_in, mlp_in_t, d_b, d_t, act_s, dact_s, hid_s, acc, acc2, dkt, dvt, proj_s,
        dx_got, gn_now, gn_got, final,
        one_send, one_recv, line_send, line_recv, unit_send, unit_recv, sib_send, sib_recv, x_send, x_recv,
        bline_send, bline_recv, back_send, back_recv, bsib_send, bsib_recv, last_send, last_recv, kv_send, kv_recv,
        dx_send, dx_recv, gn_send, gn_recv,
    ) = scratch
    p = place()
    t = lax.axis_index("tensor")
    dp = lax.axis_index("dp")
    y = p["y"]
    core = p["c"]
    own = (p["x"] % 2, core, y, p["x"] // 2, p["z"])
    greet(p)

    rows_s[...] = jnp.zeros_like(rows_s)
    out_t = wo_ref[...].astype(f32).T
    down_t = wd_ref[...].astype(f32).T
    for j in range(4):
        if j < 2:
            rows_s[j, :20, :128] = wq_ref[:, 128 * j : 128 * j + 128].astype(f32)
        else:
            rows_s[j, :20, :128] = out_t[:, 128 * j - 256 : 128 * j - 128]
        rows_s[j, :20, 128:256] = wg_ref[:, 128 * j : 128 * j + 128].astype(f32)
        rows_s[j, :20, 256:384] = wu_ref[:, 128 * j : 128 * j + 128].astype(f32)
        rows_s[j, :20, 384:512] = down_t[:, 128 * j : 128 * j + 128]
        rows_s[j, :20, 512:] = wkv_ref[:, 128 * j : 128 * j + 128].astype(f32)
    s_ref[...] = rows_s[...].astype(bf16)
    first = []
    for k in (1, 3, 2):
        q = moved(p, "y", k)
        first.append(send(s_ref.at[q["y"]], got.at[y], one_send.at[k - 1], one_recv.at[k - 1], q))

    def token_copy(src, slot, to):
        return pltpu.make_async_remote_copy(
            src_ref=src, dst_ref=xg.at[slot], send_sem=x_send.at[1 - slot], recv_sem=x_recv.at[1 - slot],
            device_id={"dp": dp, "tensor": to}, device_id_type=MESH,
        )

    @pl.when(t < 3)
    def _():
        token_copy(x_ref, 1, jnp.minimum(t + 1, 3)).start()

    @pl.when(t == 0)
    def _():
        token_copy(x_ref, 0, t + 2).start()

    xg[2] = x_ref[...]
    got[pl.ds(y, 1)] = s_ref[pl.ds(y, 1)]
    for copy in first:
        copy.wait_recv()
    for j in range(4):
        stage[20 * j : 20 * j + 20, :] = got[j].astype(f32)[:20, :512]
    for i, at in enumerate((0, G0, U0, D0)):
        w_ref[own + (slice(at, at + 80),)] = stage[:80, 128 * i : 128 * i + 128].astype(bf16)
    w_ref[own + (slice(KV0, KV0 + 32),)] = got[pl.ds(t, 1)][0, :, 512:640]
    for copy in first:
        copy.wait_send()

    sems = (line_send, line_recv, unit_send, unit_recv, sib_send, sib_recv)
    attn = gather_steps(ATTN, w_ref, p, sems, [])
    feed = gather_steps(FEED, w_ref, p, sems, [])
    next(attn)
    for _ in range(3):
        next(feed)
        next(attn)

    gin, gpa, gpf, gpo, gq, gk = (
        ref[...].reshape(1, ref.shape[0]) for ref in (gin_ref, gpa_ref, gpf_ref, gpo_ref, gq_ref, gk_ref)
    )
    scale = HD ** -0.5
    seg = seg_ref[...]
    n0 = jnp.sum(jnp.where(seg == 0, 1.0, 0.0), axis=1, keepdims=True)
    n1 = jnp.sum(jnp.where(seg <= 1, 1.0, 0.0), axis=1, keepdims=True)
    base = ((t - 2) * PART).astype(f32)
    which = lax.broadcasted_iota(jnp.int32, (8, 128), 0)
    turn_by = (jnp.where(which == 0, 0.0, jnp.where(which == 1, n0, n1)) - base) * freq_ref[...]
    cb, sb = jnp.cos(turn_by), jnp.sin(turn_by)
    token = lax.broadcasted_iota(jnp.int32, (KEYS, 1), 0).astype(f32) + base
    in0, in1 = token < n0, token < n1
    cd = jnp.where(in0, cb[0:1], jnp.where(in1, cb[1:2], cb[2:3]))
    sd = jnp.where(in0, sb[0:1], jnp.where(in1, sb[1:2], sb[2:3]))
    ca, sa = cos_tab[...], sin_tab[...]
    cos_ref[...] = ca * cd + sa * sd
    sin_ref[...] = sa * cd - ca * sd

    @pl.when(t > 0)
    def _():
        token_copy(x_ref, 1, jnp.minimum(t + 1, 3)).wait_recv()

    @pl.when(t == 2)
    def _():
        token_copy(xg.at[1], 0, jnp.minimum(t + 1, 3)).start()

    @pl.when(t >= 2)
    def _():
        token_copy(x_ref, 0, jnp.minimum(t + 1, 3)).wait_recv()

    @pl.when(t < 3)
    def _():
        token_copy(x_ref, 1, jnp.minimum(t + 1, 3)).wait_send()

    @pl.when(lax.rem(t, 2) == 0)
    def _():
        token_copy(x_ref, 0, jnp.minimum(t + 1, 3)).wait_send()

    def tokens(i):
        return jnp.where(i >= 2 - t, xg[i].astype(f32), 0.0)

    def input_norm(i, _):
        x = tokens(i)
        a = x * inv_rms(x) * gin
        attn_in[i] = a.astype(bf16)
        attn_in_t[i] = a.T.astype(bf16)
        return 0

    lax.fori_loop(0, 3, input_norm, 0)
    acc[...] = jnp.zeros_like(acc)
    next(feed)
    next(attn)
    next(feed)
    next(attn)
    next(attn)

    def keyval_in(g, _):
        for tt in range(4):
            for yy in range(4):
                stage[20 * tt : 20 * tt + 20, 128 * yy : 128 * yy + 128] = (
                    w_ref[tt // 2, tt % 2, yy, g // 4, g % 4, KV0 : KV0 + 32, :].astype(f32)[:20]
                )
        wkv[g] = stage[:80, :].astype(bf16)
        return 0

    lax.fori_loop(0, GROUPS, keyval_in, 0)

    def rows_of(i):
        return pl.ds(pl.multiple_of(i * PART, PART), PART)

    def keys_values(i, _):
        rows = rows_of(i)
        kv_raw = dot(attn_in[i], wkv[...].reshape(D, 512))
        kraw = kv_raw[:, :HD]
        k = turn(kraw * inv_rms(kraw) * gk, cos_ref[rows, :], sin_ref[rows, :])
        kb[rows, :] = k.astype(bf16)
        kt[:, rows] = k.T.astype(bf16)
        v = kv_raw[:, HD:]
        vb[rows, :] = v.astype(bf16)
        vt[:, rows] = v.T.astype(bf16)
        return 0

    lax.fori_loop(0, 3, keys_values, 0)
    next(feed)

    def head(h, _):
        cos_q, sin_q = cos_ref[2 * PART :, :], sin_ref[2 * PART :, :]
        column = lax.broadcasted_iota(jnp.int32, (PART, KEYS), 1)
        last = lax.broadcasted_iota(jnp.int32, (PART, 1), 0) + 2 * PART
        own_token = last.astype(f32) + base
        start = jnp.where(own_token < n0, 0.0, jnp.where(own_token < n1, n0, n1))
        low = jnp.maximum(own_token - (WINDOW - 1), start) - base
        raw = dot(attn_in[2], columns(w_ref, h, 0, 0))
        qraw[h] = raw
        q = turn(raw * inv_rms(raw) * gq, cos_q, sin_q).astype(bf16)
        qb[h] = q
        s = dot(q, kt[...]) * scale
        s = jnp.where((column.astype(f32) >= low) & (column <= last), s, -1e30)
        e = jnp.exp(s - jnp.max(s, axis=-1, keepdims=True))
        pr = e / jnp.sum(e, axis=-1, keepdims=True)
        probs[h] = pr
        c = dot(pr.astype(bf16), vb[...]).astype(bf16)
        ctx[h] = c
        acc[...] += dot_nt(c, columns(w_ref, h, 2, 0))
        return 0

    lax.fori_loop(0, 4, head, 0)
    proj = acc[...]
    proj_s[...] = proj
    mid = x_ref[...].astype(f32) + proj * inv_rms(proj) * gpa
    gx_ref[...] = mid
    m = mid * inv_rms(mid) * gpf
    mlp_in[...] = m.astype(bf16)
    mlp_in_t[...] = m.T.astype(bf16)
    acc[...] = jnp.zeros_like(acc)
    next(feed)

    def feed_forward(c, _):
        tt, yy = c // 2, 2 * (c % 2)
        gate = dot(mlp_in[...], columns(w_ref, tt, yy, G0))
        up = dot(mlp_in[...], columns(w_ref, tt, yy, U0))
        k0, k1 = 0.7978845608028654, 0.044715
        sq = gate * gate
        th = jnp.tanh(k0 * (gate + k1 * gate * sq))
        half = 0.5 * (1.0 + th)
        act = gate * half
        hid = (act * up).astype(bf16)
        act_s[c] = act
        dact_s[c] = up * (half + 0.5 * gate * (1.0 - th * th) * (k0 + (3.0 * k0 * k1) * sq))
        hid_s[c] = hid
        acc[...] += dot_nt(hid, columns(w_ref, tt, yy, D0))
        return 0

    lax.fori_loop(0, 8, feed_forward, 0)
    mlp = acc[...]
    r = inv_rms(mlp)
    out_ref[...] = (gx_ref[...] + mlp * r * gpo).astype(bf16)
    d_mlp, g_po = norm_back(mlp, r, gpo, cot_ref[...].astype(f32))
    gn_now[0, 3:4, :] = g_po
    d_b[...] = d_mlp.astype(bf16)
    d_t[...] = d_mlp.T.astype(bf16)
    acc[...] = jnp.zeros_like(acc)

    def feed_back(c, _):
        tt, yy = c // 2, 2 * (c % 2)
        put_columns(g_ref, tt, yy, D0, dot(d_t[...], hid_s[c]))
        d_hid = dot(d_b[...], columns(w_ref, tt, yy, D0))
        d_gate = (d_hid * dact_s[c]).astype(bf16)
        d_up = (d_hid * act_s[c]).astype(bf16)
        put_columns(g_ref, tt, yy, G0, dot(mlp_in_t[...], d_gate))
        put_columns(g_ref, tt, yy, U0, dot(mlp_in_t[...], d_up))
        acc[...] += dot_nt(d_gate, columns(w_ref, tt, yy, G0)) + dot_nt(d_up, columns(w_ref, tt, yy, U0))
        return 0

    lax.fori_loop(0, 8, feed_back, 0)
    sems = (bline_send, bline_recv, back_send, back_recv, bsib_send, bsib_recv)
    feed = reduce_steps(FEED, g_ref, other, bufs, line_bufs, p, sems)
    next(feed)

    mid = gx_ref[...]
    d_pre, g_pf = norm_back(mid, inv_rms(mid), gpf, acc[...])
    gn_now[0, 2:3, :] = g_pf
    d_mid = cot_ref[...].astype(f32) + d_pre
    proj = proj_s[...]
    d_proj, g_pa = norm_back(proj, inv_rms(proj), gpa, d_mid)
    gn_now[0, 1:2, :] = g_pa
    gx_ref[...] = d_mid
    d_b[...] = d_proj.astype(bf16)
    d_t[...] = d_proj.T.astype(bf16)
    dkt[...] = jnp.zeros_like(dkt)
    dvt[...] = jnp.zeros_like(dvt)
    acc[...] = jnp.zeros_like(acc)
    acc2[...] = jnp.zeros_like(acc2)
    next(feed)

    def head_back(h, _):
        cos_q, sin_q = cos_ref[2 * PART :, :], sin_ref[2 * PART :, :]
        put_columns(g_ref, h, 2, 0, dot(d_t[...], ctx[h]))
        d_ctx = dot(d_b[...], columns(w_ref, h, 2, 0))
        d_ctx_b = d_ctx.astype(bf16)
        pr = probs[h]
        d_pr = dot(d_ctx_b, vt[...])
        dvt[...] += dot(d_ctx.T.astype(bf16), pr.astype(bf16))
        inner = jnp.sum(pr * d_pr, axis=-1, keepdims=True)
        ds = (pr * (d_pr - inner)).astype(bf16)
        dq = dot(ds, kb[...]) * scale
        dkt[...] += dot(qb[h].astype(f32).T.astype(bf16), ds)
        raw = qraw[h]
        d_raw, g_q = norm_back(raw, inv_rms(raw), gq, turn_back(dq, cos_q, sin_q))
        acc2[...] += g_q
        d_raw = d_raw.astype(bf16)
        put_columns(g_ref, h, 0, 0, dot(attn_in_t[2], d_raw))
        acc[...] += dot_nt(d_raw, columns(w_ref, h, 0, 0))
        return 0

    lax.fori_loop(0, 2, head_back, 0)
    next(feed)
    lax.fori_loop(2, 4, head_back, 0)
    gn_now[0, 4:8, :] = jnp.zeros((4, D), f32)
    gn_now[0, 4:5, :HD] = acc2[...]
    acc2[...] = jnp.zeros_like(acc2)

    def keys_values_back(i, _):
        rows = rows_of(i)
        raw = dot(attn_in[i], wkv[:, :, :HD].reshape(D, HD))
        e = turn_back(dkt[:, rows].T * scale, cos_ref[rows, :], sin_ref[rows, :])
        dk, g_k = norm_back(raw, inv_rms(raw), gk, e)
        acc2[...] += g_k
        kb[rows, :] = dk.astype(bf16)
        vb[rows, :] = dvt[:, rows].T.astype(bf16)
        return 0

    lax.fori_loop(0, 3, keys_values_back, 0)
    gn_now[0, 5:6, :HD] = acc2[...]
    for half, src in enumerate((kb, vb)):
        grad = sum(dot(attn_in_t[i], src[PART * i : PART * i + PART, :]) for i in range(3))
        stage[80:, :] = jnp.zeros((16, 512), f32)
        for g in range(GROUPS):
            stage[:80, :HD] = grad[80 * g : 80 * g + 80]
            for tt in range(4):
                for yy in range(2):
                    g_ref[tt // 2, tt % 2, 2 * half + yy, g // 4, g % 4, KV0 : KV0 + 32, :] = (
                        stage[20 * tt : 20 * tt + 32, 128 * yy : 128 * yy + 128].astype(bf16)
                    )
    attn = reduce_steps(ATTN, g_ref, other, bufs, line_bufs, p, sems)
    next(attn)
    next(feed)

    def input_back(i, extra):
        rows = rows_of(i)
        d_in = dot_nt(kb[rows, :], wkv[:, :, :HD].reshape(D, HD)) + dot_nt(vb[rows, :], wkv[:, :, HD:].reshape(D, HD))
        x = tokens(i)
        dx, g_in = norm_back(x, inv_rms(x), gin, d_in if extra is None else d_in + extra)
        gn_now[0, 0:1, :] += g_in
        return dx

    def input_back_before(i, _):
        attn_in[i] = input_back(i, None).astype(bf16)
        return 0

    gn_now[0, 0:1, :] = jnp.zeros((1, D), f32)
    lax.fori_loop(0, 2, input_back_before, 0)
    gx_ref[...] += input_back(2, acc[...])

    def dx_copy(k):
        return pltpu.make_async_remote_copy(
            src_ref=attn_in.at[2 - k], dst_ref=dx_got.at[k - 1], send_sem=dx_send.at[k - 1], recv_sem=dx_recv.at[k - 1],
            device_id={"dp": dp, "tensor": jnp.maximum(t - k, 0)}, device_id_type=MESH,
        )

    for k in (1, 2):
        @pl.when(t - k >= 0)
        def _(k=k):
            dx_copy(k).start()

    def pair(i):
        if i == 6:
            return moved(p, "c", 1)
        axis = "xyz"[i // 2]
        m = p[axis]
        q = dict(p)
        q[axis] = (m // 2) * 2 + (1 - m % 2) if i % 2 == 0 else 3 - m
        return q

    gn_copies = []

    def gn_start(i):
        gn_copies.append(send(gn_now.at[i], gn_got.at[i], gn_send.at[i], gn_recv.at[i], pair(i)))

    def gn_add(i):
        gn_copies[i].wait_recv()
        gn_now[i + 1] = gn_now[i] + gn_got[i]

    gn_start(0)
    for i in range(6):
        next(attn)
        if i < 3:
            next(feed)
        gn_add(i)
        gn_start(i + 1)

    mine = g_ref[own].astype(f32)
    for i, at in enumerate((0, G0, U0, D0)):
        for j in range(4):
            rows_s[j, 0:20, 128 * i : 128 * i + 128] = mine[at + 20 * j : at + 20 * j + 20]
    for j in range(4):
        rows_s[j, :24, 512:] = mine[KV0 : KV0 + 24]
    last = []
    for k in (1, 3, 2):
        q = moved(p, "y", k)
        last.append(send(rows_s.at[q["y"], pl.ds(0, 24), :], final.at[y], last_send.at[k - 1], last_recv.at[k - 1], q))
    final[pl.ds(y, 1)] = rows_s[pl.ds(y, 1), :24]
    gn_add(6)
    gn_out[...] = gn_now[7]
    for k in (1, 2):
        @pl.when(t + k <= 3)
        def _(k=k):
            dx_copy(k).wait_recv()
            gx_ref[...] += dx_got[k - 1].astype(f32)

        @pl.when(t - k >= 0)
        def _(k=k):
            dx_copy(k).wait_send()

    for copy in last:
        copy.wait_recv()

    def kv_copy(k):
        return pltpu.make_async_remote_copy(
            src_ref=final.at[:, :, pl.ds(512, 128)], dst_ref=kv_ref, send_sem=kv_send.at[k - 1], recv_sem=kv_recv,
            device_id={"dp": dp, "tensor": (t + k) % 4}, device_id_type=MESH,
        )

    @pl.when(t == y)
    def _():
        for k in (1, 2, 3):
            kv_copy(k).start()
        kv_ref[...] = final[:, :, 512:640]

    shard_ref[...] = final[:, :, :512]
    for copy in gn_copies + last:
        copy.wait_send()

    @pl.when(t == y)
    def _():
        for k in (1, 2, 3):
            kv_copy(k).wait_send()

    @pl.when(t != y)
    def _():
        kv_copy(1).wait_recv()


def layer(*args):
    dma = pltpu.SemaphoreType.DMA
    vmem = pl.BlockSpec(memory_space=pltpu.VMEM)
    bufs = [pltpu.VMEM((15,) + unit_shape(order[0], rows), bf16) for _, _, rows, order in LANES]
    bufs += [pltpu.VMEM((3, rows, 128), bf16) for _, _, rows, _ in LANES]
    n = len(LANES)
    return pl.pallas_call(
        kernel,
        out_shape=(
            jax.ShapeDtypeStruct((PART, D), bf16),
            jax.ShapeDtypeStruct((PART, D), f32),
            jax.ShapeDtypeStruct((4, 24, 512), f32),
            jax.ShapeDtypeStruct((4, 24, 128), f32),
            jax.ShapeDtypeStruct((8, D), f32),
        ),
        in_specs=[vmem] * len(args),
        out_specs=(vmem,) * 5,
        scratch_shapes=[
            *bufs,
            pltpu.VMEM((2, 2, 4, 2, 4, BLOCK, 128), bf16),
            pltpu.VMEM((2, 2, 4, 2, 4, BLOCK, 128), bf16),
            pltpu.VMEM((2, 4, 2, 4, BLOCK, 128), bf16),
            pltpu.VMEM((3, PART, D), bf16),
            pltpu.VMEM((4, 32, D), f32),
            pltpu.VMEM((4, 32, D), bf16),
            pltpu.VMEM((4, 32, D), bf16),
            pltpu.VMEM((96, 512), f32),
            pltpu.VMEM((KEYS, 128), f32),
            pltpu.VMEM((KEYS, 128), f32),
            pltpu.VMEM((GROUPS, 80, 512), bf16),
            pltpu.VMEM((3, PART, D), bf16),
            pltpu.VMEM((3, D, PART), bf16),
            pltpu.VMEM((HD, KEYS), bf16),
            pltpu.VMEM((HD, KEYS), bf16),
            pltpu.VMEM((KEYS, HD), bf16),
            pltpu.VMEM((KEYS, HD), bf16),
            pltpu.VMEM((4, PART, HD), f32),
            pltpu.VMEM((4, PART, HD), bf16),
            pltpu.VMEM((4, PART, KEYS), f32),
            pltpu.VMEM((4, PART, HD), bf16),
            pltpu.VMEM((PART, D), bf16),
            pltpu.VMEM((D, PART), bf16),
            pltpu.VMEM((PART, D), bf16),
            pltpu.VMEM((D, PART), bf16),
            pltpu.VMEM((8, PART, 256), f32),
            pltpu.VMEM((8, PART, 256), f32),
            pltpu.VMEM((8, PART, 256), bf16),
            pltpu.VMEM((PART, D), f32),
            pltpu.VMEM((1, HD), f32),
            pltpu.VMEM((HD, KEYS), f32),
            pltpu.VMEM((HD, KEYS), f32),
            pltpu.VMEM((PART, D), f32),
            pltpu.VMEM((2, PART, D), bf16),
            pltpu.VMEM((8, 8, D), f32),
            pltpu.VMEM((7, 8, D), f32),
            pltpu.VMEM((4, 24, D), f32),
            dma((3,)), dma((3,)), dma((n, 3)), dma((n, 3)), dma((n, 16)), dma((n, 16)), dma((n, 16)), dma((n, 16)),
            dma((2,)), dma((2,)),
            dma((n, 3)), dma((n, 3)), dma((n, 16)), dma((n, 16)), dma((n, 16)), dma((n, 16)),
            dma((3,)), dma((3,)), dma((3,)), dma,
            dma((2,)), dma((2,)), dma((7,)), dma((7,)),
        ],
        compiler_params=pltpu.CompilerParams(
            collective_id=0, has_side_effects=True, vmem_limit_bytes=62 << 20
        ),
        name="layer",
    )(*args)


def rope_parts():
    freq = (rope_base ** (-np.arange(0, HD, 2, dtype=np.float64) / HD))[None, :]
    angles = np.arange(KEYS, dtype=np.float64)[:, None] * freq
    return tuple(jnp.asarray(item.astype(np.float32)) for item in (np.cos(angles), np.sin(angles), freq))


def per_device(
    tokens, segments, cotangent, w_query, w_keyval, w_out, w_gate, w_up, w_down,
    gain_in, gain_post_attn, gain_pre_ff, gain_post_ff, gain_query, gain_key,
):
    output, grad_x, shard, kv, gn = layer(
        segments, w_query, w_keyval, w_out, w_gate, w_up, w_down, tokens, cotangent,
        gain_in, gain_post_attn, gain_pre_ff, gain_post_ff, gain_query, gain_key, *rope_parts(),
    )
    rows = shard[:, :20].reshape(4, 20, 4, 128)
    first, gate, up, down = (jnp.moveaxis(rows[:, :, i], 0, 1).reshape(20, 512) for i in range(4))
    grad_kv = jnp.moveaxis(kv[:, :20], 0, 1).reshape(20, 512)
    return (
        output, grad_x, first[:, :256], grad_kv, first[:, 256:].T, gate, up, down.T,
        gn[0], gn[1], gn[2], gn[3], gn[4, :HD], gn[5, :HD],
    )


def solution(mesh):
    tok = P(("dp", "tensor"), None)
    weights = (
        P("dp", "tensor"), P("dp", None), P("tensor", "dp"), P("dp", "tensor"), P("dp", "tensor"), P("tensor", "dp"),
    )
    return jax.shard_map(
        per_device,
        mesh=mesh,
        in_specs=(tok, P("dp", None), tok) + weights + (P(),) * 6,
        out_specs=(tok, tok) + weights + (P(),) * 6,
        check_vma=False,
    )
```

```python
import jax
import jax.numpy as jnp
import numpy as np
from jax import lax
from jax.experimental import pallas as pl
from jax.experimental.pallas import tpu as pltpu
from jax.sharding import PartitionSpec as P

HD = 256
WINDOW = 512
D = 640
PART = 256
KEYS = 768
BLOCK = 352
CB = 16
GROUPS = 8
KV0, G0, U0, D0 = 80, 112, 192, 272
ATTN = ((0, 0, 48, "xyz"), (1, 48, 32, "yzx"), (2, 80, 32, "zxy"))
FEED = ((3, 112, 80, "xyz"), (4, 192, 64, "yzx"), (5, 256, 96, "zxy"))
LANES = ATTN + FEED
norm_eps = 1e-06
rope_base = 10000.0
MESH = pl.DeviceIdType.MESH
f32 = jnp.float32
bf16 = jnp.bfloat16


def place():
    dp = lax.axis_index("dp")
    t = lax.axis_index("tensor")
    return {
        "x": (dp // 16) * 2 + t // 2,
        "y": dp % 4,
        "z": (dp // 4) % 4,
        "c": t % 2,
    }


def device_of(p):
    return {
        "dp": (p["x"] // 2) * 16 + p["z"] * 4 + p["y"],
        "tensor": (p["x"] % 2) * 2 + p["c"],
    }


def moved(p, axis, by):
    size = 2 if axis == "c" else 4
    q = dict(p)
    q[axis] = (p[axis] + by) % size
    return q


def diagonal(p):
    q = moved(p, "c", 1)
    q["x"] = (p["x"] // 2) * 2 + (1 - p["x"] % 2)
    return q


def peers_of(p):
    found = [
        moved(p, axis, by)
        for axis, by in (
            ("x", 1), ("x", 2), ("x", 3), ("y", 1), ("y", 2), ("y", 3), ("z", 1), ("z", 2), ("z", 3), ("c", 1)
        )
    ]
    return found + [diagonal(p)]


def greet(p):
    barrier = pltpu.get_barrier_semaphore()
    peers = peers_of(p)
    for q in peers:
        pl.semaphore_signal(barrier, inc=1, device_id=device_of(q), device_id_type=MESH)
    pl.semaphore_wait(barrier, len(peers))


def send(src, dst, send_sem, recv_sem, q):
    copy = pltpu.make_async_remote_copy(
        src_ref=src,
        dst_ref=dst,
        send_sem=send_sem,
        recv_sem=recv_sem,
        device_id=device_of(q),
        device_id_type=MESH,
    )
    copy.start()
    return copy


def block_of(ref, at, first, rows, core=None):
    every = slice(None)
    where = (at["x"] % 2,) + (() if core is None else (core,)) + (at["y"], at["x"] // 2, at["z"], pl.ds(first, rows), every)
    return ref.at[where]


def unit_of(ref, at, axis, first, rows, core=None):
    every = slice(None)
    x_lo, x_hi = (every, every) if axis == "x" else (at["x"] % 2, at["x"] // 2)
    y = every if axis == "y" else at["y"]
    z = every if axis == "z" else at["z"]
    where = (x_lo,) + (() if core is None else (core,)) + (y, x_hi, z, pl.ds(first, rows), every)
    return ref.at[where]


def unit_shape(axis, rows):
    return ((2, 2) if axis == "x" else (4,)) + (rows, 128)


AWAY = (0, 1, 2, 1)
OFFSETS = [(j, k) for j in range(4) for k in range(4)]


def depth(offset):
    return AWAY[offset[0]] + AWAY[offset[1]]


def way_two(lane):
    return 1 if lane % 2 == 0 else 3


def way_three(lane, j):
    return 1 if j % 2 == 0 and lane % 3 != 1 else 3


def onward(lane, offset):
    j, k = offset
    to = []
    if k == 0:
        to += [(2, 1), (2, 3)]
        if j == 0:
            to += [(1, 1), (1, 3)]
        elif j == way_two(lane):
            to += [(1, j)]
    elif k == way_three(lane, j):
        to += [(2, k)]
    return to


def after(offset, axis_number, by):
    j, k = offset
    return ((j + by) % 4, k) if axis_number == 1 else (j, (k + by) % 4)


def source(p, order, offset):
    return moved(moved(p, order[1], 4 - offset[0]), order[2], 4 - offset[1])


def wait_bytes(ref, sem):
    pltpu.make_async_copy(ref, ref, sem).wait()


def gather_steps(lanes, w_ref, p, sems, shares):
    line_send, line_recv, unit_send, unit_recv, sib_send, sib_recv = sems
    core = p["c"]
    sibling = moved(p, "c", 1)
    sent = []
    lines = []
    for lane, at, rows, order in lanes:
        mine = block_of(w_ref, p, at, rows, core)
        for by in (1, 3, 2):
            q = moved(p, order[0], by)
            lines.append(send(mine, mine, line_send.at[lane, by - 1], line_recv.at[lane, by - 1], q))
    yield

    def pass_on(lane, at, rows, order, offset):
        unit = unit_of(w_ref, source(p, order, offset), order[0], at, rows, core)
        for number, by in onward(lane, offset):
            j, k = after(offset, number, by)
            sem = lane, j * 4 + k
            sent.append(send(unit, unit, unit_send.at[sem], unit_recv.at[sem], moved(p, order[number], by)))
        j, k = offset
        sem = lane, j * 4 + k
        shares.append(send(unit, unit, sib_send.at[sem], sib_recv.at[sem], sibling))

    for i, (lane, at, rows, order) in enumerate(lanes):
        for copy in lines[3 * i : 3 * i + 3]:
            copy.wait_recv()
        pass_on(lane, at, rows, order, (0, 0))
    yield
    for far in (1, 2, 3, 4):
        for lane, at, rows, order in lanes:
            for offset in OFFSETS:
                if depth(offset) == far:
                    j, k = offset
                    unit = unit_of(w_ref, source(p, order, offset), order[0], at, rows, core)
                    pltpu.make_async_remote_copy(
                        src_ref=unit, dst_ref=unit,
                        send_sem=unit_send.at[lane, j * 4 + k], recv_sem=unit_recv.at[lane, j * 4 + k],
                        device_id=device_of(sibling), device_id_type=MESH,
                    ).wait_recv()
                    pass_on(lane, at, rows, order, offset)
        yield
    for copy in shares:
        copy.wait_recv()
    for copy in lines + sent + shares:
        copy.wait_send()
    yield


def add_unit(acc, p, at, axis, first, rows, terms):
    def step(i, _):
        q = dict(at)
        q[axis] = i
        target = (q["x"] % 2, p["c"], q["y"], q["x"] // 2, q["z"], pl.ds(first, rows), slice(None))
        where = (i % 2, i // 2) if axis == "x" else (i,)
        total = acc[target]
        for term in terms:
            total = total + term[where]
        acc[target] = total
        return 0

    lax.fori_loop(0, 4, step, 0)


def reduce_steps(lanes, g_ref, other, bufs, line_bufs, p, sems):
    line_send, line_recv, unit_send, unit_recv, sib_send, sib_recv = sems
    core = p["c"]
    sibling = moved(p, "c", 1)
    halves, sent = {}, {}
    for far in (4, 3, 2, 1, 0):
        for lane, at, rows, order in lanes:
            for offset in OFFSETS:
                if depth(offset) == far:
                    where = source(p, order, offset)
                    src = unit_of(g_ref, where, order[0], at, rows, sibling["c"])
                    dst = unit_of(other, where, order[0], at, rows)
                    sem = lane, offset[0] * 4 + offset[1]
                    halves[lane, offset] = send(src, dst, sib_send.at[sem], sib_recv.at[sem], sibling)
    yield

    def add(lane, at, rows, order, offset):
        halves[lane, offset].wait_recv()
        where = source(p, order, offset)
        terms = [unit_of(other, where, order[0], at, rows)]
        for number, by in onward(lane, offset):
            child = after(offset, number, by)
            sent[lane, child].wait_recv()
            terms.append(bufs[lane].at[child[0] * 4 + child[1] - 1])
        add_unit(g_ref, p, where, order[0], at, rows, terms)

    def back(lane, at, rows, order, offset):
        for parent in OFFSETS:
            for number, by in onward(lane, parent):
                if after(parent, number, by) == offset:
                    j, k = offset
                    sem = lane, j * 4 + k
                    unit = unit_of(g_ref, source(p, order, offset), order[0], at, rows, core)
                    sent[lane, offset] = send(
                        unit, bufs[lane].at[j * 4 + k - 1], unit_send.at[sem], unit_recv.at[sem],
                        moved(p, order[number], 4 - by),
                    )

    for far in (4, 3, 2, 1):
        for lane, at, rows, order in lanes:
            for offset in OFFSETS:
                if depth(offset) == far:
                    add(lane, at, rows, order, offset)
                    back(lane, at, rows, order, offset)
        yield
    lines = []
    for lane, at, rows, order in lanes:
        add(lane, at, rows, order, (0, 0))
        for by in (1, 3, 2):
            q = moved(p, order[0], by)
            src = block_of(g_ref, q, at, rows, core)
            lines.append(
                send(src, line_bufs[lane].at[by - 1], line_send.at[lane, by - 1], line_recv.at[lane, by - 1], q)
            )
    yield
    for i, (lane, at, rows, order) in enumerate(lanes):
        for copy in lines[3 * i : 3 * i + 3]:
            copy.wait_recv()
        target = (p["x"] % 2, core, p["y"], p["x"] // 2, p["z"], pl.ds(at, rows), slice(None))
        total = g_ref[target].astype(f32)
        for by in range(3):
            total = total + line_bufs[lane][by].astype(f32)
        g_ref[target] = total.astype(bf16)
    for copy in lines + list(sent.values()) + list(halves.values()):
        copy.wait_send()
    yield


def dot(a, b):
    return jnp.dot(a, b, preferred_element_type=f32)


def dot_nt(a, b):
    return lax.dot_general(a, b, (((1,), (1,)), ((), ())), preferred_element_type=f32)


def inv_rms(v):
    return lax.rsqrt(jnp.mean(v * v, axis=-1, keepdims=True) + norm_eps)


def norm_back(v, r, c, e):
    ec = e * c
    vr = v * r
    dv = r * (ec - vr * jnp.mean(vr * ec, axis=-1, keepdims=True))
    return dv, jnp.sum(e * vr, axis=0, keepdims=True)


def turn(u, cos, sin):
    a, b = u[:, :128], u[:, 128:]
    return jnp.concatenate([a * cos - b * sin, b * cos + a * sin], axis=1)


def turn_back(e, cos, sin):
    a, b = e[:, :128], e[:, 128:]
    return jnp.concatenate([a * cos + b * sin, b * cos - a * sin], axis=1)


def columns(w_ref, t, y, first):
    return jnp.concatenate(
        [w_ref[t // 2, t % 2, y + i, :, :, first : first + 80, :].reshape(D, 128) for i in range(2)], axis=1
    )


def put_columns(g_ref, t, y, first, value):
    value = value.astype(bf16)
    for i in range(2):
        g_ref[t // 2, t % 2, y + i, :, :, first : first + 80, :] = (
            value[:, 128 * i : 128 * i + 128].reshape(2, 4, 80, 128)
        )


NB = len(LANES)


def kernel(
    seg_ref, wq_ref, wkv_ref, wo_ref, wg_ref, wu_ref, wd_ref, x_ref, cot_ref,
    gin_ref, gpa_ref, gpf_ref, gpo_ref, gq_ref, gk_ref, cos_tab, sin_tab, freq_ref,
    out_ref, gx_ref, shard_ref, kv_ref, gn_out,
    *scratch,
):
    bufs, line_bufs, scratch = scratch[:NB], scratch[NB : 2 * NB], scratch[2 * NB :]
    (
        w_ref, g_ref, other, xg, rows_s, s_ref, got, stage,
        cos_ref, sin_ref, wkv, attn_in, attn_in_t, kt, vt, kb, vb, qraw, qb, probs, ctx,
        mlp_in, mlp_in_t, d_b, d_t, act_s, dact_s, hid_s, acc, acc2, dkt, dvt, proj_s,
        dx_got, gn_now, gn_got, final,
        one_send, one_recv, line_send, line_recv, unit_send, unit_recv, sib_send, sib_recv, x_send, x_recv,
        bline_send, bline_recv, back_send, back_recv, bsib_send, bsib_recv, last_send, last_recv, kv_send, kv_recv,
        dx_send, dx_recv, gn_send, gn_recv,
    ) = scratch
    p = place()
    t = lax.axis_index("tensor")
    dp = lax.axis_index("dp")
    y = p["y"]
    core = p["c"]
    own = (p["x"] % 2, core, y, p["x"] // 2, p["z"])
    greet(p)

    rows_s[...] = jnp.zeros_like(rows_s)
    for j in range(4):
        if j < 2:
            rows_s[j, :20, :128] = wq_ref[:, 128 * j : 128 * j + 128].astype(f32)
        else:
            rows_s[j, :20, :128] = wo_ref[:, 128 * j - 256 : 128 * j - 128].astype(f32)
        rows_s[j, :20, 128:256] = wg_ref[:, 128 * j : 128 * j + 128].astype(f32)
        rows_s[j, :20, 256:384] = wu_ref[:, 128 * j : 128 * j + 128].astype(f32)
        rows_s[j, :20, 384:512] = wd_ref[:, 128 * j : 128 * j + 128].astype(f32)
        rows_s[j, :20, 512:] = wkv_ref[:, 128 * j : 128 * j + 128].astype(f32)
    s_ref[...] = rows_s[...].astype(bf16)
    first = []
    for k in (1, 3, 2):
        q = moved(p, "y", k)
        first.append(send(s_ref.at[q["y"]], got.at[y], one_send.at[k - 1], one_recv.at[k - 1], q))

    def token_copy(src, slot, to):
        return pltpu.make_async_remote_copy(
            src_ref=src, dst_ref=xg.at[slot], send_sem=x_send.at[1 - slot], recv_sem=x_recv.at[1 - slot],
            device_id={"dp": dp, "tensor": to}, device_id_type=MESH,
        )

    @pl.when(t < 3)
    def _():
        token_copy(x_ref, 1, jnp.minimum(t + 1, 3)).start()

    @pl.when(t == 0)
    def _():
        token_copy(x_ref, 0, t + 2).start()

    xg[2] = x_ref[...]
    got[pl.ds(y, 1)] = s_ref[pl.ds(y, 1)]
    for copy in first:
        copy.wait_recv()
    for j in range(4):
        stage[20 * j : 20 * j + 20, :] = got[j].astype(f32)[:20, :512]
    for i, at in enumerate((0, G0, U0, D0)):
        w_ref[own + (slice(at, at + 80),)] = stage[:80, 128 * i : 128 * i + 128].astype(bf16)
    w_ref[own + (slice(KV0, KV0 + 32),)] = got[pl.ds(t, 1)][0, :, 512:640]
    for copy in first:
        copy.wait_send()

    sems = (line_send, line_recv, unit_send, unit_recv, sib_send, sib_recv)
    attn = gather_steps(ATTN, w_ref, p, sems, [])
    feed = gather_steps(FEED, w_ref, p, sems, [])
    next(attn)
    for _ in range(3):
        next(feed)
        next(attn)

    gin, gpa, gpf, gpo, gq, gk = (
        ref[...].reshape(1, ref.shape[0]) for ref in (gin_ref, gpa_ref, gpf_ref, gpo_ref, gq_ref, gk_ref)
    )
    scale = HD ** -0.5
    seg = seg_ref[...]
    n0 = jnp.sum(jnp.where(seg == 0, 1.0, 0.0), axis=1, keepdims=True)
    n1 = jnp.sum(jnp.where(seg <= 1, 1.0, 0.0), axis=1, keepdims=True)
    base = ((t - 2) * PART).astype(f32)
    which = lax.broadcasted_iota(jnp.int32, (8, 128), 0)
    turn_by = (jnp.where(which == 0, 0.0, jnp.where(which == 1, n0, n1)) - base) * freq_ref[...]
    cb, sb = jnp.cos(turn_by), jnp.sin(turn_by)
    token = lax.broadcasted_iota(jnp.int32, (KEYS, 1), 0).astype(f32) + base
    in0, in1 = token < n0, token < n1
    cd = jnp.where(in0, cb[0:1], jnp.where(in1, cb[1:2], cb[2:3]))
    sd = jnp.where(in0, sb[0:1], jnp.where(in1, sb[1:2], sb[2:3]))
    ca, sa = cos_tab[...], sin_tab[...]
    cos_ref[...] = ca * cd + sa * sd
    sin_ref[...] = sa * cd - ca * sd

    @pl.when(t > 0)
    def _():
        token_copy(x_ref, 1, jnp.minimum(t + 1, 3)).wait_recv()

    @pl.when(t == 2)
    def _():
        token_copy(xg.at[1], 0, jnp.minimum(t + 1, 3)).start()

    @pl.when(t >= 2)
    def _():
        token_copy(x_ref, 0, jnp.minimum(t + 1, 3)).wait_recv()

    @pl.when(t < 3)
    def _():
        token_copy(x_ref, 1, jnp.minimum(t + 1, 3)).wait_send()

    @pl.when(lax.rem(t, 2) == 0)
    def _():
        token_copy(x_ref, 0, jnp.minimum(t + 1, 3)).wait_send()

    def tokens(i):
        return jnp.where(i >= 2 - t, xg[i].astype(f32), 0.0)

    def input_norm(i, _):
        x = tokens(i)
        a = x * inv_rms(x) * gin
        attn_in[i] = a.astype(bf16)
        attn_in_t[i] = a.T.astype(bf16)
        return 0

    lax.fori_loop(0, 3, input_norm, 0)
    acc[...] = jnp.zeros_like(acc)
    next(feed)
    next(attn)
    next(feed)
    next(attn)
    next(attn)

    def keyval_in(g, _):
        for tt in range(4):
            for yy in range(4):
                stage[20 * tt : 20 * tt + 20, 128 * yy : 128 * yy + 128] = (
                    w_ref[tt // 2, tt % 2, yy, g // 4, g % 4, KV0 : KV0 + 32, :].astype(f32)[:20]
                )
        wkv[g] = stage[:80, :].astype(bf16)
        return 0

    lax.fori_loop(0, GROUPS, keyval_in, 0)

    def rows_of(i):
        return pl.ds(pl.multiple_of(i * PART, PART), PART)

    def keys_values(i, _):
        rows = rows_of(i)
        kv_raw = dot(attn_in[i], wkv[...].reshape(D, 512))
        kraw = kv_raw[:, :HD]
        k = turn(kraw * inv_rms(kraw) * gk, cos_ref[rows, :], sin_ref[rows, :])
        kb[rows, :] = k.astype(bf16)
        kt[:, rows] = k.T.astype(bf16)
        v = kv_raw[:, HD:]
        vb[rows, :] = v.astype(bf16)
        vt[:, rows] = v.T.astype(bf16)
        return 0

    lax.fori_loop(0, 3, keys_values, 0)
    next(feed)

    def head(h, _):
        cos_q, sin_q = cos_ref[2 * PART :, :], sin_ref[2 * PART :, :]
        column = lax.broadcasted_iota(jnp.int32, (PART, KEYS), 1)
        last = lax.broadcasted_iota(jnp.int32, (PART, 1), 0) + 2 * PART
        own_token = last.astype(f32) + base
        start = jnp.where(own_token < n0, 0.0, jnp.where(own_token < n1, n0, n1))
        low = jnp.maximum(own_token - (WINDOW - 1), start) - base
        raw = dot(attn_in[2], columns(w_ref, h, 0, 0))
        qraw[h] = raw
        q = turn(raw * inv_rms(raw) * gq, cos_q, sin_q).astype(bf16)
        qb[h] = q
        s = dot(q, kt[...]) * scale
        s = jnp.where((column.astype(f32) >= low) & (column <= last), s, -1e30)
        e = jnp.exp(s - jnp.max(s, axis=-1, keepdims=True))
        pr = e / jnp.sum(e, axis=-1, keepdims=True)
        probs[h] = pr
        c = dot(pr.astype(bf16), vb[...]).astype(bf16)
        ctx[h] = c
        acc[...] += dot_nt(c, columns(w_ref, h, 2, 0))
        return 0

    lax.fori_loop(0, 4, head, 0)
    proj = acc[...]
    proj_s[...] = proj
    mid = x_ref[...].astype(f32) + proj * inv_rms(proj) * gpa
    gx_ref[...] = mid
    m = mid * inv_rms(mid) * gpf
    mlp_in[...] = m.astype(bf16)
    mlp_in_t[...] = m.T.astype(bf16)
    acc[...] = jnp.zeros_like(acc)
    next(feed)

    def feed_forward(c, _):
        tt, yy = c // 2, 2 * (c % 2)
        gate = dot(mlp_in[...], columns(w_ref, tt, yy, G0))
        up = dot(mlp_in[...], columns(w_ref, tt, yy, U0))
        k0, k1 = 0.7978845608028654, 0.044715
        sq = gate * gate
        th = jnp.tanh(k0 * (gate + k1 * gate * sq))
        half = 0.5 * (1.0 + th)
        act = gate * half
        hid = (act * up).astype(bf16)
        act_s[c] = act
        dact_s[c] = up * (half + 0.5 * gate * (1.0 - th * th) * (k0 + (3.0 * k0 * k1) * sq))
        hid_s[c] = hid
        acc[...] += dot_nt(hid, columns(w_ref, tt, yy, D0))
        return 0

    lax.fori_loop(0, 8, feed_forward, 0)
    mlp = acc[...]
    r = inv_rms(mlp)
    out_ref[...] = (gx_ref[...] + mlp * r * gpo).astype(bf16)
    d_mlp, g_po = norm_back(mlp, r, gpo, cot_ref[...].astype(f32))
    gn_now[0, 3:4, :] = g_po
    d_b[...] = d_mlp.astype(bf16)
    d_t[...] = d_mlp.T.astype(bf16)
    acc[...] = jnp.zeros_like(acc)

    def feed_back(c, _):
        tt, yy = c // 2, 2 * (c % 2)
        put_columns(g_ref, tt, yy, D0, dot(d_t[...], hid_s[c]))
        d_hid = dot(d_b[...], columns(w_ref, tt, yy, D0))
        d_gate = (d_hid * dact_s[c]).astype(bf16)
        d_up = (d_hid * act_s[c]).astype(bf16)
        put_columns(g_ref, tt, yy, G0, dot(mlp_in_t[...], d_gate))
        put_columns(g_ref, tt, yy, U0, dot(mlp_in_t[...], d_up))
        acc[...] += dot_nt(d_gate, columns(w_ref, tt, yy, G0)) + dot_nt(d_up, columns(w_ref, tt, yy, U0))
        return 0

    lax.fori_loop(0, 8, feed_back, 0)
    sems = (bline_send, bline_recv, back_send, back_recv, bsib_send, bsib_recv)
    feed = reduce_steps(FEED, g_ref, other, bufs, line_bufs, p, sems)
    next(feed)

    mid = gx_ref[...]
    d_pre, g_pf = norm_back(mid, inv_rms(mid), gpf, acc[...])
    gn_now[0, 2:3, :] = g_pf
    d_mid = cot_ref[...].astype(f32) + d_pre
    proj = proj_s[...]
    d_proj, g_pa = norm_back(proj, inv_rms(proj), gpa, d_mid)
    gn_now[0, 1:2, :] = g_pa
    gx_ref[...] = d_mid
    d_b[...] = d_proj.astype(bf16)
    d_t[...] = d_proj.T.astype(bf16)
    dkt[...] = jnp.zeros_like(dkt)
    dvt[...] = jnp.zeros_like(dvt)
    acc[...] = jnp.zeros_like(acc)
    acc2[...] = jnp.zeros_like(acc2)
    next(feed)

    def head_back(h, _):
        cos_q, sin_q = cos_ref[2 * PART :, :], sin_ref[2 * PART :, :]
        put_columns(g_ref, h, 2, 0, dot(d_t[...], ctx[h]))
        d_ctx = dot(d_b[...], columns(w_ref, h, 2, 0))
        d_ctx_b = d_ctx.astype(bf16)
        pr = probs[h]
        d_pr = dot(d_ctx_b, vt[...])
        dvt[...] += dot(d_ctx.T.astype(bf16), pr.astype(bf16))
        inner = jnp.sum(pr * d_pr, axis=-1, keepdims=True)
        ds = (pr * (d_pr - inner)).astype(bf16)
        dq = dot(ds, kb[...]) * scale
        dkt[...] += dot(qb[h].astype(f32).T.astype(bf16), ds)
        raw = qraw[h]
        d_raw, g_q = norm_back(raw, inv_rms(raw), gq, turn_back(dq, cos_q, sin_q))
        acc2[...] += g_q
        d_raw = d_raw.astype(bf16)
        put_columns(g_ref, h, 0, 0, dot(attn_in_t[2], d_raw))
        acc[...] += dot_nt(d_raw, columns(w_ref, h, 0, 0))
        return 0

    lax.fori_loop(0, 2, head_back, 0)
    next(feed)
    lax.fori_loop(2, 4, head_back, 0)
    gn_now[0, 4:8, :] = jnp.zeros((4, D), f32)
    gn_now[0, 4:5, :HD] = acc2[...]
    acc2[...] = jnp.zeros_like(acc2)

    def keys_values_back(i, _):
        rows = rows_of(i)
        raw = dot(attn_in[i], wkv[:, :, :HD].reshape(D, HD))
        e = turn_back(dkt[:, rows].T * scale, cos_ref[rows, :], sin_ref[rows, :])
        dk, g_k = norm_back(raw, inv_rms(raw), gk, e)
        acc2[...] += g_k
        kb[rows, :] = dk.astype(bf16)
        vb[rows, :] = dvt[:, rows].T.astype(bf16)
        return 0

    lax.fori_loop(0, 3, keys_values_back, 0)
    gn_now[0, 5:6, :HD] = acc2[...]
    for half, src in enumerate((kb, vb)):
        grad = sum(dot(attn_in_t[i], src[PART * i : PART * i + PART, :]) for i in range(3))
        stage[80:, :] = jnp.zeros((16, 512), f32)
        for g in range(GROUPS):
            stage[:80, :HD] = grad[80 * g : 80 * g + 80]
            for tt in range(4):
                for yy in range(2):
                    g_ref[tt // 2, tt % 2, 2 * half + yy, g // 4, g % 4, KV0 : KV0 + 32, :] = (
                        stage[20 * tt : 20 * tt + 32, 128 * yy : 128 * yy + 128].astype(bf16)
                    )
    attn = reduce_steps(ATTN, g_ref, other, bufs, line_bufs, p, sems)
    next(attn)
    next(feed)

    def input_back(i, extra):
        rows = rows_of(i)
        d_in = dot_nt(kb[rows, :], wkv[:, :, :HD].reshape(D, HD)) + dot_nt(vb[rows, :], wkv[:, :, HD:].reshape(D, HD))
        x = tokens(i)
        dx, g_in = norm_back(x, inv_rms(x), gin, d_in if extra is None else d_in + extra)
        gn_now[0, 0:1, :] += g_in
        return dx

    def input_back_before(i, _):
        attn_in[i] = input_back(i, None).astype(bf16)
        return 0

    gn_now[0, 0:1, :] = jnp.zeros((1, D), f32)
    lax.fori_loop(0, 2, input_back_before, 0)
    gx_ref[...] += input_back(2, acc[...])

    def dx_copy(k):
        to = jnp.maximum(t - 1, 0) if k == 1 else jnp.where(t == 3, 2, 0)
        return pltpu.make_async_remote_copy(
            src_ref=attn_in.at[2 - k], dst_ref=dx_got.at[k - 1], send_sem=dx_send.at[k - 1], recv_sem=dx_recv.at[k - 1],
            device_id={"dp": dp, "tensor": to}, device_id_type=MESH,
        )

    @pl.when(t >= 2)
    def _():
        dx_copy(2).start()

    @pl.when(lax.rem(t, 2) == 1)
    def _():
        dx_copy(1).start()

    def pair(i):
        if i == 6:
            return moved(p, "c", 1)
        axis = "xyz"[i // 2]
        m = p[axis]
        q = dict(p)
        q[axis] = (m // 2) * 2 + (1 - m % 2) if i % 2 == 0 else 3 - m
        return q

    gn_copies = []

    def gn_start(i):
        gn_copies.append(send(gn_now.at[i], gn_got.at[i], gn_send.at[i], gn_recv.at[i], pair(i)))

    def gn_add(i):
        gn_copies[i].wait_recv()
        gn_now[i + 1] = gn_now[i] + gn_got[i]

    gn_start(0)
    for i in range(6):
        next(attn)
        if i == 0:
            @pl.when(t == 2)
            def _():
                dx_copy(2).wait_recv()
                attn_in[1] = (attn_in[1].astype(f32) + dx_got[1].astype(f32)).astype(bf16)
                dx_copy(1).start()

        if i < 3:
            next(feed)
        gn_add(i)
        gn_start(i + 1)

    mine = g_ref[own].astype(f32)
    for i, at in enumerate((0, G0, U0, D0)):
        for j in range(4):
            rows_s[j, 0:20, 128 * i : 128 * i + 128] = mine[at + 20 * j : at + 20 * j + 20]
    for j in range(4):
        rows_s[j, :24, 512:] = mine[KV0 : KV0 + 24]
    last = []
    for k in (1, 3, 2):
        q = moved(p, "y", k)
        last.append(send(rows_s.at[q["y"], pl.ds(0, 24), :], final.at[y], last_send.at[k - 1], last_recv.at[k - 1], q))
    final[pl.ds(y, 1)] = rows_s[pl.ds(y, 1), :24]
    gn_add(6)
    gn_out[...] = gn_now[7]

    @pl.when(t < 3)
    def _():
        dx_copy(1).wait_recv()
        gx_ref[...] += dx_got[0].astype(f32)

    @pl.when(t == 0)
    def _():
        dx_copy(2).wait_recv()
        gx_ref[...] += dx_got[1].astype(f32)

    @pl.when(t >= 1)
    def _():
        dx_copy(1).wait_send()

    @pl.when(t >= 2)
    def _():
        dx_copy(2).wait_send()

    for copy in last:
        copy.wait_recv()

    def kv_copy(k):
        return pltpu.make_async_remote_copy(
            src_ref=final.at[:, :, pl.ds(512, 128)], dst_ref=kv_ref, send_sem=kv_send.at[k - 1], recv_sem=kv_recv,
            device_id={"dp": dp, "tensor": (t + k) % 4}, device_id_type=MESH,
        )

    @pl.when(t == y)
    def _():
        for k in (1, 2, 3):
            kv_copy(k).start()
        kv_ref[...] = final[:, :, 512:640]

    shard_ref[...] = final[:, :, :512]
    for copy in gn_copies + last:
        copy.wait_send()

    @pl.when(t == y)
    def _():
        for k in (1, 2, 3):
            kv_copy(k).wait_send()

    @pl.when(t != y)
    def _():
        kv_copy(1).wait_recv()


def layer(*args):
    dma = pltpu.SemaphoreType.DMA
    vmem = pl.BlockSpec(memory_space=pltpu.VMEM)
    bufs = [pltpu.VMEM((15,) + unit_shape(order[0], rows), bf16) for _, _, rows, order in LANES]
    bufs += [pltpu.VMEM((3, rows, 128), bf16) for _, _, rows, _ in LANES]
    n = len(LANES)
    return pl.pallas_call(
        kernel,
        out_shape=(
            jax.ShapeDtypeStruct((PART, D), bf16),
            jax.ShapeDtypeStruct((PART, D), f32),
            jax.ShapeDtypeStruct((4, 24, 512), f32),
            jax.ShapeDtypeStruct((4, 24, 128), f32),
            jax.ShapeDtypeStruct((8, D), f32),
        ),
        in_specs=[vmem] * len(args),
        out_specs=(vmem,) * 5,
        scratch_shapes=[
            *bufs,
            pltpu.VMEM((2, 2, 4, 2, 4, BLOCK, 128), bf16),
            pltpu.VMEM((2, 2, 4, 2, 4, BLOCK, 128), bf16),
            pltpu.VMEM((2, 4, 2, 4, BLOCK, 128), bf16),
            pltpu.VMEM((3, PART, D), bf16),
            pltpu.VMEM((4, 32, D), f32),
            pltpu.VMEM((4, 32, D), bf16),
            pltpu.VMEM((4, 32, D), bf16),
            pltpu.VMEM((96, 512), f32),
            pltpu.VMEM((KEYS, 128), f32),
            pltpu.VMEM((KEYS, 128), f32),
            pltpu.VMEM((GROUPS, 80, 512), bf16),
            pltpu.VMEM((3, PART, D), bf16),
            pltpu.VMEM((3, D, PART), bf16),
            pltpu.VMEM((HD, KEYS), bf16),
            pltpu.VMEM((HD, KEYS), bf16),
            pltpu.VMEM((KEYS, HD), bf16),
            pltpu.VMEM((KEYS, HD), bf16),
            pltpu.VMEM((4, PART, HD), f32),
            pltpu.VMEM((4, PART, HD), bf16),
            pltpu.VMEM((4, PART, KEYS), f32),
            pltpu.VMEM((4, PART, HD), bf16),
            pltpu.VMEM((PART, D), bf16),
            pltpu.VMEM((D, PART), bf16),
            pltpu.VMEM((PART, D), bf16),
            pltpu.VMEM((D, PART), bf16),
            pltpu.VMEM((8, PART, 256), f32),
            pltpu.VMEM((8, PART, 256), f32),
            pltpu.VMEM((8, PART, 256), bf16),
            pltpu.VMEM((PART, D), f32),
            pltpu.VMEM((1, HD), f32),
            pltpu.VMEM((HD, KEYS), f32),
            pltpu.VMEM((HD, KEYS), f32),
            pltpu.VMEM((PART, D), f32),
            pltpu.VMEM((2, PART, D), bf16),
            pltpu.VMEM((8, 8, D), f32),
            pltpu.VMEM((7, 8, D), f32),
            pltpu.VMEM((4, 24, D), f32),
            dma((3,)), dma((3,)), dma((n, 3)), dma((n, 3)), dma((n, 16)), dma((n, 16)), dma((n, 16)), dma((n, 16)),
            dma((2,)), dma((2,)),
            dma((n, 3)), dma((n, 3)), dma((n, 16)), dma((n, 16)), dma((n, 16)), dma((n, 16)),
            dma((3,)), dma((3,)), dma((3,)), dma,
            dma((2,)), dma((2,)), dma((7,)), dma((7,)),
        ],
        compiler_params=pltpu.CompilerParams(
            collective_id=0, has_side_effects=True, vmem_limit_bytes=62 << 20
        ),
        name="layer",
    )(*args)


def finish_kernel(
    out_ref, gx_ref, shard_ref, kv_ref, gn_ref,
    out_to, gx_to, query_to, keyval_to, out_t_to, gate_to, up_to, down_t_to, *gains_to,
):
    out_to[...] = out_ref[...]
    gx_to[...] = gx_ref[...]
    for j in range(4):
        here = slice(128 * j, 128 * j + 128)
        if j < 2:
            query_to[:, here] = shard_ref[j, :20, :128]
        else:
            out_t_to[:, 128 * j - 256 : 128 * j - 128] = shard_ref[j, :20, :128]
        gate_to[:, here] = shard_ref[j, :20, 128:256]
        up_to[:, here] = shard_ref[j, :20, 256:384]
        down_t_to[:, here] = shard_ref[j, :20, 384:512]
        keyval_to[:, here] = kv_ref[j, :20, :]
    for i, ref in enumerate(gains_to):
        ref[...] = gn_ref[i : i + 1, : ref.shape[0]].reshape(ref.shape[0])


def finish(*args):
    vmem = pl.BlockSpec(memory_space=pltpu.VMEM)
    shapes = [((PART, D), bf16), ((PART, D), f32)]
    shapes += [((20, n), f32) for n in (256, 512, 256, 512, 512, 512)]
    shapes += [((n,), f32) for n in (D, D, D, D, HD, HD)]
    return pl.pallas_call(
        finish_kernel,
        out_shape=tuple(jax.ShapeDtypeStruct(*item) for item in shapes),
        in_specs=[vmem] * len(args),
        out_specs=(vmem,) * len(shapes),
        name="finish",
    )(*args)


def rope_parts():
    freq = (rope_base ** (-np.arange(0, HD, 2, dtype=np.float64) / HD))[None, :]
    angles = np.arange(KEYS, dtype=np.float64)[:, None] * freq
    return tuple(jnp.asarray(item.astype(np.float32)) for item in (np.cos(angles), np.sin(angles), freq))


def per_device(
    tokens, segments, cotangent, w_query, w_keyval, w_out, w_gate, w_up, w_down,
    gain_in, gain_post_attn, gain_pre_ff, gain_post_ff, gain_query, gain_key,
):
    made = layer(
        segments, w_query, w_keyval, w_out.T, w_gate, w_up, w_down.T, tokens, cotangent,
        gain_in, gain_post_attn, gain_pre_ff, gain_post_ff, gain_query, gain_key, *rope_parts(),
    )
    output, grad_x, query, keyval, out_t, gate, up, down_t, *gains = finish(*made)
    return (output, grad_x, query, keyval, out_t.T, gate, up, down_t.T, *gains)


def solution(mesh):
    tok = P(("dp", "tensor"), None)
    weights = (
        P("dp", "tensor"), P("dp", None), P("tensor", "dp"), P("dp", "tensor"), P("dp", "tensor"), P("tensor", "dp"),
    )
    return jax.shard_map(
        per_device,
        mesh=mesh,
        in_specs=(tok, P("dp", None), tok) + weights + (P(),) * 6,
        out_specs=(tok, tok) + weights + (P(),) * 6,
        check_vma=False,
    )
```

```python
import jax
import jax.numpy as jnp
import numpy as np
from jax import lax
from jax.experimental import pallas as pl
from jax.experimental.pallas import tpu as pltpu
from jax.sharding import PartitionSpec as P

HD = 256
WINDOW = 512
D = 640
PART = 256
KEYS = 768
BLOCK = 352
CB = 16
GROUPS = 8
KV0, G0, U0, D0 = 80, 112, 192, 272
ATTN = ((0, 0, 48, "xyz"), (1, 48, 32, "yzx"), (2, 80, 32, "zxy"))
FEED = ((3, 112, 80, "xyz"), (4, 192, 64, "yzx"), (5, 256, 96, "zxy"))
LANES = ATTN + FEED
norm_eps = 1e-06
rope_base = 10000.0
MESH = pl.DeviceIdType.MESH
f32 = jnp.float32
bf16 = jnp.bfloat16


def place():
    dp = lax.axis_index("dp")
    t = lax.axis_index("tensor")
    return {
        "x": (dp // 16) * 2 + t // 2,
        "y": dp % 4,
        "z": (dp // 4) % 4,
        "c": t % 2,
    }


def device_of(p):
    return {
        "dp": (p["x"] // 2) * 16 + p["z"] * 4 + p["y"],
        "tensor": (p["x"] % 2) * 2 + p["c"],
    }


def moved(p, axis, by):
    size = 2 if axis == "c" else 4
    q = dict(p)
    q[axis] = (p[axis] + by) % size
    return q


def diagonal(p):
    q = moved(p, "c", 1)
    q["x"] = (p["x"] // 2) * 2 + (1 - p["x"] % 2)
    return q


def peers_of(p):
    found = [
        moved(p, axis, by)
        for axis, by in (
            ("x", 1), ("x", 2), ("x", 3), ("y", 1), ("y", 2), ("y", 3), ("z", 1), ("z", 2), ("z", 3), ("c", 1)
        )
    ]
    return found + [diagonal(p)]


def say_here(p, t):
    barrier = pltpu.get_barrier_semaphore()
    for q in peers_of(p):
        pl.semaphore_signal(barrier, inc=1, device_id=device_of(q), device_id_type=MESH)
    for y in range(4):
        @pl.when((t != p["y"]) | (y != p["y"]))
        def _(y=y):
            there = {"dp": lax.axis_index("dp") - p["y"] + y, "tensor": p["y"]}
            pl.semaphore_signal(barrier, inc=1, device_id=there, device_id_type=MESH)


def all_here(p, t):
    barrier = pltpu.get_barrier_semaphore()
    pl.semaphore_wait(barrier, len(peers_of(p)) + jnp.where(t == p["y"], 3, 4))


def send(src, dst, send_sem, recv_sem, q):
    copy = pltpu.make_async_remote_copy(
        src_ref=src,
        dst_ref=dst,
        send_sem=send_sem,
        recv_sem=recv_sem,
        device_id=device_of(q),
        device_id_type=MESH,
    )
    copy.start()
    return copy


def block_of(ref, at, first, rows, core=None):
    every = slice(None)
    where = (at["x"] % 2,) + (() if core is None else (core,)) + (at["y"], at["x"] // 2, at["z"], pl.ds(first, rows), every)
    return ref.at[where]


def unit_of(ref, at, axis, first, rows, core=None):
    every = slice(None)
    x_lo, x_hi = (every, every) if axis == "x" else (at["x"] % 2, at["x"] // 2)
    y = every if axis == "y" else at["y"]
    z = every if axis == "z" else at["z"]
    where = (x_lo,) + (() if core is None else (core,)) + (y, x_hi, z, pl.ds(first, rows), every)
    return ref.at[where]


def unit_shape(axis, rows):
    return ((2, 2) if axis == "x" else (4,)) + (rows, 128)


AWAY = (0, 1, 2, 1)
OFFSETS = [(j, k) for j in range(4) for k in range(4)]


def depth(offset):
    return AWAY[offset[0]] + AWAY[offset[1]]


def way_two(lane):
    return 1 if lane % 2 == 0 else 3


def way_three(lane, j):
    return 1 if j % 2 == 0 and lane % 3 != 1 else 3


def onward(lane, offset):
    j, k = offset
    to = []
    if k == 0:
        to += [(2, 1), (2, 3)]
        if j == 0:
            to += [(1, 1), (1, 3)]
        elif j == way_two(lane):
            to += [(1, j)]
    elif k == way_three(lane, j):
        to += [(2, k)]
    return to


def after(offset, axis_number, by):
    j, k = offset
    return ((j + by) % 4, k) if axis_number == 1 else (j, (k + by) % 4)


def source(p, order, offset):
    return moved(moved(p, order[1], 4 - offset[0]), order[2], 4 - offset[1])


def wait_bytes(ref, sem):
    pltpu.make_async_copy(ref, ref, sem).wait()


def gather_steps(lanes, w_ref, p, sems, shares):
    line_send, line_recv, unit_send, unit_recv, sib_send, sib_recv = sems
    core = p["c"]
    sibling = moved(p, "c", 1)
    sent = []
    lines = []
    for lane, at, rows, order in lanes:
        mine = block_of(w_ref, p, at, rows, core)
        for by in (1, 3, 2):
            q = moved(p, order[0], by)
            lines.append(send(mine, mine, line_send.at[lane, by - 1], line_recv.at[lane, by - 1], q))
    yield

    def pass_on(lane, at, rows, order, offset):
        unit = unit_of(w_ref, source(p, order, offset), order[0], at, rows, core)
        for number, by in onward(lane, offset):
            j, k = after(offset, number, by)
            sem = lane, j * 4 + k
            sent.append(send(unit, unit, unit_send.at[sem], unit_recv.at[sem], moved(p, order[number], by)))
        j, k = offset
        sem = lane, j * 4 + k
        shares.append(send(unit, unit, sib_send.at[sem], sib_recv.at[sem], sibling))

    for i, (lane, at, rows, order) in enumerate(lanes):
        for copy in lines[3 * i : 3 * i + 3]:
            copy.wait_recv()
        pass_on(lane, at, rows, order, (0, 0))
    yield
    for far in (1, 2, 3, 4):
        for lane, at, rows, order in lanes:
            for offset in OFFSETS:
                if depth(offset) == far:
                    j, k = offset
                    unit = unit_of(w_ref, source(p, order, offset), order[0], at, rows, core)
                    pltpu.make_async_remote_copy(
                        src_ref=unit, dst_ref=unit,
                        send_sem=unit_send.at[lane, j * 4 + k], recv_sem=unit_recv.at[lane, j * 4 + k],
                        device_id=device_of(sibling), device_id_type=MESH,
                    ).wait_recv()
                    pass_on(lane, at, rows, order, offset)
        yield
    for copy in shares:
        copy.wait_recv()
    for copy in lines + sent + shares:
        copy.wait_send()
    yield


def add_unit(acc, p, at, axis, first, rows, terms):
    def step(i, _):
        q = dict(at)
        q[axis] = i
        target = (q["x"] % 2, p["c"], q["y"], q["x"] // 2, q["z"], pl.ds(first, rows), slice(None))
        where = (i % 2, i // 2) if axis == "x" else (i,)
        total = acc[target]
        for term in terms:
            total = total + term[where]
        acc[target] = total
        return 0

    lax.fori_loop(0, 4, step, 0, unroll=rows < 64)


def reduce_steps(lanes, g_ref, other, bufs, line_bufs, p, sems):
    line_send, line_recv, unit_send, unit_recv, sib_send, sib_recv = sems
    core = p["c"]
    sibling = moved(p, "c", 1)
    halves, sent = {}, {}
    for far in (4, 3, 2, 1, 0):
        for lane, at, rows, order in lanes:
            for offset in OFFSETS:
                if depth(offset) == far:
                    where = source(p, order, offset)
                    src = unit_of(g_ref, where, order[0], at, rows, sibling["c"])
                    dst = unit_of(other, where, order[0], at, rows)
                    sem = lane, offset[0] * 4 + offset[1]
                    halves[lane, offset] = send(src, dst, sib_send.at[sem], sib_recv.at[sem], sibling)
    yield

    def add(lane, at, rows, order, offset):
        halves[lane, offset].wait_recv()
        where = source(p, order, offset)
        terms = [unit_of(other, where, order[0], at, rows)]
        for number, by in onward(lane, offset):
            child = after(offset, number, by)
            sent[lane, child].wait_recv()
            terms.append(bufs[lane].at[child[0] * 4 + child[1] - 1])
        add_unit(g_ref, p, where, order[0], at, rows, terms)

    def back(lane, at, rows, order, offset):
        for parent in OFFSETS:
            for number, by in onward(lane, parent):
                if after(parent, number, by) == offset:
                    j, k = offset
                    sem = lane, j * 4 + k
                    unit = unit_of(g_ref, source(p, order, offset), order[0], at, rows, core)
                    sent[lane, offset] = send(
                        unit, bufs[lane].at[j * 4 + k - 1], unit_send.at[sem], unit_recv.at[sem],
                        moved(p, order[number], 4 - by),
                    )

    for far in (4, 3, 2, 1):
        for lane, at, rows, order in lanes:
            for offset in OFFSETS:
                if depth(offset) == far:
                    add(lane, at, rows, order, offset)
                    back(lane, at, rows, order, offset)
        yield
    lines = []
    for lane, at, rows, order in lanes:
        add(lane, at, rows, order, (0, 0))
        for by in (1, 3, 2):
            q = moved(p, order[0], by)
            src = block_of(g_ref, q, at, rows, core)
            lines.append(
                send(src, line_bufs[lane].at[by - 1], line_send.at[lane, by - 1], line_recv.at[lane, by - 1], q)
            )
    yield
    for i, (lane, at, rows, order) in enumerate(lanes):
        for copy in lines[3 * i : 3 * i + 3]:
            copy.wait_recv()
        target = (p["x"] % 2, core, p["y"], p["x"] // 2, p["z"], pl.ds(at, rows), slice(None))
        total = g_ref[target].astype(f32)
        for by in range(3):
            total = total + line_bufs[lane][by].astype(f32)
        g_ref[target] = total.astype(bf16)
    for copy in lines + list(sent.values()) + list(halves.values()):
        copy.wait_send()
    yield


def dot(a, b):
    return jnp.dot(a, b, preferred_element_type=f32)


def dot_nt(a, b):
    return lax.dot_general(a, b, (((1,), (1,)), ((), ())), preferred_element_type=f32)


def inv_rms(v):
    return lax.rsqrt(jnp.mean(v * v, axis=-1, keepdims=True) + norm_eps)


def norm_back(v, r, c, e):
    ec = e * c
    vr = v * r
    dv = r * (ec - vr * jnp.mean(vr * ec, axis=-1, keepdims=True))
    return dv, jnp.sum(e * vr, axis=0, keepdims=True)


def turn(u, cos, sin):
    a, b = u[:, :128], u[:, 128:]
    return jnp.concatenate([a * cos - b * sin, b * cos + a * sin], axis=1)


def turn_back(e, cos, sin):
    a, b = e[:, :128], e[:, 128:]
    return jnp.concatenate([a * cos + b * sin, b * cos - a * sin], axis=1)


def columns(w_ref, t, y, first):
    return jnp.concatenate(
        [w_ref[t // 2, t % 2, y + i, :, :, first : first + 80, :].reshape(D, 128) for i in range(2)], axis=1
    )


def put_columns(g_ref, t, y, first, value):
    value = value.astype(bf16)
    for i in range(2):
        g_ref[t // 2, t % 2, y + i, :, :, first : first + 80, :] = (
            value[:, 128 * i : 128 * i + 128].reshape(2, 4, 80, 128)
        )


NB = len(LANES)


def kernel(
    seg_ref, wq_ref, wkv_ref, wo_ref, wg_ref, wu_ref, wd_ref, x_ref, cot_ref,
    gin_ref, gpa_ref, gpf_ref, gpo_ref, gq_ref, gk_ref, cos_tab, sin_tab, freq_ref,
    out_ref, gx_ref, shard_ref, kv_ref, gn_out,
    *scratch,
):
    bufs, line_bufs, scratch = scratch[:NB], scratch[NB : 2 * NB], scratch[2 * NB :]
    (
        w_ref, g_ref, other, xg, rows_s, s_ref, got, stage,
        cos_ref, sin_ref, wkv, attn_in, attn_in_t, kt, vt, kb, vb, qraw, qb, probs, ctx,
        mlp_in, mlp_in_t, d_b, d_t, act_s, dact_s, hid_s, acc, acc2, dkt, dvt, proj_s,
        dx_got, gn_now, gn_got, final,
        one_send, one_recv, line_send, line_recv, unit_send, unit_recv, sib_send, sib_recv, x_send, x_recv,
        bline_send, bline_recv, back_send, back_recv, bsib_send, bsib_recv, last_send, last_recv, kv_send, kv_recv,
        dx_send, dx_recv, gn_send, gn_recv,
    ) = scratch
    p = place()
    t = lax.axis_index("tensor")
    dp = lax.axis_index("dp")
    y = p["y"]
    core = p["c"]
    own = (p["x"] % 2, core, y, p["x"] // 2, p["z"])
    say_here(p, t)

    rows_s[...] = jnp.zeros_like(rows_s)
    for j in range(4):
        if j < 2:
            rows_s[j, :20, :128] = wq_ref[:, 128 * j : 128 * j + 128].astype(f32)
        else:
            rows_s[j, :20, :128] = wo_ref[:, 128 * j - 256 : 128 * j - 128].astype(f32)
        rows_s[j, :20, 128:256] = wg_ref[:, 128 * j : 128 * j + 128].astype(f32)
        rows_s[j, :20, 256:384] = wu_ref[:, 128 * j : 128 * j + 128].astype(f32)
        rows_s[j, :20, 384:512] = wd_ref[:, 128 * j : 128 * j + 128].astype(f32)
        rows_s[j, :20, 512:] = wkv_ref[:, 128 * j : 128 * j + 128].astype(f32)
    s_ref[...] = rows_s[...].astype(bf16)
    gin, gpa, gpf, gpo, gq, gk = (
        ref[...].reshape(1, ref.shape[0]) for ref in (gin_ref, gpa_ref, gpf_ref, gpo_ref, gq_ref, gk_ref)
    )
    scale = HD ** -0.5
    seg = seg_ref[...]
    n0 = jnp.sum(jnp.where(seg == 0, 1.0, 0.0), axis=1, keepdims=True)
    n1 = jnp.sum(jnp.where(seg <= 1, 1.0, 0.0), axis=1, keepdims=True)
    base = ((t - 2) * PART).astype(f32)
    which = lax.broadcasted_iota(jnp.int32, (8, 128), 0)
    turn_by = (jnp.where(which == 0, 0.0, jnp.where(which == 1, n0, n1)) - base) * freq_ref[...]
    cb, sb = jnp.cos(turn_by), jnp.sin(turn_by)
    token = lax.broadcasted_iota(jnp.int32, (KEYS, 1), 0).astype(f32) + base
    in0, in1 = token < n0, token < n1
    cd = jnp.where(in0, cb[0:1], jnp.where(in1, cb[1:2], cb[2:3]))
    sd = jnp.where(in0, sb[0:1], jnp.where(in1, sb[1:2], sb[2:3]))
    ca, sa = cos_tab[...], sin_tab[...]
    cos_ref[...] = ca * cd + sa * sd
    sin_ref[...] = sa * cd - ca * sd

    xg[2] = x_ref[...]
    got[pl.ds(y, 1)] = s_ref[pl.ds(y, 1)]
    all_here(p, t)
    first = []
    for k in (1, 3, 2):
        q = moved(p, "y", k)
        first.append(send(s_ref.at[q["y"]], got.at[y], one_send.at[k - 1], one_recv.at[k - 1], q))

    def token_copy(src, slot, to):
        return pltpu.make_async_remote_copy(
            src_ref=src, dst_ref=xg.at[slot], send_sem=x_send.at[1 - slot], recv_sem=x_recv.at[1 - slot],
            device_id={"dp": dp, "tensor": to}, device_id_type=MESH,
        )

    @pl.when(t < 3)
    def _():
        token_copy(x_ref, 1, jnp.minimum(t + 1, 3)).start()

    @pl.when(t == 0)
    def _():
        token_copy(x_ref, 0, t + 2).start()

    for copy in first:
        copy.wait_recv()
    for j in range(4):
        stage[20 * j : 20 * j + 20, :] = got[j].astype(f32)[:20, :512]
    for i, at in enumerate((0, G0, U0, D0)):
        w_ref[own + (slice(at, at + 80),)] = stage[:80, 128 * i : 128 * i + 128].astype(bf16)
    w_ref[own + (slice(KV0, KV0 + 32),)] = got[pl.ds(t, 1)][0, :, 512:640]
    for copy in first:
        copy.wait_send()

    sems = (line_send, line_recv, unit_send, unit_recv, sib_send, sib_recv)
    attn = gather_steps(ATTN, w_ref, p, sems, [])
    feed = gather_steps(FEED, w_ref, p, sems, [])
    next(attn)
    for _ in range(5):
        next(feed)
        next(attn)

    @pl.when(t > 0)
    def _():
        token_copy(x_ref, 1, jnp.minimum(t + 1, 3)).wait_recv()

    @pl.when(t == 2)
    def _():
        token_copy(xg.at[1], 0, jnp.minimum(t + 1, 3)).start()

    @pl.when(t >= 2)
    def _():
        token_copy(x_ref, 0, jnp.minimum(t + 1, 3)).wait_recv()

    @pl.when(t < 3)
    def _():
        token_copy(x_ref, 1, jnp.minimum(t + 1, 3)).wait_send()

    @pl.when(lax.rem(t, 2) == 0)
    def _():
        token_copy(x_ref, 0, jnp.minimum(t + 1, 3)).wait_send()

    def tokens(i):
        return jnp.where(i >= 2 - t, xg[i].astype(f32), 0.0)

    def input_norm(i, _):
        x = tokens(i)
        a = x * inv_rms(x) * gin
        attn_in[i] = a.astype(bf16)
        attn_in_t[i] = a.T.astype(bf16)
        return 0

    lax.fori_loop(0, 3, input_norm, 0)
    acc[...] = jnp.zeros_like(acc)
    next(attn)

    def keyval_in(g, _):
        for tt in range(4):
            for yy in range(4):
                stage[20 * tt : 20 * tt + 20, 128 * yy : 128 * yy + 128] = (
                    w_ref[tt // 2, tt % 2, yy, g // 4, g % 4, KV0 : KV0 + 32, :].astype(f32)[:20]
                )
        wkv[g] = stage[:80, :].astype(bf16)
        return 0

    lax.fori_loop(0, GROUPS, keyval_in, 0)

    def rows_of(i):
        return pl.ds(pl.multiple_of(i * PART, PART), PART)

    def keys_values(i, _):
        rows = rows_of(i)
        kv_raw = dot(attn_in[i], wkv[...].reshape(D, 512))
        kraw = kv_raw[:, :HD]
        k = turn(kraw * inv_rms(kraw) * gk, cos_ref[rows, :], sin_ref[rows, :])
        kb[rows, :] = k.astype(bf16)
        kt[:, rows] = k.T.astype(bf16)
        v = kv_raw[:, HD:]
        vb[rows, :] = v.astype(bf16)
        vt[:, rows] = v.T.astype(bf16)
        return 0

    lax.fori_loop(0, 3, keys_values, 0)
    next(feed)

    def head(h, _):
        cos_q, sin_q = cos_ref[2 * PART :, :], sin_ref[2 * PART :, :]
        column = lax.broadcasted_iota(jnp.int32, (PART, KEYS), 1)
        last = lax.broadcasted_iota(jnp.int32, (PART, 1), 0) + 2 * PART
        own_token = last.astype(f32) + base
        start = jnp.where(own_token < n0, 0.0, jnp.where(own_token < n1, n0, n1))
        low = jnp.maximum(own_token - (WINDOW - 1), start) - base
        raw = dot(attn_in[2], columns(w_ref, h, 0, 0))
        qraw[h] = raw
        q = turn(raw * inv_rms(raw) * gq, cos_q, sin_q).astype(bf16)
        qb[h] = q
        s = dot(q, kt[...]) * scale
        s = jnp.where((column.astype(f32) >= low) & (column <= last), s, -1e30)
        e = jnp.exp(s - jnp.max(s, axis=-1, keepdims=True))
        pr = e / jnp.sum(e, axis=-1, keepdims=True)
        probs[h] = pr
        c = dot(pr.astype(bf16), vb[...]).astype(bf16)
        ctx[h] = c
        acc[...] += dot_nt(c, columns(w_ref, h, 2, 0))
        return 0

    lax.fori_loop(0, 4, head, 0)
    proj = acc[...]
    proj_s[...] = proj
    mid = x_ref[...].astype(f32) + proj * inv_rms(proj) * gpa
    gx_ref[...] = mid
    m = mid * inv_rms(mid) * gpf
    mlp_in[...] = m.astype(bf16)
    mlp_in_t[...] = m.T.astype(bf16)
    acc[...] = jnp.zeros_like(acc)
    next(feed)

    def feed_forward(c, _):
        tt, yy = c // 2, 2 * (c % 2)
        gate = dot(mlp_in[...], columns(w_ref, tt, yy, G0))
        up = dot(mlp_in[...], columns(w_ref, tt, yy, U0))
        k0, k1 = 0.7978845608028654, 0.044715
        sq = gate * gate
        th = jnp.tanh(k0 * (gate + k1 * gate * sq))
        half = 0.5 * (1.0 + th)
        act = gate * half
        hid = (act * up).astype(bf16)
        act_s[c] = act
        dact_s[c] = up * (half + 0.5 * gate * (1.0 - th * th) * (k0 + (3.0 * k0 * k1) * sq))
        hid_s[c] = hid
        acc[...] += dot_nt(hid, columns(w_ref, tt, yy, D0))
        return 0

    lax.fori_loop(0, 8, feed_forward, 0)
    mlp = acc[...]
    r = inv_rms(mlp)
    out_ref[...] = (gx_ref[...] + mlp * r * gpo).astype(bf16)
    d_mlp, g_po = norm_back(mlp, r, gpo, cot_ref[...].astype(f32))
    gn_now[0, 3:4, :] = g_po
    d_b[...] = d_mlp.astype(bf16)
    d_t[...] = d_mlp.T.astype(bf16)
    acc[...] = jnp.zeros_like(acc)

    def feed_back(c, _):
        tt, yy = c // 2, 2 * (c % 2)
        put_columns(g_ref, tt, yy, D0, dot(d_t[...], hid_s[c]))
        d_hid = dot(d_b[...], columns(w_ref, tt, yy, D0))
        d_gate = (d_hid * dact_s[c]).astype(bf16)
        d_up = (d_hid * act_s[c]).astype(bf16)
        put_columns(g_ref, tt, yy, G0, dot(mlp_in_t[...], d_gate))
        put_columns(g_ref, tt, yy, U0, dot(mlp_in_t[...], d_up))
        acc[...] += dot_nt(d_gate, columns(w_ref, tt, yy, G0)) + dot_nt(d_up, columns(w_ref, tt, yy, U0))
        return 0

    lax.fori_loop(0, 8, feed_back, 0)
    sems = (bline_send, bline_recv, back_send, back_recv, bsib_send, bsib_recv)
    feed = reduce_steps(FEED, g_ref, other, bufs, line_bufs, p, sems)
    next(feed)

    mid = gx_ref[...]
    d_pre, g_pf = norm_back(mid, inv_rms(mid), gpf, acc[...])
    gn_now[0, 2:3, :] = g_pf
    d_mid = cot_ref[...].astype(f32) + d_pre
    proj = proj_s[...]
    d_proj, g_pa = norm_back(proj, inv_rms(proj), gpa, d_mid)
    gn_now[0, 1:2, :] = g_pa
    gx_ref[...] = d_mid
    d_b[...] = d_proj.astype(bf16)
    d_t[...] = d_proj.T.astype(bf16)
    dkt[...] = jnp.zeros_like(dkt)
    dvt[...] = jnp.zeros_like(dvt)
    acc[...] = jnp.zeros_like(acc)
    acc2[...] = jnp.zeros_like(acc2)
    next(feed)

    def head_back(h, _):
        cos_q, sin_q = cos_ref[2 * PART :, :], sin_ref[2 * PART :, :]
        put_columns(g_ref, h, 2, 0, dot(d_t[...], ctx[h]))
        d_ctx = dot(d_b[...], columns(w_ref, h, 2, 0))
        d_ctx_b = d_ctx.astype(bf16)
        pr = probs[h]
        d_pr = dot(d_ctx_b, vt[...])
        dvt[...] += dot(d_ctx.T.astype(bf16), pr.astype(bf16))
        inner = jnp.sum(pr * d_pr, axis=-1, keepdims=True)
        ds = (pr * (d_pr - inner)).astype(bf16)
        dq = dot(ds, kb[...]) * scale
        dkt[...] += dot(qb[h].astype(f32).T.astype(bf16), ds)
        raw = qraw[h]
        d_raw, g_q = norm_back(raw, inv_rms(raw), gq, turn_back(dq, cos_q, sin_q))
        acc2[...] += g_q
        d_raw = d_raw.astype(bf16)
        put_columns(g_ref, h, 0, 0, dot(attn_in_t[2], d_raw))
        acc[...] += dot_nt(d_raw, columns(w_ref, h, 0, 0))
        return 0

    lax.fori_loop(0, 2, head_back, 0)
    next(feed)
    lax.fori_loop(2, 4, head_back, 0)
    gn_now[0, 4:8, :] = jnp.zeros((4, D), f32)
    gn_now[0, 4:5, :HD] = acc2[...]
    acc2[...] = jnp.zeros_like(acc2)

    def keys_values_back(i, _):
        rows = rows_of(i)
        raw = dot(attn_in[i], wkv[:, :, :HD].reshape(D, HD))
        e = turn_back(dkt[:, rows].T * scale, cos_ref[rows, :], sin_ref[rows, :])
        dk, g_k = norm_back(raw, inv_rms(raw), gk, e)
        acc2[...] += g_k
        kb[rows, :] = dk.astype(bf16)
        vb[rows, :] = dvt[:, rows].T.astype(bf16)
        return 0

    lax.fori_loop(0, 3, keys_values_back, 0)
    gn_now[0, 5:6, :HD] = acc2[...]
    for half, src in enumerate((kb, vb)):
        grad = sum(dot(attn_in_t[i], src[PART * i : PART * i + PART, :]) for i in range(3))
        stage[80:, :] = jnp.zeros((16, 512), f32)
        for g in range(GROUPS):
            stage[:80, :HD] = grad[80 * g : 80 * g + 80]
            for tt in range(4):
                for yy in range(2):
                    g_ref[tt // 2, tt % 2, 2 * half + yy, g // 4, g % 4, KV0 : KV0 + 32, :] = (
                        stage[20 * tt : 20 * tt + 32, 128 * yy : 128 * yy + 128].astype(bf16)
                    )
    attn = reduce_steps(ATTN, g_ref, other, bufs, line_bufs, p, sems)
    next(attn)
    next(feed)

    def input_back(i, extra):
        rows = rows_of(i)
        d_in = dot_nt(kb[rows, :], wkv[:, :, :HD].reshape(D, HD)) + dot_nt(vb[rows, :], wkv[:, :, HD:].reshape(D, HD))
        x = tokens(i)
        dx, g_in = norm_back(x, inv_rms(x), gin, d_in if extra is None else d_in + extra)
        gn_now[0, 0:1, :] += g_in
        return dx

    def input_back_before(i, _):
        attn_in[i] = input_back(i, None).astype(bf16)
        return 0

    gn_now[0, 0:1, :] = jnp.zeros((1, D), f32)
    lax.fori_loop(0, 2, input_back_before, 0)
    gx_ref[...] += input_back(2, acc[...])

    def dx_copy(k):
        to = jnp.maximum(t - 1, 0) if k == 1 else jnp.where(t == 3, 2, 0)
        return pltpu.make_async_remote_copy(
            src_ref=attn_in.at[2 - k], dst_ref=dx_got.at[k - 1], send_sem=dx_send.at[k - 1], recv_sem=dx_recv.at[k - 1],
            device_id={"dp": dp, "tensor": to}, device_id_type=MESH,
        )

    @pl.when(t >= 2)
    def _():
        dx_copy(2).start()

    @pl.when(lax.rem(t, 2) == 1)
    def _():
        dx_copy(1).start()

    def pair(i):
        if i == 6:
            return moved(p, "c", 1)
        axis = "xyz"[i // 2]
        m = p[axis]
        q = dict(p)
        q[axis] = (m // 2) * 2 + (1 - m % 2) if i % 2 == 0 else 3 - m
        return q

    gn_copies = []

    def gn_start(i):
        gn_copies.append(send(gn_now.at[i], gn_got.at[i], gn_send.at[i], gn_recv.at[i], pair(i)))

    def gn_add(i):
        gn_copies[i].wait_recv()
        gn_now[i + 1] = gn_now[i] + gn_got[i]

    gn_start(0)
    for i in range(6):
        next(attn)
        if i == 0:
            @pl.when(t == 2)
            def _():
                dx_copy(2).wait_recv()
                attn_in[1] = (attn_in[1].astype(f32) + dx_got[1].astype(f32)).astype(bf16)
                dx_copy(1).start()

        if i < 3:
            next(feed)
        gn_add(i)
        gn_start(i + 1)

    mine = g_ref[own].astype(f32)
    for i, at in enumerate((0, G0, U0, D0)):
        for j in range(4):
            rows_s[j, 0:20, 128 * i : 128 * i + 128] = mine[at + 20 * j : at + 20 * j + 20]
    for j in range(4):
        rows_s[j, :24, 512:] = mine[KV0 : KV0 + 24]

    @pl.when(t == y)
    def _():
        kv_ref[pl.ds(y, 1)] = mine[KV0 : KV0 + 24][None]


    def kv_copy(k):
        return pltpu.make_async_remote_copy(
            src_ref=rows_s.at[0, pl.ds(0, 24), pl.ds(512, 128)], dst_ref=kv_ref.at[y],
            send_sem=kv_send.at[k], recv_sem=kv_recv.at[y],
            device_id={"dp": dp - y + t, "tensor": (t + k) % 4}, device_id_type=MESH,
        )

    @pl.when(t != y)
    def _():
        kv_copy(0).start()

    for k in (1, 2, 3):
        kv_copy(k).start()
    last = []
    for k in (1, 3, 2):
        q = moved(p, "y", k)
        last.append(send(rows_s.at[q["y"], pl.ds(0, 24), :], final.at[y], last_send.at[k - 1], last_recv.at[k - 1], q))
    final[pl.ds(y, 1)] = rows_s[pl.ds(y, 1), :24]
    gn_add(6)
    gn_out[...] = gn_now[7]

    @pl.when(t < 3)
    def _():
        dx_copy(1).wait_recv()
        gx_ref[...] += dx_got[0].astype(f32)

    @pl.when(t == 0)
    def _():
        dx_copy(2).wait_recv()
        gx_ref[...] += dx_got[1].astype(f32)

    @pl.when(t >= 1)
    def _():
        dx_copy(1).wait_send()

    @pl.when(t >= 2)
    def _():
        dx_copy(2).wait_send()

    for copy in last:
        copy.wait_recv()

    shard_ref[...] = final[:, :, :512]
    for copy in gn_copies + last:
        copy.wait_send()

    for k in (1, 2, 3):
        kv_copy(k).wait_send()

    @pl.when(t != y)
    def _():
        kv_copy(0).wait_send()

    for j in range(4):
        @pl.when((t != y) | (y != j))
        def _(j=j):
            pltpu.make_async_remote_copy(
                src_ref=kv_ref.at[j], dst_ref=kv_ref.at[j], send_sem=kv_send.at[0], recv_sem=kv_recv.at[j],
                device_id={"dp": dp, "tensor": (t + 1) % 4}, device_id_type=MESH,
            ).wait_recv()


def layer(*args):
    dma = pltpu.SemaphoreType.DMA
    vmem = pl.BlockSpec(memory_space=pltpu.VMEM)
    bufs = [pltpu.VMEM((15,) + unit_shape(order[0], rows), bf16) for _, _, rows, order in LANES]
    bufs += [pltpu.VMEM((3, rows, 128), bf16) for _, _, rows, _ in LANES]
    n = len(LANES)
    return pl.pallas_call(
        kernel,
        out_shape=(
            jax.ShapeDtypeStruct((PART, D), bf16),
            jax.ShapeDtypeStruct((PART, D), f32),
            jax.ShapeDtypeStruct((4, 24, 512), f32),
            jax.ShapeDtypeStruct((4, 24, 128), f32),
            jax.ShapeDtypeStruct((8, D), f32),
        ),
        in_specs=[vmem] * len(args),
        out_specs=(vmem,) * 5,
        scratch_shapes=[
            *bufs,
            pltpu.VMEM((2, 2, 4, 2, 4, BLOCK, 128), bf16),
            pltpu.VMEM((2, 2, 4, 2, 4, BLOCK, 128), bf16),
            pltpu.VMEM((2, 4, 2, 4, BLOCK, 128), bf16),
            pltpu.VMEM((3, PART, D), bf16),
            pltpu.VMEM((4, 32, D), f32),
            pltpu.VMEM((4, 32, D), bf16),
            pltpu.VMEM((4, 32, D), bf16),
            pltpu.VMEM((96, 512), f32),
            pltpu.VMEM((KEYS, 128), f32),
            pltpu.VMEM((KEYS, 128), f32),
            pltpu.VMEM((GROUPS, 80, 512), bf16),
            pltpu.VMEM((3, PART, D), bf16),
            pltpu.VMEM((3, D, PART), bf16),
            pltpu.VMEM((HD, KEYS), bf16),
            pltpu.VMEM((HD, KEYS), bf16),
            pltpu.VMEM((KEYS, HD), bf16),
            pltpu.VMEM((KEYS, HD), bf16),
            pltpu.VMEM((4, PART, HD), f32),
            pltpu.VMEM((4, PART, HD), bf16),
            pltpu.VMEM((4, PART, KEYS), f32),
            pltpu.VMEM((4, PART, HD), bf16),
            pltpu.VMEM((PART, D), bf16),
            pltpu.VMEM((D, PART), bf16),
            pltpu.VMEM((PART, D), bf16),
            pltpu.VMEM((D, PART), bf16),
            pltpu.VMEM((8, PART, 256), f32),
            pltpu.VMEM((8, PART, 256), f32),
            pltpu.VMEM((8, PART, 256), bf16),
            pltpu.VMEM((PART, D), f32),
            pltpu.VMEM((1, HD), f32),
            pltpu.VMEM((HD, KEYS), f32),
            pltpu.VMEM((HD, KEYS), f32),
            pltpu.VMEM((PART, D), f32),
            pltpu.VMEM((2, PART, D), bf16),
            pltpu.VMEM((8, 8, D), f32),
            pltpu.VMEM((7, 8, D), f32),
            pltpu.VMEM((4, 24, D), f32),
            dma((3,)), dma((3,)), dma((n, 3)), dma((n, 3)), dma((n, 16)), dma((n, 16)), dma((n, 16)), dma((n, 16)),
            dma((2,)), dma((2,)),
            dma((n, 3)), dma((n, 3)), dma((n, 16)), dma((n, 16)), dma((n, 16)), dma((n, 16)),
            dma((3,)), dma((3,)), dma((4,)), dma((4,)),
            dma((2,)), dma((2,)), dma((7,)), dma((7,)),
        ],
        compiler_params=pltpu.CompilerParams(
            collective_id=0, has_side_effects=True, vmem_limit_bytes=62 << 20
        ),
        name="layer",
    )(*args)


def finish_kernel(
    out_ref, gx_ref, shard_ref, kv_ref, gn_ref,
    out_to, gx_to, query_to, keyval_to, out_t_to, gate_to, up_to, down_t_to, *gains_to,
):
    out_to[...] = out_ref[...]
    gx_to[...] = gx_ref[...]
    for j in range(4):
        here = slice(128 * j, 128 * j + 128)
        if j < 2:
            query_to[:, here] = shard_ref[j, :20, :128]
        else:
            out_t_to[:, 128 * j - 256 : 128 * j - 128] = shard_ref[j, :20, :128]
        gate_to[:, here] = shard_ref[j, :20, 128:256]
        up_to[:, here] = shard_ref[j, :20, 256:384]
        down_t_to[:, here] = shard_ref[j, :20, 384:512]
        keyval_to[:, here] = kv_ref[j, :20, :]
    for i, ref in enumerate(gains_to):
        ref[...] = gn_ref[i : i + 1, : ref.shape[0]].reshape(ref.shape[0])


def finish(*args):
    vmem = pl.BlockSpec(memory_space=pltpu.VMEM)
    shapes = [((PART, D), bf16), ((PART, D), f32)]
    shapes += [((20, n), f32) for n in (256, 512, 256, 512, 512, 512)]
    shapes += [((n,), f32) for n in (D, D, D, D, HD, HD)]
    return pl.pallas_call(
        finish_kernel,
        out_shape=tuple(jax.ShapeDtypeStruct(*item) for item in shapes),
        in_specs=[vmem] * len(args),
        out_specs=(vmem,) * len(shapes),
        name="finish",
    )(*args)


def rope_parts():
    freq = (rope_base ** (-np.arange(0, HD, 2, dtype=np.float64) / HD))[None, :]
    angles = np.arange(KEYS, dtype=np.float64)[:, None] * freq
    return tuple(jnp.asarray(item.astype(np.float32)) for item in (np.cos(angles), np.sin(angles), freq))


def per_device(
    tokens, segments, cotangent, w_query, w_keyval, w_out, w_gate, w_up, w_down,
    gain_in, gain_post_attn, gain_pre_ff, gain_post_ff, gain_query, gain_key,
):
    made = layer(
        segments, w_query, w_keyval, w_out.T, w_gate, w_up, w_down.T, tokens, cotangent,
        gain_in, gain_post_attn, gain_pre_ff, gain_post_ff, gain_query, gain_key, *rope_parts(),
    )
    output, grad_x, query, keyval, out_t, gate, up, down_t, *gains = finish(*made)
    return (output, grad_x, query, keyval, out_t.T, gate, up, down_t.T, *gains)


def solution(mesh):
    tok = P(("dp", "tensor"), None)
    weights = (
        P("dp", "tensor"), P("dp", None), P("tensor", "dp"), P("dp", "tensor"), P("dp", "tensor"), P("tensor", "dp"),
    )
    return jax.shard_map(
        per_device,
        mesh=mesh,
        in_specs=(tok, P("dp", None), tok) + weights + (P(),) * 6,
        out_specs=(tok, tok) + weights + (P(),) * 6,
        check_vma=False,
    )
```

```python
import jax
import jax.numpy as jnp
import numpy as np
from jax import lax
from jax.experimental import pallas as pl
from jax.experimental.pallas import tpu as pltpu
from jax.sharding import PartitionSpec as P

HD = 256
WINDOW = 512
D = 640
PART = 256
KEYS = 768
BLOCK = 352
CB = 16
GROUPS = 8
KV0, G0, U0, D0 = 80, 112, 192, 272
ATTN = ((0, 0, 48, "xyz"), (1, 48, 32, "yzx"), (2, 80, 32, "zxy"))
FEED = ((3, 112, 80, "xyz"), (4, 192, 64, "yzx"), (5, 256, 96, "zxy"))
LANES = ATTN + FEED
norm_eps = 1e-06
rope_base = 10000.0
MESH = pl.DeviceIdType.MESH
f32 = jnp.float32
bf16 = jnp.bfloat16


def place():
    dp = lax.axis_index("dp")
    t = lax.axis_index("tensor")
    return {
        "x": (dp // 16) * 2 + t // 2,
        "y": dp % 4,
        "z": (dp // 4) % 4,
        "c": t % 2,
    }


def device_of(p):
    return {
        "dp": (p["x"] // 2) * 16 + p["z"] * 4 + p["y"],
        "tensor": (p["x"] % 2) * 2 + p["c"],
    }


def moved(p, axis, by):
    size = 2 if axis == "c" else 4
    q = dict(p)
    q[axis] = (p[axis] + by) % size
    return q


def diagonal(p):
    q = moved(p, "c", 1)
    q["x"] = (p["x"] // 2) * 2 + (1 - p["x"] % 2)
    return q


def peers_of(p):
    found = [
        moved(p, axis, by)
        for axis, by in (
            ("x", 1), ("x", 2), ("x", 3), ("y", 1), ("y", 2), ("y", 3), ("z", 1), ("z", 2), ("z", 3), ("c", 1)
        )
    ]
    return found + [diagonal(p)]


def say_here(p, t):
    barrier = pltpu.get_barrier_semaphore()
    for q in peers_of(p):
        pl.semaphore_signal(barrier, inc=1, device_id=device_of(q), device_id_type=MESH)
    for y in range(4):
        @pl.when((t != p["y"]) | (y != p["y"]))
        def _(y=y):
            there = {"dp": lax.axis_index("dp") - p["y"] + y, "tensor": p["y"]}
            pl.semaphore_signal(barrier, inc=1, device_id=there, device_id_type=MESH)


def all_here(p, t):
    barrier = pltpu.get_barrier_semaphore()
    pl.semaphore_wait(barrier, len(peers_of(p)) + jnp.where(t == p["y"], 3, 4))


def send(src, dst, send_sem, recv_sem, q):
    copy = pltpu.make_async_remote_copy(
        src_ref=src,
        dst_ref=dst,
        send_sem=send_sem,
        recv_sem=recv_sem,
        device_id=device_of(q),
        device_id_type=MESH,
    )
    copy.start()
    return copy


def block_of(ref, at, first, rows, core=None):
    every = slice(None)
    where = (at["x"] % 2,) + (() if core is None else (core,)) + (at["y"], at["x"] // 2, at["z"], pl.ds(first, rows), every)
    return ref.at[where]


def unit_of(ref, at, axis, first, rows, core=None):
    every = slice(None)
    x_lo, x_hi = (every, every) if axis == "x" else (at["x"] % 2, at["x"] // 2)
    y = every if axis == "y" else at["y"]
    z = every if axis == "z" else at["z"]
    where = (x_lo,) + (() if core is None else (core,)) + (y, x_hi, z, pl.ds(first, rows), every)
    return ref.at[where]


def unit_shape(axis, rows):
    return ((2, 2) if axis == "x" else (4,)) + (rows, 128)


AWAY = (0, 1, 2, 1)
OFFSETS = [(j, k) for j in range(4) for k in range(4)]


def depth(offset):
    return AWAY[offset[0]] + AWAY[offset[1]]


def way_two(lane):
    return 1 if lane % 2 == 0 else 3


def way_three(lane, j):
    return 1 if j % 2 == 0 and lane % 3 != 1 else 3


def onward(lane, offset):
    j, k = offset
    to = []
    if k == 0:
        to += [(2, 1), (2, 3)]
        if j == 0:
            to += [(1, 1), (1, 3)]
        elif j == way_two(lane):
            to += [(1, j)]
    elif k == way_three(lane, j):
        to += [(2, k)]
    return to


def after(offset, axis_number, by):
    j, k = offset
    return ((j + by) % 4, k) if axis_number == 1 else (j, (k + by) % 4)


def source(p, order, offset):
    return moved(moved(p, order[1], 4 - offset[0]), order[2], 4 - offset[1])


def wait_bytes(ref, sem):
    pltpu.make_async_copy(ref, ref, sem).wait()


def gather_steps(lanes, w_ref, p, sems, shares):
    line_send, line_recv, unit_send, unit_recv, sib_send, sib_recv = sems
    core = p["c"]
    sibling = moved(p, "c", 1)
    sent = []
    lines = []
    for lane, at, rows, order in lanes:
        mine = block_of(w_ref, p, at, rows, core)
        for by in (1, 3, 2):
            q = moved(p, order[0], by)
            lines.append(send(mine, mine, line_send.at[lane, by - 1], line_recv.at[lane, by - 1], q))
    yield

    def pass_on(lane, at, rows, order, offset):
        unit = unit_of(w_ref, source(p, order, offset), order[0], at, rows, core)
        for number, by in onward(lane, offset):
            j, k = after(offset, number, by)
            sem = lane, j * 4 + k
            sent.append(send(unit, unit, unit_send.at[sem], unit_recv.at[sem], moved(p, order[number], by)))
        j, k = offset
        sem = lane, j * 4 + k
        shares.append(send(unit, unit, sib_send.at[sem], sib_recv.at[sem], sibling))

    for i, (lane, at, rows, order) in enumerate(lanes):
        for copy in lines[3 * i : 3 * i + 3]:
            copy.wait_recv()
        pass_on(lane, at, rows, order, (0, 0))
    yield
    for far in (1, 2, 3, 4):
        for lane, at, rows, order in lanes:
            for offset in OFFSETS:
                if depth(offset) == far:
                    j, k = offset
                    unit = unit_of(w_ref, source(p, order, offset), order[0], at, rows, core)
                    pltpu.make_async_remote_copy(
                        src_ref=unit, dst_ref=unit,
                        send_sem=unit_send.at[lane, j * 4 + k], recv_sem=unit_recv.at[lane, j * 4 + k],
                        device_id=device_of(sibling), device_id_type=MESH,
                    ).wait_recv()
                    pass_on(lane, at, rows, order, offset)
        yield
    for copy in shares:
        copy.wait_recv()
    for copy in lines + sent + shares:
        copy.wait_send()
    yield


def add_unit(acc, p, at, axis, first, rows, terms):
    def step(i, _):
        q = dict(at)
        q[axis] = i
        target = (q["x"] % 2, p["c"], q["y"], q["x"] // 2, q["z"], pl.ds(first, rows), slice(None))
        where = (i % 2, i // 2) if axis == "x" else (i,)
        total = acc[target]
        for term in terms:
            total = total + term[where]
        acc[target] = total
        return 0

    lax.fori_loop(0, 4, step, 0, unroll=True)


def reduce_steps(lanes, g_ref, other, bufs, line_bufs, p, sems):
    line_send, line_recv, unit_send, unit_recv, sib_send, sib_recv = sems
    core = p["c"]
    sibling = moved(p, "c", 1)
    halves, sent = {}, {}
    for far in (4, 3, 2, 1, 0):
        for lane, at, rows, order in lanes:
            for offset in OFFSETS:
                if depth(offset) == far:
                    where = source(p, order, offset)
                    src = unit_of(g_ref, where, order[0], at, rows, sibling["c"])
                    dst = unit_of(other, where, order[0], at, rows)
                    sem = lane, offset[0] * 4 + offset[1]
                    halves[lane, offset] = send(src, dst, sib_send.at[sem], sib_recv.at[sem], sibling)
    yield

    def add(lane, at, rows, order, offset):
        halves[lane, offset].wait_recv()
        where = source(p, order, offset)
        terms = [unit_of(other, where, order[0], at, rows)]
        for number, by in onward(lane, offset):
            child = after(offset, number, by)
            sent[lane, child].wait_recv()
            terms.append(bufs[lane].at[child[0] * 4 + child[1] - 1])
        add_unit(g_ref, p, where, order[0], at, rows, terms)

    def back(lane, at, rows, order, offset):
        for parent in OFFSETS:
            for number, by in onward(lane, parent):
                if after(parent, number, by) == offset:
                    j, k = offset
                    sem = lane, j * 4 + k
                    unit = unit_of(g_ref, source(p, order, offset), order[0], at, rows, core)
                    sent[lane, offset] = send(
                        unit, bufs[lane].at[j * 4 + k - 1], unit_send.at[sem], unit_recv.at[sem],
                        moved(p, order[number], 4 - by),
                    )

    for far in (4, 3, 2, 1):
        for lane, at, rows, order in lanes:
            for offset in OFFSETS:
                if depth(offset) == far:
                    add(lane, at, rows, order, offset)
                    back(lane, at, rows, order, offset)
        yield
    lines = []
    for lane, at, rows, order in lanes:
        add(lane, at, rows, order, (0, 0))
        for by in (1, 3, 2):
            q = moved(p, order[0], by)
            src = block_of(g_ref, q, at, rows, core)
            lines.append(
                send(src, line_bufs[lane].at[by - 1], line_send.at[lane, by - 1], line_recv.at[lane, by - 1], q)
            )
    yield
    for i, (lane, at, rows, order) in enumerate(lanes):
        for copy in lines[3 * i : 3 * i + 3]:
            copy.wait_recv()
        target = (p["x"] % 2, core, p["y"], p["x"] // 2, p["z"], pl.ds(at, rows), slice(None))
        total = g_ref[target].astype(f32)
        for by in range(3):
            total = total + line_bufs[lane][by].astype(f32)
        g_ref[target] = total.astype(bf16)
    for copy in lines + list(sent.values()) + list(halves.values()):
        copy.wait_send()
    yield


def dot(a, b):
    return jnp.dot(a, b, preferred_element_type=f32)


def dot_nt(a, b):
    return lax.dot_general(a, b, (((1,), (1,)), ((), ())), preferred_element_type=f32)


def inv_rms(v):
    return lax.rsqrt(jnp.mean(v * v, axis=-1, keepdims=True) + norm_eps)


def norm_back(v, r, c, e):
    ec = e * c
    vr = v * r
    dv = r * (ec - vr * jnp.mean(vr * ec, axis=-1, keepdims=True))
    return dv, jnp.sum(e * vr, axis=0, keepdims=True)


def turn(u, cos, sin):
    a, b = u[:, :128], u[:, 128:]
    return jnp.concatenate([a * cos - b * sin, b * cos + a * sin], axis=1)


def turn_back(e, cos, sin):
    a, b = e[:, :128], e[:, 128:]
    return jnp.concatenate([a * cos + b * sin, b * cos - a * sin], axis=1)


def columns(w_ref, t, y, first):
    return jnp.concatenate(
        [w_ref[t // 2, t % 2, y + i, :, :, first : first + 80, :].reshape(D, 128) for i in range(2)], axis=1
    )


def put_columns(g_ref, t, y, first, value):
    value = value.astype(bf16)
    for i in range(2):
        g_ref[t // 2, t % 2, y + i, :, :, first : first + 80, :] = (
            value[:, 128 * i : 128 * i + 128].reshape(2, 4, 80, 128)
        )


NB = len(LANES)


def kernel(
    seg_ref, wq_ref, wkv_ref, wo_ref, wg_ref, wu_ref, wd_ref, x_ref, cot_ref,
    gin_ref, gpa_ref, gpf_ref, gpo_ref, gq_ref, gk_ref, cos_tab, sin_tab, freq_ref,
    out_ref, gx_ref, shard_ref, kv_ref, gn_out,
    *scratch,
):
    bufs, line_bufs, scratch = scratch[:NB], scratch[NB : 2 * NB], scratch[2 * NB :]
    (
        w_ref, g_ref, other, xg, rows_s, s_ref, got, stage,
        cos_ref, sin_ref, wkv, attn_in, attn_in_t, kt, vt, kb, vb, qraw, qb, probs, ctx,
        mlp_in, mlp_in_t, d_b, d_t, act_s, dact_s, hid_s, acc, acc2, dkt, dvt, proj_s,
        dx_got, gn_now, gn_got, final,
        one_send, one_recv, line_send, line_recv, unit_send, unit_recv, sib_send, sib_recv, x_send, x_recv,
        bline_send, bline_recv, back_send, back_recv, bsib_send, bsib_recv, last_send, last_recv, kv_send, kv_recv,
        dx_send, dx_recv, gn_send, gn_recv,
    ) = scratch
    p = place()
    t = lax.axis_index("tensor")
    dp = lax.axis_index("dp")
    y = p["y"]
    core = p["c"]
    own = (p["x"] % 2, core, y, p["x"] // 2, p["z"])
    say_here(p, t)

    rows_s[...] = jnp.zeros_like(rows_s)
    for j in range(4):
        if j < 2:
            rows_s[j, :20, :128] = wq_ref[:, 128 * j : 128 * j + 128].astype(f32)
        else:
            rows_s[j, :20, :128] = wo_ref[:, 128 * j - 256 : 128 * j - 128].astype(f32)
        rows_s[j, :20, 128:256] = wg_ref[:, 128 * j : 128 * j + 128].astype(f32)
        rows_s[j, :20, 256:384] = wu_ref[:, 128 * j : 128 * j + 128].astype(f32)
        rows_s[j, :20, 384:512] = wd_ref[:, 128 * j : 128 * j + 128].astype(f32)
        rows_s[j, :20, 512:] = wkv_ref[:, 128 * j : 128 * j + 128].astype(f32)
    s_ref[...] = rows_s[...].astype(bf16)
    gin, gpa, gpf, gpo, gq, gk = (
        ref[...].reshape(1, ref.shape[0]) for ref in (gin_ref, gpa_ref, gpf_ref, gpo_ref, gq_ref, gk_ref)
    )
    scale = HD ** -0.5
    seg = seg_ref[...]
    n0 = jnp.sum(jnp.where(seg == 0, 1.0, 0.0), axis=1, keepdims=True)
    n1 = jnp.sum(jnp.where(seg <= 1, 1.0, 0.0), axis=1, keepdims=True)
    base = ((t - 2) * PART).astype(f32)
    which = lax.broadcasted_iota(jnp.int32, (8, 128), 0)
    turn_by = (jnp.where(which == 0, 0.0, jnp.where(which == 1, n0, n1)) - base) * freq_ref[...]
    cb, sb = jnp.cos(turn_by), jnp.sin(turn_by)
    token = lax.broadcasted_iota(jnp.int32, (KEYS, 1), 0).astype(f32) + base
    in0, in1 = token < n0, token < n1
    cd = jnp.where(in0, cb[0:1], jnp.where(in1, cb[1:2], cb[2:3]))
    sd = jnp.where(in0, sb[0:1], jnp.where(in1, sb[1:2], sb[2:3]))
    ca, sa = cos_tab[...], sin_tab[...]
    cos_ref[...] = ca * cd + sa * sd
    sin_ref[...] = sa * cd - ca * sd

    xg[2] = x_ref[...]
    got[pl.ds(y, 1)] = s_ref[pl.ds(y, 1)]
    all_here(p, t)
    first = []
    for k in (1, 3, 2):
        q = moved(p, "y", k)
        first.append(send(s_ref.at[q["y"]], got.at[y], one_send.at[k - 1], one_recv.at[k - 1], q))

    def token_copy(src, slot, to):
        return pltpu.make_async_remote_copy(
            src_ref=src, dst_ref=xg.at[slot], send_sem=x_send.at[1 - slot], recv_sem=x_recv.at[1 - slot],
            device_id={"dp": dp, "tensor": to}, device_id_type=MESH,
        )

    @pl.when(t < 3)
    def _():
        token_copy(x_ref, 1, jnp.minimum(t + 1, 3)).start()

    @pl.when(t == 0)
    def _():
        token_copy(x_ref, 0, t + 2).start()

    for copy in first:
        copy.wait_recv()
    for j in range(4):
        stage[20 * j : 20 * j + 20, :] = got[j].astype(f32)[:20, :512]
    for i, at in enumerate((0, G0, U0, D0)):
        w_ref[own + (slice(at, at + 80),)] = stage[:80, 128 * i : 128 * i + 128].astype(bf16)
    w_ref[own + (slice(KV0, KV0 + 32),)] = got[pl.ds(t, 1)][0, :, 512:640]
    for copy in first:
        copy.wait_send()

    sems = (line_send, line_recv, unit_send, unit_recv, sib_send, sib_recv)
    attn = gather_steps(ATTN, w_ref, p, sems, [])
    feed = gather_steps(FEED, w_ref, p, sems, [])
    next(attn)
    for _ in range(5):
        next(feed)
        next(attn)

    @pl.when(t > 0)
    def _():
        token_copy(x_ref, 1, jnp.minimum(t + 1, 3)).wait_recv()

    @pl.when(t == 2)
    def _():
        token_copy(xg.at[1], 0, jnp.minimum(t + 1, 3)).start()

    @pl.when(t >= 2)
    def _():
        token_copy(x_ref, 0, jnp.minimum(t + 1, 3)).wait_recv()

    @pl.when(t < 3)
    def _():
        token_copy(x_ref, 1, jnp.minimum(t + 1, 3)).wait_send()

    @pl.when(lax.rem(t, 2) == 0)
    def _():
        token_copy(x_ref, 0, jnp.minimum(t + 1, 3)).wait_send()

    def tokens(i):
        return jnp.where(i >= 2 - t, xg[i].astype(f32), 0.0)

    def input_norm(i, _):
        x = tokens(i)
        a = x * inv_rms(x) * gin
        attn_in[i] = a.astype(bf16)
        attn_in_t[i] = a.T.astype(bf16)
        return 0

    lax.fori_loop(0, 3, input_norm, 0)
    acc[...] = jnp.zeros_like(acc)
    next(attn)

    def keyval_in(g, _):
        for tt in range(4):
            for yy in range(4):
                stage[20 * tt : 20 * tt + 20, 128 * yy : 128 * yy + 128] = (
                    w_ref[tt // 2, tt % 2, yy, g // 4, g % 4, KV0 : KV0 + 32, :].astype(f32)[:20]
                )
        wkv[g] = stage[:80, :].astype(bf16)
        return 0

    lax.fori_loop(0, GROUPS, keyval_in, 0)

    def rows_of(i):
        return pl.ds(pl.multiple_of(i * PART, PART), PART)

    def keys_values(i, _):
        rows = rows_of(i)
        kv_raw = dot(attn_in[i], wkv[...].reshape(D, 512))
        kraw = kv_raw[:, :HD]
        k = turn(kraw * inv_rms(kraw) * gk, cos_ref[rows, :], sin_ref[rows, :])
        kb[rows, :] = k.astype(bf16)
        kt[:, rows] = k.T.astype(bf16)
        v = kv_raw[:, HD:]
        vb[rows, :] = v.astype(bf16)
        vt[:, rows] = v.T.astype(bf16)
        return 0

    lax.fori_loop(0, 3, keys_values, 0)
    next(feed)

    def head(h, _):
        cos_q, sin_q = cos_ref[2 * PART :, :], sin_ref[2 * PART :, :]
        column = lax.broadcasted_iota(jnp.int32, (PART, KEYS), 1)
        last = lax.broadcasted_iota(jnp.int32, (PART, 1), 0) + 2 * PART
        own_token = last.astype(f32) + base
        start = jnp.where(own_token < n0, 0.0, jnp.where(own_token < n1, n0, n1))
        low = jnp.maximum(own_token - (WINDOW - 1), start) - base
        raw = dot(attn_in[2], columns(w_ref, h, 0, 0))
        qraw[h] = raw
        q = turn(raw * inv_rms(raw) * gq, cos_q, sin_q).astype(bf16)
        qb[h] = q
        s = dot(q, kt[...]) * scale
        s = jnp.where((column.astype(f32) >= low) & (column <= last), s, -1e30)
        e = jnp.exp(s - jnp.max(s, axis=-1, keepdims=True))
        pr = e / jnp.sum(e, axis=-1, keepdims=True)
        probs[h] = pr
        c = dot(pr.astype(bf16), vb[...]).astype(bf16)
        ctx[h] = c
        acc[...] += dot_nt(c, columns(w_ref, h, 2, 0))
        return 0

    lax.fori_loop(0, 4, head, 0)
    proj = acc[...]
    proj_s[...] = proj
    mid = x_ref[...].astype(f32) + proj * inv_rms(proj) * gpa
    gx_ref[...] = mid
    m = mid * inv_rms(mid) * gpf
    mlp_in[...] = m.astype(bf16)
    mlp_in_t[...] = m.T.astype(bf16)
    acc[...] = jnp.zeros_like(acc)
    next(feed)

    def feed_forward(c, _):
        tt, yy = c // 2, 2 * (c % 2)
        gate = dot(mlp_in[...], columns(w_ref, tt, yy, G0))
        up = dot(mlp_in[...], columns(w_ref, tt, yy, U0))
        k0, k1 = 0.7978845608028654, 0.044715
        sq = gate * gate
        th = jnp.tanh(k0 * (gate + k1 * gate * sq))
        half = 0.5 * (1.0 + th)
        act = gate * half
        hid = (act * up).astype(bf16)
        act_s[c] = act
        dact_s[c] = up * (half + 0.5 * gate * (1.0 - th * th) * (k0 + (3.0 * k0 * k1) * sq))
        hid_s[c] = hid
        acc[...] += dot_nt(hid, columns(w_ref, tt, yy, D0))
        return 0

    lax.fori_loop(0, 8, feed_forward, 0)
    mlp = acc[...]
    r = inv_rms(mlp)
    out_ref[...] = (gx_ref[...] + mlp * r * gpo).astype(bf16)
    d_mlp, g_po = norm_back(mlp, r, gpo, cot_ref[...].astype(f32))
    gn_now[0, 3:4, :] = g_po
    d_b[...] = d_mlp.astype(bf16)
    d_t[...] = d_mlp.T.astype(bf16)
    acc[...] = jnp.zeros_like(acc)

    def feed_back(c, _):
        tt, yy = c // 2, 2 * (c % 2)
        put_columns(g_ref, tt, yy, D0, dot(d_t[...], hid_s[c]))
        d_hid = dot(d_b[...], columns(w_ref, tt, yy, D0))
        d_gate = (d_hid * dact_s[c]).astype(bf16)
        d_up = (d_hid * act_s[c]).astype(bf16)
        put_columns(g_ref, tt, yy, G0, dot(mlp_in_t[...], d_gate))
        put_columns(g_ref, tt, yy, U0, dot(mlp_in_t[...], d_up))
        acc[...] += dot_nt(d_gate, columns(w_ref, tt, yy, G0)) + dot_nt(d_up, columns(w_ref, tt, yy, U0))
        return 0

    lax.fori_loop(0, 8, feed_back, 0)
    sems = (bline_send, bline_recv, back_send, back_recv, bsib_send, bsib_recv)
    feed = reduce_steps(FEED, g_ref, other, bufs, line_bufs, p, sems)
    next(feed)

    mid = gx_ref[...]
    d_pre, g_pf = norm_back(mid, inv_rms(mid), gpf, acc[...])
    gn_now[0, 2:3, :] = g_pf
    d_mid = cot_ref[...].astype(f32) + d_pre
    proj = proj_s[...]
    d_proj, g_pa = norm_back(proj, inv_rms(proj), gpa, d_mid)
    gn_now[0, 1:2, :] = g_pa
    gx_ref[...] = d_mid
    d_b[...] = d_proj.astype(bf16)
    d_t[...] = d_proj.T.astype(bf16)
    dkt[...] = jnp.zeros_like(dkt)
    dvt[...] = jnp.zeros_like(dvt)
    acc[...] = jnp.zeros_like(acc)
    acc2[...] = jnp.zeros_like(acc2)
    next(feed)

    def head_back(h, _):
        cos_q, sin_q = cos_ref[2 * PART :, :], sin_ref[2 * PART :, :]
        put_columns(g_ref, h, 2, 0, dot(d_t[...], ctx[h]))
        d_ctx = dot(d_b[...], columns(w_ref, h, 2, 0))
        d_ctx_b = d_ctx.astype(bf16)
        pr = probs[h]
        d_pr = dot(d_ctx_b, vt[...])
        dvt[...] += dot(d_ctx.T.astype(bf16), pr.astype(bf16))
        inner = jnp.sum(pr * d_pr, axis=-1, keepdims=True)
        ds = (pr * (d_pr - inner)).astype(bf16)
        dq = dot(ds, kb[...]) * scale
        dkt[...] += dot(qb[h].astype(f32).T.astype(bf16), ds)
        raw = qraw[h]
        d_raw, g_q = norm_back(raw, inv_rms(raw), gq, turn_back(dq, cos_q, sin_q))
        acc2[...] += g_q
        d_raw = d_raw.astype(bf16)
        put_columns(g_ref, h, 0, 0, dot(attn_in_t[2], d_raw))
        acc[...] += dot_nt(d_raw, columns(w_ref, h, 0, 0))
        return 0

    lax.fori_loop(0, 2, head_back, 0)
    next(feed)
    lax.fori_loop(2, 4, head_back, 0)
    gn_now[0, 4:8, :] = jnp.zeros((4, D), f32)
    gn_now[0, 4:5, :HD] = acc2[...]
    acc2[...] = jnp.zeros_like(acc2)

    def keys_values_back(i, _):
        rows = rows_of(i)
        raw = dot(attn_in[i], wkv[:, :, :HD].reshape(D, HD))
        e = turn_back(dkt[:, rows].T * scale, cos_ref[rows, :], sin_ref[rows, :])
        dk, g_k = norm_back(raw, inv_rms(raw), gk, e)
        acc2[...] += g_k
        kb[rows, :] = dk.astype(bf16)
        vb[rows, :] = dvt[:, rows].T.astype(bf16)
        return 0

    lax.fori_loop(0, 3, keys_values_back, 0)
    gn_now[0, 5:6, :HD] = acc2[...]
    for half, src in enumerate((kb, vb)):
        grad = sum(dot(attn_in_t[i], src[PART * i : PART * i + PART, :]) for i in range(3))
        stage[80:, :] = jnp.zeros((16, 512), f32)
        for g in range(GROUPS):
            stage[:80, :HD] = grad[80 * g : 80 * g + 80]
            for tt in range(4):
                for yy in range(2):
                    g_ref[tt // 2, tt % 2, 2 * half + yy, g // 4, g % 4, KV0 : KV0 + 32, :] = (
                        stage[20 * tt : 20 * tt + 32, 128 * yy : 128 * yy + 128].astype(bf16)
                    )
    attn = reduce_steps(ATTN, g_ref, other, bufs, line_bufs, p, sems)
    next(attn)
    next(feed)

    def input_back(i, extra):
        rows = rows_of(i)
        d_in = dot_nt(kb[rows, :], wkv[:, :, :HD].reshape(D, HD)) + dot_nt(vb[rows, :], wkv[:, :, HD:].reshape(D, HD))
        x = tokens(i)
        dx, g_in = norm_back(x, inv_rms(x), gin, d_in if extra is None else d_in + extra)
        gn_now[0, 0:1, :] += g_in
        return dx

    def input_back_before(i, _):
        attn_in[i] = input_back(i, None).astype(bf16)
        return 0

    gn_now[0, 0:1, :] = jnp.zeros((1, D), f32)
    lax.fori_loop(0, 2, input_back_before, 0)
    gx_ref[...] += input_back(2, acc[...])

    def dx_copy(k):
        to = jnp.maximum(t - 1, 0) if k == 1 else jnp.where(t == 3, 2, 0)
        return pltpu.make_async_remote_copy(
            src_ref=attn_in.at[2 - k], dst_ref=dx_got.at[k - 1], send_sem=dx_send.at[k - 1], recv_sem=dx_recv.at[k - 1],
            device_id={"dp": dp, "tensor": to}, device_id_type=MESH,
        )

    @pl.when(t >= 2)
    def _():
        dx_copy(2).start()

    @pl.when(lax.rem(t, 2) == 1)
    def _():
        dx_copy(1).start()

    def pair(i):
        if i == 6:
            return moved(p, "c", 1)
        axis = "xyz"[i // 2]
        m = p[axis]
        q = dict(p)
        q[axis] = (m // 2) * 2 + (1 - m % 2) if i % 2 == 0 else 3 - m
        return q

    gn_copies = []

    def gn_start(i):
        gn_copies.append(send(gn_now.at[i], gn_got.at[i], gn_send.at[i], gn_recv.at[i], pair(i)))

    def gn_add(i):
        gn_copies[i].wait_recv()
        gn_now[i + 1] = gn_now[i] + gn_got[i]

    gn_start(0)
    for i in range(6):
        next(attn)
        if i == 0:
            @pl.when(t == 2)
            def _():
                dx_copy(2).wait_recv()
                attn_in[1] = (attn_in[1].astype(f32) + dx_got[1].astype(f32)).astype(bf16)
                dx_copy(1).start()

        if i < 3:
            next(feed)
        gn_add(i)
        gn_start(i + 1)

    mine = g_ref[own].astype(f32)
    for i, at in enumerate((0, G0, U0, D0)):
        for j in range(4):
            rows_s[j, 0:20, 128 * i : 128 * i + 128] = mine[at + 20 * j : at + 20 * j + 20]
    for j in range(4):
        rows_s[j, :24, 512:] = mine[KV0 : KV0 + 24]

    @pl.when(t == y)
    def _():
        kv_ref[pl.ds(y, 1)] = mine[KV0 : KV0 + 24][None]


    def kv_copy(k):
        return pltpu.make_async_remote_copy(
            src_ref=rows_s.at[0, pl.ds(0, 24), pl.ds(512, 128)], dst_ref=kv_ref.at[y],
            send_sem=kv_send.at[k], recv_sem=kv_recv.at[y],
            device_id={"dp": dp - y + t, "tensor": (t + k) % 4}, device_id_type=MESH,
        )

    @pl.when(t != y)
    def _():
        kv_copy(0).start()

    for k in (1, 2, 3):
        kv_copy(k).start()
    last = []
    for k in (1, 3, 2):
        q = moved(p, "y", k)
        last.append(send(rows_s.at[q["y"], pl.ds(0, 24), :], final.at[y], last_send.at[k - 1], last_recv.at[k - 1], q))
    final[pl.ds(y, 1)] = rows_s[pl.ds(y, 1), :24]
    gn_add(6)
    gn_out[...] = gn_now[7]

    @pl.when(t < 3)
    def _():
        dx_copy(1).wait_recv()
        gx_ref[...] += dx_got[0].astype(f32)

    @pl.when(t == 0)
    def _():
        dx_copy(2).wait_recv()
        gx_ref[...] += dx_got[1].astype(f32)

    @pl.when(t >= 1)
    def _():
        dx_copy(1).wait_send()

    @pl.when(t >= 2)
    def _():
        dx_copy(2).wait_send()

    for copy in last:
        copy.wait_recv()

    shard_ref[...] = final[:, :, :512]
    for copy in gn_copies + last:
        copy.wait_send()

    for k in (1, 2, 3):
        kv_copy(k).wait_send()

    @pl.when(t != y)
    def _():
        kv_copy(0).wait_send()

    for j in range(4):
        @pl.when((t != y) | (y != j))
        def _(j=j):
            pltpu.make_async_remote_copy(
                src_ref=kv_ref.at[j], dst_ref=kv_ref.at[j], send_sem=kv_send.at[0], recv_sem=kv_recv.at[j],
                device_id={"dp": dp, "tensor": (t + 1) % 4}, device_id_type=MESH,
            ).wait_recv()


def layer(*args):
    dma = pltpu.SemaphoreType.DMA
    vmem = pl.BlockSpec(memory_space=pltpu.VMEM)
    bufs = [pltpu.VMEM((15,) + unit_shape(order[0], rows), bf16) for _, _, rows, order in LANES]
    bufs += [pltpu.VMEM((3, rows, 128), bf16) for _, _, rows, _ in LANES]
    n = len(LANES)
    return pl.pallas_call(
        kernel,
        out_shape=(
            jax.ShapeDtypeStruct((PART, D), bf16),
            jax.ShapeDtypeStruct((PART, D), f32),
            jax.ShapeDtypeStruct((4, 24, 512), f32),
            jax.ShapeDtypeStruct((4, 24, 128), f32),
            jax.ShapeDtypeStruct((8, D), f32),
        ),
        in_specs=[vmem] * len(args),
        out_specs=(vmem,) * 5,
        scratch_shapes=[
            *bufs,
            pltpu.VMEM((2, 2, 4, 2, 4, BLOCK, 128), bf16),
            pltpu.VMEM((2, 2, 4, 2, 4, BLOCK, 128), bf16),
            pltpu.VMEM((2, 4, 2, 4, BLOCK, 128), bf16),
            pltpu.VMEM((3, PART, D), bf16),
            pltpu.VMEM((4, 32, D), f32),
            pltpu.VMEM((4, 32, D), bf16),
            pltpu.VMEM((4, 32, D), bf16),
            pltpu.VMEM((96, 512), f32),
            pltpu.VMEM((KEYS, 128), f32),
            pltpu.VMEM((KEYS, 128), f32),
            pltpu.VMEM((GROUPS, 80, 512), bf16),
            pltpu.VMEM((3, PART, D), bf16),
            pltpu.VMEM((3, D, PART), bf16),
            pltpu.VMEM((HD, KEYS), bf16),
            pltpu.VMEM((HD, KEYS), bf16),
            pltpu.VMEM((KEYS, HD), bf16),
            pltpu.VMEM((KEYS, HD), bf16),
            pltpu.VMEM((4, PART, HD), f32),
            pltpu.VMEM((4, PART, HD), bf16),
            pltpu.VMEM((4, PART, KEYS), f32),
            pltpu.VMEM((4, PART, HD), bf16),
            pltpu.VMEM((PART, D), bf16),
            pltpu.VMEM((D, PART), bf16),
            pltpu.VMEM((PART, D), bf16),
            pltpu.VMEM((D, PART), bf16),
            pltpu.VMEM((8, PART, 256), f32),
            pltpu.VMEM((8, PART, 256), f32),
            pltpu.VMEM((8, PART, 256), bf16),
            pltpu.VMEM((PART, D), f32),
            pltpu.VMEM((1, HD), f32),
            pltpu.VMEM((HD, KEYS), f32),
            pltpu.VMEM((HD, KEYS), f32),
            pltpu.VMEM((PART, D), f32),
            pltpu.VMEM((2, PART, D), bf16),
            pltpu.VMEM((8, 8, D), f32),
            pltpu.VMEM((7, 8, D), f32),
            pltpu.VMEM((4, 24, D), f32),
            dma((3,)), dma((3,)), dma((n, 3)), dma((n, 3)), dma((n, 16)), dma((n, 16)), dma((n, 16)), dma((n, 16)),
            dma((2,)), dma((2,)),
            dma((n, 3)), dma((n, 3)), dma((n, 16)), dma((n, 16)), dma((n, 16)), dma((n, 16)),
            dma((3,)), dma((3,)), dma((4,)), dma((4,)),
            dma((2,)), dma((2,)), dma((7,)), dma((7,)),
        ],
        compiler_params=pltpu.CompilerParams(
            collective_id=0, has_side_effects=True, vmem_limit_bytes=62 << 20
        ),
        name="layer",
    )(*args)


def finish_kernel(
    out_ref, gx_ref, shard_ref, kv_ref, gn_ref,
    out_to, gx_to, query_to, keyval_to, out_t_to, gate_to, up_to, down_t_to, *gains_to,
):
    out_to[...] = out_ref[...]
    gx_to[...] = gx_ref[...]
    for j in range(4):
        here = slice(128 * j, 128 * j + 128)
        if j < 2:
            query_to[:, here] = shard_ref[j, :20, :128]
        else:
            out_t_to[:, 128 * j - 256 : 128 * j - 128] = shard_ref[j, :20, :128]
        gate_to[:, here] = shard_ref[j, :20, 128:256]
        up_to[:, here] = shard_ref[j, :20, 256:384]
        down_t_to[:, here] = shard_ref[j, :20, 384:512]
        keyval_to[:, here] = kv_ref[j, :20, :]
    for i, ref in enumerate(gains_to):
        ref[...] = gn_ref[i : i + 1, : ref.shape[0]].reshape(ref.shape[0])


def finish(*args):
    vmem = pl.BlockSpec(memory_space=pltpu.VMEM)
    shapes = [((PART, D), bf16), ((PART, D), f32)]
    shapes += [((20, n), f32) for n in (256, 512, 256, 512, 512, 512)]
    shapes += [((n,), f32) for n in (D, D, D, D, HD, HD)]
    return pl.pallas_call(
        finish_kernel,
        out_shape=tuple(jax.ShapeDtypeStruct(*item) for item in shapes),
        in_specs=[vmem] * len(args),
        out_specs=(vmem,) * len(shapes),
        name="finish",
    )(*args)


def rope_parts():
    freq = (rope_base ** (-np.arange(0, HD, 2, dtype=np.float64) / HD))[None, :]
    angles = np.arange(KEYS, dtype=np.float64)[:, None] * freq
    return tuple(jnp.asarray(item.astype(np.float32)) for item in (np.cos(angles), np.sin(angles), freq))


def per_device(
    tokens, segments, cotangent, w_query, w_keyval, w_out, w_gate, w_up, w_down,
    gain_in, gain_post_attn, gain_pre_ff, gain_post_ff, gain_query, gain_key,
):
    made = layer(
        segments, w_query, w_keyval, w_out.T, w_gate, w_up, w_down.T, tokens, cotangent,
        gain_in, gain_post_attn, gain_pre_ff, gain_post_ff, gain_query, gain_key, *rope_parts(),
    )
    output, grad_x, query, keyval, out_t, gate, up, down_t, *gains = finish(*made)
    return (output, grad_x, query, keyval, out_t.T, gate, up, down_t.T, *gains)


def solution(mesh):
    tok = P(("dp", "tensor"), None)
    weights = (
        P("dp", "tensor"), P("dp", None), P("tensor", "dp"), P("dp", "tensor"), P("dp", "tensor"), P("tensor", "dp"),
    )
    return jax.shard_map(
        per_device,
        mesh=mesh,
        in_specs=(tok, P("dp", None), tok) + weights + (P(),) * 6,
        out_specs=(tok, tok) + weights + (P(),) * 6,
        check_vma=False,
    )
```

```python
import jax
import jax.numpy as jnp
import numpy as np
from jax import lax
from jax.experimental import pallas as pl
from jax.experimental.pallas import tpu as pltpu
from jax.sharding import PartitionSpec as P

HD = 256
WINDOW = 512
D = 640
PART = 256
KEYS = 768
BLOCK = 352
CB = 16
GROUPS = 8
KV0, G0, U0, D0 = 80, 112, 192, 272
ATTN = ((0, 0, 48, "xyz"), (1, 48, 32, "yzx"), (2, 80, 32, "zxy"))
FEED = ((3, 112, 80, "xyz"), (4, 192, 64, "yzx"), (5, 256, 96, "zxy"))
LANES = ATTN + FEED
norm_eps = 1e-06
rope_base = 10000.0
MESH = pl.DeviceIdType.MESH
f32 = jnp.float32
bf16 = jnp.bfloat16


def place():
    dp = lax.axis_index("dp")
    t = lax.axis_index("tensor")
    return {
        "x": (dp // 16) * 2 + t // 2,
        "y": dp % 4,
        "z": (dp // 4) % 4,
        "c": t % 2,
    }


def device_of(p):
    return {
        "dp": (p["x"] // 2) * 16 + p["z"] * 4 + p["y"],
        "tensor": (p["x"] % 2) * 2 + p["c"],
    }


def moved(p, axis, by):
    size = 2 if axis == "c" else 4
    q = dict(p)
    q[axis] = (p[axis] + by) % size
    return q


def diagonal(p):
    q = moved(p, "c", 1)
    q["x"] = (p["x"] // 2) * 2 + (1 - p["x"] % 2)
    return q


def peers_of(p):
    found = [
        moved(p, axis, by)
        for axis, by in (
            ("x", 1), ("x", 2), ("x", 3), ("y", 1), ("y", 2), ("y", 3), ("z", 1), ("z", 2), ("z", 3), ("c", 1)
        )
    ]
    return found + [diagonal(p)]


def say_here(p, t):
    barrier = pltpu.get_barrier_semaphore()
    for q in peers_of(p):
        pl.semaphore_signal(barrier, inc=1, device_id=device_of(q), device_id_type=MESH)
    for y in range(4):
        @pl.when((t != p["y"]) | (y != p["y"]))
        def _(y=y):
            there = {"dp": lax.axis_index("dp") - p["y"] + y, "tensor": p["y"]}
            pl.semaphore_signal(barrier, inc=1, device_id=there, device_id_type=MESH)


def all_here(p, t):
    barrier = pltpu.get_barrier_semaphore()
    pl.semaphore_wait(barrier, len(peers_of(p)) + jnp.where(t == p["y"], 3, 4))


def send(src, dst, send_sem, recv_sem, q):
    copy = pltpu.make_async_remote_copy(
        src_ref=src,
        dst_ref=dst,
        send_sem=send_sem,
        recv_sem=recv_sem,
        device_id=device_of(q),
        device_id_type=MESH,
    )
    copy.start()
    return copy


def block_of(ref, at, first, rows, core=None):
    every = slice(None)
    where = (at["x"] % 2,) + (() if core is None else (core,)) + (at["y"], at["x"] // 2, at["z"], pl.ds(first, rows), every)
    return ref.at[where]


def unit_of(ref, at, axis, first, rows, core=None):
    every = slice(None)
    x_lo, x_hi = (every, every) if axis == "x" else (at["x"] % 2, at["x"] // 2)
    y = every if axis == "y" else at["y"]
    z = every if axis == "z" else at["z"]
    where = (x_lo,) + (() if core is None else (core,)) + (y, x_hi, z, pl.ds(first, rows), every)
    return ref.at[where]


def unit_shape(axis, rows):
    return ((2, 2) if axis == "x" else (4,)) + (rows, 128)


AWAY = (0, 1, 2, 1)
OFFSETS = [(j, k) for j in range(4) for k in range(4)]


def depth(offset):
    return AWAY[offset[0]] + AWAY[offset[1]]


def way_two(lane):
    return 1 if lane % 2 == 0 else 3


def way_three(lane, j):
    return 1 if j % 2 == 0 and lane % 3 != 1 else 3


def onward(lane, offset):
    j, k = offset
    to = []
    if k == 0:
        to += [(2, 1), (2, 3)]
        if j == 0:
            to += [(1, 1), (1, 3)]
        elif j == way_two(lane):
            to += [(1, j)]
    elif k == way_three(lane, j):
        to += [(2, k)]
    return to


def after(offset, axis_number, by):
    j, k = offset
    return ((j + by) % 4, k) if axis_number == 1 else (j, (k + by) % 4)


def source(p, order, offset):
    return moved(moved(p, order[1], 4 - offset[0]), order[2], 4 - offset[1])


def wait_bytes(ref, sem):
    pltpu.make_async_copy(ref, ref, sem).wait()


def gather_steps(lanes, w_ref, p, sems, shares):
    line_send, line_recv, unit_send, unit_recv, sib_send, sib_recv = sems
    core = p["c"]
    sibling = moved(p, "c", 1)
    sent = []
    lines = []
    for lane, at, rows, order in lanes:
        mine = block_of(w_ref, p, at, rows, core)
        for by in (1, 3, 2):
            q = moved(p, order[0], by)
            lines.append(send(mine, mine, line_send.at[lane, by - 1], line_recv.at[lane, by - 1], q))
    yield

    def pass_on(lane, at, rows, order, offset):
        unit = unit_of(w_ref, source(p, order, offset), order[0], at, rows, core)
        for number, by in onward(lane, offset):
            j, k = after(offset, number, by)
            sem = lane, j * 4 + k
            sent.append(send(unit, unit, unit_send.at[sem], unit_recv.at[sem], moved(p, order[number], by)))
        j, k = offset
        sem = lane, j * 4 + k
        shares.append(send(unit, unit, sib_send.at[sem], sib_recv.at[sem], sibling))

    for i, (lane, at, rows, order) in enumerate(lanes):
        for copy in lines[3 * i : 3 * i + 3]:
            copy.wait_recv()
        pass_on(lane, at, rows, order, (0, 0))
    yield
    for far in (1, 2, 3, 4):
        for lane, at, rows, order in lanes:
            for offset in OFFSETS:
                if depth(offset) == far:
                    j, k = offset
                    unit = unit_of(w_ref, source(p, order, offset), order[0], at, rows, core)
                    pltpu.make_async_remote_copy(
                        src_ref=unit, dst_ref=unit,
                        send_sem=unit_send.at[lane, j * 4 + k], recv_sem=unit_recv.at[lane, j * 4 + k],
                        device_id=device_of(sibling), device_id_type=MESH,
                    ).wait_recv()
                    pass_on(lane, at, rows, order, offset)
        yield
    for copy in shares:
        copy.wait_recv()
    for copy in lines + sent + shares:
        copy.wait_send()
    yield


def add_unit(acc, p, at, axis, first, rows, terms):
    def step(i, _):
        q = dict(at)
        q[axis] = i
        target = (q["x"] % 2, p["c"], q["y"], q["x"] // 2, q["z"], pl.ds(first, rows), slice(None))
        where = (i % 2, i // 2) if axis == "x" else (i,)
        total = acc[target]
        for term in terms:
            total = total + term[where]
        acc[target] = total
        return 0

    lax.fori_loop(0, 4, step, 0, unroll=True)


def reduce_steps(lanes, g_ref, other, bufs, line_bufs, p, sems):
    line_send, line_recv, unit_send, unit_recv, sib_send, sib_recv = sems
    core = p["c"]
    sibling = moved(p, "c", 1)
    halves, sent = {}, {}
    for far in (4, 3, 2, 1, 0):
        for lane, at, rows, order in lanes:
            for offset in OFFSETS:
                if depth(offset) == far:
                    where = source(p, order, offset)
                    src = unit_of(g_ref, where, order[0], at, rows, sibling["c"])
                    dst = unit_of(other, where, order[0], at, rows)
                    sem = lane, offset[0] * 4 + offset[1]
                    halves[lane, offset] = send(src, dst, sib_send.at[sem], sib_recv.at[sem], sibling)
    yield

    def add(lane, at, rows, order, offset):
        halves[lane, offset].wait_recv()
        where = source(p, order, offset)
        terms = [unit_of(other, where, order[0], at, rows)]
        for number, by in onward(lane, offset):
            child = after(offset, number, by)
            sent[lane, child].wait_recv()
            terms.append(bufs[lane].at[child[0] * 4 + child[1] - 1])
        add_unit(g_ref, p, where, order[0], at, rows, terms)

    def back(lane, at, rows, order, offset):
        for parent in OFFSETS:
            for number, by in onward(lane, parent):
                if after(parent, number, by) == offset:
                    j, k = offset
                    sem = lane, j * 4 + k
                    unit = unit_of(g_ref, source(p, order, offset), order[0], at, rows, core)
                    sent[lane, offset] = send(
                        unit, bufs[lane].at[j * 4 + k - 1], unit_send.at[sem], unit_recv.at[sem],
                        moved(p, order[number], 4 - by),
                    )

    for far in (4, 3, 2, 1):
        for lane, at, rows, order in lanes:
            for offset in OFFSETS:
                if depth(offset) == far:
                    add(lane, at, rows, order, offset)
                    back(lane, at, rows, order, offset)
        yield
    lines = []
    for lane, at, rows, order in lanes:
        add(lane, at, rows, order, (0, 0))
        for by in (1, 3, 2):
            q = moved(p, order[0], by)
            src = block_of(g_ref, q, at, rows, core)
            lines.append(
                send(src, line_bufs[lane].at[by - 1], line_send.at[lane, by - 1], line_recv.at[lane, by - 1], q)
            )
    yield
    for i, (lane, at, rows, order) in enumerate(lanes):
        for copy in lines[3 * i : 3 * i + 3]:
            copy.wait_recv()
        target = (p["x"] % 2, core, p["y"], p["x"] // 2, p["z"], pl.ds(at, rows), slice(None))
        total = g_ref[target].astype(f32)
        for by in range(3):
            total = total + line_bufs[lane][by].astype(f32)
        g_ref[target] = total.astype(bf16)
    for copy in lines + list(sent.values()) + list(halves.values()):
        copy.wait_send()
    yield


def dot(a, b):
    return jnp.dot(a, b, preferred_element_type=f32)


def dot_nt(a, b):
    return lax.dot_general(a, b, (((1,), (1,)), ((), ())), preferred_element_type=f32)


def inv_rms(v):
    return lax.rsqrt(jnp.mean(v * v, axis=-1, keepdims=True) + norm_eps)


def norm_back(v, r, c, e):
    ec = e * c
    vr = v * r
    dv = r * (ec - vr * jnp.mean(vr * ec, axis=-1, keepdims=True))
    return dv, jnp.sum(e * vr, axis=0, keepdims=True)


def turn(u, cos, sin):
    a, b = u[:, :128], u[:, 128:]
    return jnp.concatenate([a * cos - b * sin, b * cos + a * sin], axis=1)


def turn_back(e, cos, sin):
    a, b = e[:, :128], e[:, 128:]
    return jnp.concatenate([a * cos + b * sin, b * cos - a * sin], axis=1)


def columns(w_ref, t, y, first):
    return jnp.concatenate(
        [w_ref[t // 2, t % 2, y + i, :, :, first : first + 80, :].reshape(D, 128) for i in range(2)], axis=1
    )


def put_columns(g_ref, t, y, first, value):
    value = value.astype(bf16)
    for i in range(2):
        g_ref[t // 2, t % 2, y + i, :, :, first : first + 80, :] = (
            value[:, 128 * i : 128 * i + 128].reshape(2, 4, 80, 128)
        )


NB = len(LANES)


def kernel(
    seg_ref, wq_ref, wkv_ref, wo_ref, wg_ref, wu_ref, wd_ref, x_ref, cot_ref,
    gin_ref, gpa_ref, gpf_ref, gpo_ref, gq_ref, gk_ref, cos_tab, sin_tab, freq_ref,
    out_ref, gx_ref, shard_ref, kv_ref, gn_out,
    *scratch,
):
    bufs, line_bufs, scratch = scratch[:NB], scratch[NB : 2 * NB], scratch[2 * NB :]
    (
        w_ref, g_ref, other, xg, rows_s, s_ref, got, stage,
        cos_ref, sin_ref, wkv, attn_in, attn_in_t, kt, vt, kb, vb, qraw, qb, probs, ctx,
        mlp_in, mlp_in_t, d_b, d_t, act_s, dact_s, hid_s, acc, acc2, dkt, dvt, proj_s,
        dx_got, gn_now, gn_got, final,
        one_send, one_recv, line_send, line_recv, unit_send, unit_recv, sib_send, sib_recv, x_send, x_recv,
        bline_send, bline_recv, back_send, back_recv, bsib_send, bsib_recv, last_send, last_recv, kv_send, kv_recv,
        dx_send, dx_recv, gn_send, gn_recv,
    ) = scratch
    p = place()
    t = lax.axis_index("tensor")
    dp = lax.axis_index("dp")
    y = p["y"]
    core = p["c"]
    own = (p["x"] % 2, core, y, p["x"] // 2, p["z"])
    say_here(p, t)

    rows_s[...] = jnp.zeros_like(rows_s)
    for j in range(4):
        if j < 2:
            rows_s[j, :20, :128] = wq_ref[:, 128 * j : 128 * j + 128].astype(f32)
        else:
            rows_s[j, :20, :128] = wo_ref[:, 128 * j - 256 : 128 * j - 128].astype(f32)
        rows_s[j, :20, 128:256] = wg_ref[:, 128 * j : 128 * j + 128].astype(f32)
        rows_s[j, :20, 256:384] = wu_ref[:, 128 * j : 128 * j + 128].astype(f32)
        rows_s[j, :20, 384:512] = wd_ref[:, 128 * j : 128 * j + 128].astype(f32)
        rows_s[j, :20, 512:] = wkv_ref[:, 128 * j : 128 * j + 128].astype(f32)
    s_ref[...] = rows_s[...].astype(bf16)
    gin, gpa, gpf, gpo, gq, gk = (
        ref[...].reshape(1, ref.shape[0]) for ref in (gin_ref, gpa_ref, gpf_ref, gpo_ref, gq_ref, gk_ref)
    )
    scale = HD ** -0.5
    seg = seg_ref[...]
    n0 = jnp.sum(jnp.where(seg == 0, 1.0, 0.0), axis=1, keepdims=True)
    n1 = jnp.sum(jnp.where(seg <= 1, 1.0, 0.0), axis=1, keepdims=True)
    base = ((t - 2) * PART).astype(f32)
    which = lax.broadcasted_iota(jnp.int32, (8, 128), 0)
    turn_by = (jnp.where(which == 0, 0.0, jnp.where(which == 1, n0, n1)) - base) * freq_ref[...]
    cb, sb = jnp.cos(turn_by), jnp.sin(turn_by)
    token = lax.broadcasted_iota(jnp.int32, (KEYS, 1), 0).astype(f32) + base
    in0, in1 = token < n0, token < n1
    cd = jnp.where(in0, cb[0:1], jnp.where(in1, cb[1:2], cb[2:3]))
    sd = jnp.where(in0, sb[0:1], jnp.where(in1, sb[1:2], sb[2:3]))
    ca, sa = cos_tab[...], sin_tab[...]
    cos_ref[...] = ca * cd + sa * sd
    sin_ref[...] = sa * cd - ca * sd

    xg[2] = x_ref[...]
    got[pl.ds(y, 1)] = s_ref[pl.ds(y, 1)]
    all_here(p, t)
    first = []
    for k in (1, 3, 2):
        q = moved(p, "y", k)
        first.append(send(s_ref.at[q["y"]], got.at[y], one_send.at[k - 1], one_recv.at[k - 1], q))

    def token_copy(src, slot, to):
        return pltpu.make_async_remote_copy(
            src_ref=src, dst_ref=xg.at[slot], send_sem=x_send.at[1 - slot], recv_sem=x_recv.at[1 - slot],
            device_id={"dp": dp, "tensor": to}, device_id_type=MESH,
        )

    @pl.when(t < 3)
    def _():
        token_copy(x_ref, 1, jnp.minimum(t + 1, 3)).start()

    @pl.when(t == 0)
    def _():
        token_copy(x_ref, 0, t + 2).start()

    for copy in first:
        copy.wait_recv()
    for j in range(4):
        stage[20 * j : 20 * j + 20, :] = got[j].astype(f32)[:20, :512]
    for i, at in enumerate((0, G0, U0, D0)):
        w_ref[own + (slice(at, at + 80),)] = stage[:80, 128 * i : 128 * i + 128].astype(bf16)
    w_ref[own + (slice(KV0, KV0 + 32),)] = got[pl.ds(t, 1)][0, :, 512:640]
    for copy in first:
        copy.wait_send()

    sems = (line_send, line_recv, unit_send, unit_recv, sib_send, sib_recv)
    attn = gather_steps(ATTN, w_ref, p, sems, [])
    feed = gather_steps(FEED, w_ref, p, sems, [])
    next(attn)
    for _ in range(5):
        next(feed)
        next(attn)

    @pl.when(t > 0)
    def _():
        token_copy(x_ref, 1, jnp.minimum(t + 1, 3)).wait_recv()

    @pl.when(t == 2)
    def _():
        token_copy(xg.at[1], 0, jnp.minimum(t + 1, 3)).start()

    @pl.when(t >= 2)
    def _():
        token_copy(x_ref, 0, jnp.minimum(t + 1, 3)).wait_recv()

    @pl.when(t < 3)
    def _():
        token_copy(x_ref, 1, jnp.minimum(t + 1, 3)).wait_send()

    @pl.when(lax.rem(t, 2) == 0)
    def _():
        token_copy(x_ref, 0, jnp.minimum(t + 1, 3)).wait_send()

    def tokens(i):
        return jnp.where(i >= 2 - t, xg[i].astype(f32), 0.0)

    def input_norm(i, _):
        x = tokens(i)
        a = x * inv_rms(x) * gin
        attn_in[i] = a.astype(bf16)
        attn_in_t[i] = a.T.astype(bf16)
        return 0

    lax.fori_loop(0, 3, input_norm, 0)
    acc[...] = jnp.zeros_like(acc)
    next(attn)

    def keyval_in(g, _):
        for tt in range(4):
            for yy in range(4):
                stage[20 * tt : 20 * tt + 20, 128 * yy : 128 * yy + 128] = (
                    w_ref[tt // 2, tt % 2, yy, g // 4, g % 4, KV0 : KV0 + 32, :].astype(f32)[:20]
                )
        wkv[g] = stage[:80, :].astype(bf16)
        return 0

    lax.fori_loop(0, GROUPS, keyval_in, 0)

    def rows_of(i):
        return pl.ds(pl.multiple_of(i * PART, PART), PART)

    def keys_values(i, _):
        rows = rows_of(i)
        kv_raw = dot(attn_in[i], wkv[...].reshape(D, 512))
        kraw = kv_raw[:, :HD]
        k = turn(kraw * inv_rms(kraw) * gk, cos_ref[rows, :], sin_ref[rows, :])
        kb[rows, :] = k.astype(bf16)
        kt[:, rows] = k.T.astype(bf16)
        v = kv_raw[:, HD:]
        vb[rows, :] = v.astype(bf16)
        vt[:, rows] = v.T.astype(bf16)
        return 0

    lax.fori_loop(0, 3, keys_values, 0)
    next(feed)

    def head(h, _):
        cos_q, sin_q = cos_ref[2 * PART :, :], sin_ref[2 * PART :, :]
        column = lax.broadcasted_iota(jnp.int32, (PART, KEYS), 1)
        last = lax.broadcasted_iota(jnp.int32, (PART, 1), 0) + 2 * PART
        own_token = last.astype(f32) + base
        start = jnp.where(own_token < n0, 0.0, jnp.where(own_token < n1, n0, n1))
        low = jnp.maximum(own_token - (WINDOW - 1), start) - base
        raw = dot(attn_in[2], columns(w_ref, h, 0, 0))
        qraw[h] = raw
        q = turn(raw * inv_rms(raw) * gq, cos_q, sin_q).astype(bf16)
        qb[h] = q
        s = dot(q, kt[...]) * scale
        s = jnp.where((column.astype(f32) >= low) & (column <= last), s, -1e30)
        e = jnp.exp(s - jnp.max(s, axis=-1, keepdims=True))
        pr = e / jnp.sum(e, axis=-1, keepdims=True)
        probs[h] = pr
        c = dot(pr.astype(bf16), vb[...]).astype(bf16)
        ctx[h] = c
        acc[...] += dot_nt(c, columns(w_ref, h, 2, 0))
        return 0

    lax.fori_loop(0, 4, head, 0)
    proj = acc[...]
    proj_s[...] = proj
    mid = x_ref[...].astype(f32) + proj * inv_rms(proj) * gpa
    gx_ref[...] = mid
    m = mid * inv_rms(mid) * gpf
    mlp_in[...] = m.astype(bf16)
    mlp_in_t[...] = m.T.astype(bf16)
    acc[...] = jnp.zeros_like(acc)
    next(feed)

    def feed_forward(c, _):
        tt, yy = c // 2, 2 * (c % 2)
        gate = dot(mlp_in[...], columns(w_ref, tt, yy, G0))
        up = dot(mlp_in[...], columns(w_ref, tt, yy, U0))
        k0, k1 = 0.7978845608028654, 0.044715
        sq = gate * gate
        th = jnp.tanh(k0 * (gate + k1 * gate * sq))
        half = 0.5 * (1.0 + th)
        act = gate * half
        hid = (act * up).astype(bf16)
        act_s[c] = act
        dact_s[c] = up * (half + 0.5 * gate * (1.0 - th * th) * (k0 + (3.0 * k0 * k1) * sq))
        hid_s[c] = hid
        acc[...] += dot_nt(hid, columns(w_ref, tt, yy, D0))
        return 0

    lax.fori_loop(0, 8, feed_forward, 0)
    mlp = acc[...]
    r = inv_rms(mlp)
    out_ref[...] = (gx_ref[...] + mlp * r * gpo).astype(bf16)
    d_mlp, g_po = norm_back(mlp, r, gpo, cot_ref[...].astype(f32))
    gn_now[0, 3:4, :] = g_po
    d_b[...] = d_mlp.astype(bf16)
    d_t[...] = d_mlp.T.astype(bf16)
    acc[...] = jnp.zeros_like(acc)

    def feed_back(c, _):
        tt, yy = c // 2, 2 * (c % 2)
        put_columns(g_ref, tt, yy, D0, dot(d_t[...], hid_s[c]))
        d_hid = dot(d_b[...], columns(w_ref, tt, yy, D0))
        d_gate = (d_hid * dact_s[c]).astype(bf16)
        d_up = (d_hid * act_s[c]).astype(bf16)
        put_columns(g_ref, tt, yy, G0, dot(mlp_in_t[...], d_gate))
        put_columns(g_ref, tt, yy, U0, dot(mlp_in_t[...], d_up))
        acc[...] += dot_nt(d_gate, columns(w_ref, tt, yy, G0)) + dot_nt(d_up, columns(w_ref, tt, yy, U0))
        return 0

    lax.fori_loop(0, 8, feed_back, 0)
    sems = (bline_send, bline_recv, back_send, back_recv, bsib_send, bsib_recv)
    feed = reduce_steps(FEED, g_ref, other, bufs, line_bufs, p, sems)
    next(feed)

    mid = gx_ref[...]
    d_pre, g_pf = norm_back(mid, inv_rms(mid), gpf, acc[...])
    gn_now[0, 2:3, :] = g_pf
    d_mid = cot_ref[...].astype(f32) + d_pre
    proj = proj_s[...]
    d_proj, g_pa = norm_back(proj, inv_rms(proj), gpa, d_mid)
    gn_now[0, 1:2, :] = g_pa
    gx_ref[...] = d_mid
    d_b[...] = d_proj.astype(bf16)
    d_t[...] = d_proj.T.astype(bf16)
    dkt[...] = jnp.zeros_like(dkt)
    dvt[...] = jnp.zeros_like(dvt)
    acc[...] = jnp.zeros_like(acc)
    acc2[...] = jnp.zeros_like(acc2)
    next(feed)

    def head_back(h, _):
        cos_q, sin_q = cos_ref[2 * PART :, :], sin_ref[2 * PART :, :]
        put_columns(g_ref, h, 2, 0, dot(d_t[...], ctx[h]))
        d_ctx = dot(d_b[...], columns(w_ref, h, 2, 0))
        d_ctx_b = d_ctx.astype(bf16)
        pr = probs[h]
        d_pr = dot(d_ctx_b, vt[...])
        dvt[...] += dot(d_ctx.T.astype(bf16), pr.astype(bf16))
        inner = jnp.sum(pr * d_pr, axis=-1, keepdims=True)
        ds = (pr * (d_pr - inner)).astype(bf16)
        dq = dot(ds, kb[...]) * scale
        dkt[...] += dot(qb[h].astype(f32).T.astype(bf16), ds)
        raw = qraw[h]
        d_raw, g_q = norm_back(raw, inv_rms(raw), gq, turn_back(dq, cos_q, sin_q))
        acc2[...] += g_q
        d_raw = d_raw.astype(bf16)
        put_columns(g_ref, h, 0, 0, dot(attn_in_t[2], d_raw))
        acc[...] += dot_nt(d_raw, columns(w_ref, h, 0, 0))
        return 0

    lax.fori_loop(0, 2, head_back, 0)
    next(feed)
    lax.fori_loop(2, 4, head_back, 0)
    gn_now[0, 4:8, :] = jnp.zeros((4, D), f32)
    gn_now[0, 4:5, :HD] = acc2[...]
    acc2[...] = jnp.zeros_like(acc2)

    def keys_values_back(i, _):
        rows = rows_of(i)
        raw = dot(attn_in[i], wkv[:, :, :HD].reshape(D, HD))
        e = turn_back(dkt[:, rows].T * scale, cos_ref[rows, :], sin_ref[rows, :])
        dk, g_k = norm_back(raw, inv_rms(raw), gk, e)
        acc2[...] += g_k
        kb[rows, :] = dk.astype(bf16)
        vb[rows, :] = dvt[:, rows].T.astype(bf16)
        return 0

    lax.fori_loop(0, 3, keys_values_back, 0)
    gn_now[0, 5:6, :HD] = acc2[...]
    for half, src in enumerate((kb, vb)):
        grad = sum(dot(attn_in_t[i], src[PART * i : PART * i + PART, :]) for i in range(3))
        stage[80:, :] = jnp.zeros((16, 512), f32)
        for g in range(GROUPS):
            stage[:80, :HD] = grad[80 * g : 80 * g + 80]
            for tt in range(4):
                for yy in range(2):
                    g_ref[tt // 2, tt % 2, 2 * half + yy, g // 4, g % 4, KV0 : KV0 + 32, :] = (
                        stage[20 * tt : 20 * tt + 32, 128 * yy : 128 * yy + 128].astype(bf16)
                    )
    attn = reduce_steps(ATTN, g_ref, other, bufs, line_bufs, p, sems)
    next(attn)
    next(feed)
    next(attn)

    def input_back(i, extra):
        rows = rows_of(i)
        d_in = dot_nt(kb[rows, :], wkv[:, :, :HD].reshape(D, HD)) + dot_nt(vb[rows, :], wkv[:, :, HD:].reshape(D, HD))
        x = tokens(i)
        dx, g_in = norm_back(x, inv_rms(x), gin, d_in if extra is None else d_in + extra)
        gn_now[0, 0:1, :] += g_in
        return dx

    def input_back_before(i, _):
        attn_in[i] = input_back(i, None).astype(bf16)
        return 0

    gn_now[0, 0:1, :] = jnp.zeros((1, D), f32)
    lax.fori_loop(0, 2, input_back_before, 0)
    def dx_copy(k):
        to = jnp.maximum(t - 1, 0) if k == 1 else jnp.where(t == 3, 2, 0)
        return pltpu.make_async_remote_copy(
            src_ref=attn_in.at[2 - k], dst_ref=dx_got.at[k - 1], send_sem=dx_send.at[k - 1], recv_sem=dx_recv.at[k - 1],
            device_id={"dp": dp, "tensor": to}, device_id_type=MESH,
        )

    @pl.when(t >= 2)
    def _():
        dx_copy(2).start()

    @pl.when(lax.rem(t, 2) == 1)
    def _():
        dx_copy(1).start()

    gn_copies = [[], [], [], []]

    def gn_start(i):
        if i == 3:
            gn_copies[3].append(send(gn_now.at[3], gn_got.at[12], gn_send.at[9], gn_recv.at[9], moved(p, "c", 1)))
            return
        axis = "xyz"[i]
        gn_got[pl.ds(4 * i + p[axis], 1)] = gn_now[i][None]
        for by in (1, 3, 2):
            sem = 3 * i + by - 1
            dst = gn_got.at[4 * i + p[axis]]
            gn_copies[i].append(send(gn_now.at[i], dst, gn_send.at[sem], gn_recv.at[sem], moved(p, axis, by)))

    def gn_add(i):
        for copy in gn_copies[i]:
            copy.wait_recv()
        if i == 3:
            gn_now[4] = gn_now[3] + gn_got[12]
        else:
            gn_now[i + 1] = (gn_got[4 * i] + gn_got[4 * i + 1]) + (gn_got[4 * i + 2] + gn_got[4 * i + 3])

    next(attn)
    gx_ref[...] += input_back(2, acc[...])
    gn_start(0)
    for i in range(4):
        next(attn)
        if i == 0:
            @pl.when(t == 2)
            def _():
                dx_copy(2).wait_recv()
                attn_in[1] = (attn_in[1].astype(f32) + dx_got[1].astype(f32)).astype(bf16)
                dx_copy(1).start()

        if i < 3:
            next(feed)
            gn_add(i)
            gn_start(i + 1)

    mine = g_ref[own].astype(f32)
    for i, at in enumerate((0, G0, U0, D0)):
        for j in range(4):
            rows_s[j, 0:20, 128 * i : 128 * i + 128] = mine[at + 20 * j : at + 20 * j + 20]
    for j in range(4):
        rows_s[j, :24, 512:] = mine[KV0 : KV0 + 24]

    @pl.when(t == y)
    def _():
        kv_ref[pl.ds(y, 1)] = mine[KV0 : KV0 + 24][None]


    def kv_copy(k):
        return pltpu.make_async_remote_copy(
            src_ref=rows_s.at[0, pl.ds(0, 24), pl.ds(512, 128)], dst_ref=kv_ref.at[y],
            send_sem=kv_send.at[k], recv_sem=kv_recv.at[y],
            device_id={"dp": dp - y + t, "tensor": (t + k) % 4}, device_id_type=MESH,
        )

    @pl.when(t != y)
    def _():
        kv_copy(0).start()

    for k in (1, 2, 3):
        kv_copy(k).start()
    last = []
    for k in (1, 3, 2):
        q = moved(p, "y", k)
        last.append(send(rows_s.at[q["y"], pl.ds(0, 24), :], final.at[y], last_send.at[k - 1], last_recv.at[k - 1], q))
    final[pl.ds(y, 1)] = rows_s[pl.ds(y, 1), :24]
    gn_add(3)
    gn_out[...] = gn_now[4]

    @pl.when(t < 3)
    def _():
        dx_copy(1).wait_recv()
        gx_ref[...] += dx_got[0].astype(f32)

    @pl.when(t == 0)
    def _():
        dx_copy(2).wait_recv()
        gx_ref[...] += dx_got[1].astype(f32)

    @pl.when(t >= 1)
    def _():
        dx_copy(1).wait_send()

    @pl.when(t >= 2)
    def _():
        dx_copy(2).wait_send()

    for copy in last:
        copy.wait_recv()

    shard_ref[...] = final[:, :, :512]
    for copy in sum(gn_copies, last):
        copy.wait_send()

    for k in (1, 2, 3):
        kv_copy(k).wait_send()

    @pl.when(t != y)
    def _():
        kv_copy(0).wait_send()

    for j in range(4):
        @pl.when((t != y) | (y != j))
        def _(j=j):
            pltpu.make_async_remote_copy(
                src_ref=kv_ref.at[j], dst_ref=kv_ref.at[j], send_sem=kv_send.at[0], recv_sem=kv_recv.at[j],
                device_id={"dp": dp, "tensor": (t + 1) % 4}, device_id_type=MESH,
            ).wait_recv()


def layer(*args):
    dma = pltpu.SemaphoreType.DMA
    vmem = pl.BlockSpec(memory_space=pltpu.VMEM)
    bufs = [pltpu.VMEM((15,) + unit_shape(order[0], rows), bf16) for _, _, rows, order in LANES]
    bufs += [pltpu.VMEM((3, rows, 128), bf16) for _, _, rows, _ in LANES]
    n = len(LANES)
    return pl.pallas_call(
        kernel,
        out_shape=(
            jax.ShapeDtypeStruct((PART, D), bf16),
            jax.ShapeDtypeStruct((PART, D), f32),
            jax.ShapeDtypeStruct((4, 24, 512), f32),
            jax.ShapeDtypeStruct((4, 24, 128), f32),
            jax.ShapeDtypeStruct((8, D), f32),
        ),
        in_specs=[vmem] * len(args),
        out_specs=(vmem,) * 5,
        scratch_shapes=[
            *bufs,
            pltpu.VMEM((2, 2, 4, 2, 4, BLOCK, 128), bf16),
            pltpu.VMEM((2, 2, 4, 2, 4, BLOCK, 128), bf16),
            pltpu.VMEM((2, 4, 2, 4, BLOCK, 128), bf16),
            pltpu.VMEM((3, PART, D), bf16),
            pltpu.VMEM((4, 32, D), f32),
            pltpu.VMEM((4, 32, D), bf16),
            pltpu.VMEM((4, 32, D), bf16),
            pltpu.VMEM((96, 512), f32),
            pltpu.VMEM((KEYS, 128), f32),
            pltpu.VMEM((KEYS, 128), f32),
            pltpu.VMEM((GROUPS, 80, 512), bf16),
            pltpu.VMEM((3, PART, D), bf16),
            pltpu.VMEM((3, D, PART), bf16),
            pltpu.VMEM((HD, KEYS), bf16),
            pltpu.VMEM((HD, KEYS), bf16),
            pltpu.VMEM((KEYS, HD), bf16),
            pltpu.VMEM((KEYS, HD), bf16),
            pltpu.VMEM((4, PART, HD), f32),
            pltpu.VMEM((4, PART, HD), bf16),
            pltpu.VMEM((4, PART, KEYS), f32),
            pltpu.VMEM((4, PART, HD), bf16),
            pltpu.VMEM((PART, D), bf16),
            pltpu.VMEM((D, PART), bf16),
            pltpu.VMEM((PART, D), bf16),
            pltpu.VMEM((D, PART), bf16),
            pltpu.VMEM((8, PART, 256), f32),
            pltpu.VMEM((8, PART, 256), f32),
            pltpu.VMEM((8, PART, 256), bf16),
            pltpu.VMEM((PART, D), f32),
            pltpu.VMEM((1, HD), f32),
            pltpu.VMEM((HD, KEYS), f32),
            pltpu.VMEM((HD, KEYS), f32),
            pltpu.VMEM((PART, D), f32),
            pltpu.VMEM((2, PART, D), bf16),
            pltpu.VMEM((5, 8, D), f32),
            pltpu.VMEM((13, 8, D), f32),
            pltpu.VMEM((4, 24, D), f32),
            dma((3,)), dma((3,)), dma((n, 3)), dma((n, 3)), dma((n, 16)), dma((n, 16)), dma((n, 16)), dma((n, 16)),
            dma((2,)), dma((2,)),
            dma((n, 3)), dma((n, 3)), dma((n, 16)), dma((n, 16)), dma((n, 16)), dma((n, 16)),
            dma((3,)), dma((3,)), dma((4,)), dma((4,)),
            dma((2,)), dma((2,)), dma((10,)), dma((10,)),
        ],
        compiler_params=pltpu.CompilerParams(
            collective_id=0, has_side_effects=True, vmem_limit_bytes=62 << 20
        ),
        name="layer",
    )(*args)


def finish_kernel(
    out_ref, gx_ref, shard_ref, kv_ref, gn_ref,
    out_to, gx_to, query_to, keyval_to, out_t_to, gate_to, up_to, down_t_to, *gains_to,
):
    out_to[...] = out_ref[...]
    gx_to[...] = gx_ref[...]
    for j in range(4):
        here = slice(128 * j, 128 * j + 128)
        if j < 2:
            query_to[:, here] = shard_ref[j, :20, :128]
        else:
            out_t_to[:, 128 * j - 256 : 128 * j - 128] = shard_ref[j, :20, :128]
        gate_to[:, here] = shard_ref[j, :20, 128:256]
        up_to[:, here] = shard_ref[j, :20, 256:384]
        down_t_to[:, here] = shard_ref[j, :20, 384:512]
        keyval_to[:, here] = kv_ref[j, :20, :]
    for i, ref in enumerate(gains_to):
        ref[...] = gn_ref[i : i + 1, : ref.shape[0]].reshape(ref.shape[0])


def finish(*args):
    vmem = pl.BlockSpec(memory_space=pltpu.VMEM)
    shapes = [((PART, D), bf16), ((PART, D), f32)]
    shapes += [((20, n), f32) for n in (256, 512, 256, 512, 512, 512)]
    shapes += [((n,), f32) for n in (D, D, D, D, HD, HD)]
    return pl.pallas_call(
        finish_kernel,
        out_shape=tuple(jax.ShapeDtypeStruct(*item) for item in shapes),
        in_specs=[vmem] * len(args),
        out_specs=(vmem,) * len(shapes),
        name="finish",
    )(*args)


def rope_parts():
    freq = (rope_base ** (-np.arange(0, HD, 2, dtype=np.float64) / HD))[None, :]
    angles = np.arange(KEYS, dtype=np.float64)[:, None] * freq
    return tuple(jnp.asarray(item.astype(np.float32)) for item in (np.cos(angles), np.sin(angles), freq))


def per_device(
    tokens, segments, cotangent, w_query, w_keyval, w_out, w_gate, w_up, w_down,
    gain_in, gain_post_attn, gain_pre_ff, gain_post_ff, gain_query, gain_key,
):
    made = layer(
        segments, w_query, w_keyval, w_out.T, w_gate, w_up, w_down.T, tokens, cotangent,
        gain_in, gain_post_attn, gain_pre_ff, gain_post_ff, gain_query, gain_key, *rope_parts(),
    )
    output, grad_x, query, keyval, out_t, gate, up, down_t, *gains = finish(*made)
    return (output, grad_x, query, keyval, out_t.T, gate, up, down_t.T, *gains)


def solution(mesh):
    tok = P(("dp", "tensor"), None)
    weights = (
        P("dp", "tensor"), P("dp", None), P("tensor", "dp"), P("dp", "tensor"), P("dp", "tensor"), P("tensor", "dp"),
    )
    return jax.shard_map(
        per_device,
        mesh=mesh,
        in_specs=(tok, P("dp", None), tok) + weights + (P(),) * 6,
        out_specs=(tok, tok) + weights + (P(),) * 6,
        check_vma=False,
    )
```
